32 devices in a mesh: group: 4 (over y, x), seq: 8 (over z, core).
Axes of the slice: x: 2, y: 2, z: 4, core: 2. Of those that a mesh axis runs over, the one named last changes fastest.
Arguments:
- features: bfloat16 [4096, 768], P(('group', 'seq')), may hold values from -6 to 6
- tiles: bfloat16 [4096, 1024], P(('group', 'seq')), may hold values from -0.5 to 0.5
- tile_src: int32 [32, 8], P(('group', 'seq')), may hold values from 0 to 3
- tile_count: int32 [32], P(('group', 'seq')), may hold values from 1 to 8, as said below
- node_bucket: int32 [4096], P(('group', 'seq')), may hold values from 0 to 15
- w_qk: bfloat16 [768, 1536], replicated, may hold values from -0.3125 to 0.3125
- w_v: bfloat16 [768, 768], replicated, may hold values from -1.25 to 1.25
- bias_table: float32 [32, 256], replicated, may hold values from -2 to 300
Outputs:
- attended: bfloat16 [4096, 768], P(('group', 'seq'))
The draws below stay inside these ranges and needn't reach their ends.
Inputs may be any that keep to these rules, and one draw needn't show every extreme that they name: `tile_count`: some row block uses all 8 slots.
All inputs are finite; a program needn't handle non-finite values.
Results may differ from the reference program's by a relative error of at most 0.012.
Values may be sent and summed in bfloat16 or wider, within the bound.
No kernel may reach another device: no remote copies, remote signals or barrier semaphores. Data moves between devices by JAX's collectives and lax.ppermute only.
A program may use at most 64 MiB of HBM per device.

```python
import math
import jax
import jax.numpy as jnp
from jax import lax

D = 768
H = 32
HD = 24
NB = 16
TILES = 8
NODE_DEV = 128
GROUPS = 4
NODES_G = 1024
BLOCKS = 32
NODES = 4096
N_SEQ = 8


def draw_tile_count(key, part):
    counts = jax.random.randint(jax.random.fold_in(key, 11), (BLOCKS,), 1, TILES + 1)
    full_block = jax.random.randint(jax.random.fold_in(key, 12), (), 0, BLOCKS)
    return jnp.where(jnp.arange(BLOCKS) == full_block, TILES, counts).astype(jnp.int32)


def draw_bias_table(key, part):
    table_now = jax.random.uniform(jax.random.fold_in(key, 21), (H, NB, NB), jnp.float32, -2.0, 2.0)
    return table_now.reshape(H, NB * NB)


def set_ends(result, own_key, low, high):
    extent = result.shape
    index_at = [jax.random.randint(jax.random.fold_in(own_key, axis), (), 0, extent[axis]) for axis in range(len(extent))]
    result = result.at[tuple(index_at)].set(low)
    longest = extent.index(max(extent))
    index_at[longest] = (index_at[longest] + 1) % extent[longest]
    return result.at[tuple(index_at)].set(high)


def block_levels(rng, extent, pieces, least, high):
    def one(dim, shards_of):
        draws = jax.random.uniform(jax.random.fold_in(jax.random.fold_in(rng, 6), dim), (shards_of,), jnp.float32, least / len(pieces), high / len(pieces))
        return jnp.repeat(jnp.exp(draws), extent[dim] // shards_of).reshape((-1,) + (1,) * (len(extent) - dim - 1))

    gain = one(*pieces[0])
    for cut in pieces[1:]:
        gain = gain * one(*cut)
    return gain


def gaussian(rng, shape, deviation, most, cuts=(), dtype=jnp.bfloat16):
    array = deviation * jax.random.normal(rng, shape, jnp.float32)
    if cuts:
        array = array * block_levels(rng, shape, cuts, -0.22, 0.18)
    return jnp.clip(array, -most, most).astype(dtype)


def setup_inputs(seed: int = 0) -> dict:
    keys = jax.random.split(jax.random.key(seed), 9)
    features = gaussian(keys[0], (NODES, D), 1.0, 6.0, ((0, 32),))
    tiles = gaussian(keys[1], (NODES, TILES * NODE_DEV), NODE_DEV ** -0.5, 0.5, ((0, 32),))
    tile_src = set_ends(jax.random.randint(keys[2], (BLOCKS, TILES), 0, GROUPS), jax.random.fold_in(keys[2], 1), 0, GROUPS - 1).astype(jnp.int32)
    tile_count = draw_tile_count(jax.random.fold_in(keys[8], 71), 0)
    node_bucket = set_ends(jax.random.randint(keys[4], (NODES,), 0, NB), jax.random.fold_in(keys[4], 1), 0, NB - 1).astype(jnp.int32)
    w_qk = gaussian(keys[5], (D, 2 * D), (D // 2) ** -0.5, 0.3125)
    w_v = gaussian(keys[6], (D, D), (D // 32) ** -0.5, 1.25)
    bias_table = draw_bias_table(jax.random.fold_in(keys[8], 71), 0)
    return dict(features=features, tiles=tiles, tile_src=tile_src, tile_count=tile_count, node_bucket=node_bucket, w_qk=w_qk, w_v=w_v, bias_table=bias_table)


def reference(features, tiles, tile_src, tile_count, node_bucket, w_qk, w_v, bias_table):
    blocks_all = features.reshape(BLOCKS, NODE_DEV, D)
    tile_blocks = tiles.reshape(BLOCKS, NODE_DEV, TILES, NODE_DEV)

    def aggregate_block(block_id):
        block_ids = (tile_src[block_id] * N_SEQ + block_id % N_SEQ).astype(jnp.int32)
        chosen = blocks_all[block_ids].astype(jnp.float32)
        live_mask = (jnp.arange(TILES) < tile_count[block_id]).astype(jnp.float32)
        tile_weights = tile_blocks[block_id].astype(jnp.float32) * live_mask[None, :, None]
        summed = jnp.einsum('rtc,tcd->rd', tile_weights, chosen, precision=lax.Precision.HIGHEST)
        return blocks_all[block_id].astype(jnp.float32) + summed
    aggregated = lax.map(aggregate_block, jnp.arange(BLOCKS)).reshape(NODES, D)
    mean_square = lax.optimization_barrier(jnp.mean(aggregated * aggregated, axis=-1, keepdims=True))
    normed = (aggregated * lax.rsqrt(mean_square + 1e-06)).astype(jnp.bfloat16)
    query_key = jnp.dot(normed, w_qk, preferred_element_type=jnp.float32).astype(jnp.bfloat16)
    values = jnp.dot(normed, w_v, preferred_element_type=jnp.float32).astype(jnp.bfloat16)
    queries = query_key[:, :D].reshape(GROUPS, NODES_G, H, HD)
    keys_all = query_key[:, D:].reshape(GROUPS, NODES_G, H, HD)
    values_all = values.reshape(GROUPS, NODES_G, H, HD)
    buckets = node_bucket.reshape(GROUPS, NODES_G)
    bias_cube = bias_table.reshape(H, NB, NB)
    scale = 1.0 / math.sqrt(HD)

    def group_attention(operands):
        group_q, group_k, group_v, group_b = operands

        def one_head(head_id):
            scores = jnp.dot(group_q[:, head_id, :], group_k[:, head_id, :].T, preferred_element_type=jnp.float32) * scale
            row_bias = bias_cube[head_id][group_b]
            scores = scores + row_bias[:, group_b]
            peak = lax.optimization_barrier(jnp.max(scores, axis=-1, keepdims=True))
            weights = jnp.exp(scores - peak)
            total_weight = lax.optimization_barrier(jnp.sum(weights, axis=-1, keepdims=True))
            mixed = jnp.dot(weights.astype(jnp.bfloat16), group_v[:, head_id, :], preferred_element_type=jnp.float32)
            return mixed / total_weight
        return lax.map(one_head, jnp.arange(H))
    heads_out = lax.map(group_attention, (queries, keys_all, values_all, buckets))
    return heads_out.transpose(0, 2, 1, 3).reshape(NODES, D).astype(jnp.bfloat16)
```

```python
import functools
import math

import jax
import jax.numpy as jnp
import numpy as np
from jax import lax
from jax.experimental import pallas as pl
from jax.experimental.pallas import tpu as pltpu
from jax.sharding import PartitionSpec as P

H = 32
HD = 24
NB = 16
TILES = 8
LANES = 128
PAD = 32
QUAD = LANES // PAD
NT = (((1,), (1,)), ((), ()))
VMEM_LIMIT = 56 * 1024 * 1024


def vmem():
    return pl.BlockSpec(memory_space=pltpu.VMEM)


def smem():
    return pl.BlockSpec(memory_space=pltpu.SMEM)


def pad_matrix():
    rows = np.arange(16 * HD)
    cols = (rows // HD) * PAD + rows % HD
    sel = np.zeros((16 * HD, 16 * PAD), np.float32)
    sel[rows, cols] = 1.0
    return sel


def prepare_kernel(w_qk_ref, w_v_ref, bias_ref, sel_ref, wq_ref, wk_ref, wv_ref, table_ref):
    width = w_v_ref.shape[1]
    half = 16 * HD
    sel = sel_ref[...]
    for src, base, dst in ((w_qk_ref, 0, wq_ref), (w_qk_ref, width, wk_ref), (w_v_ref, 0, wv_ref)):
        for part in range(width // half):
            block = src[:, base + part * half : base + (part + 1) * half]
            dst[:, part * 512 : (part + 1) * 512] = jnp.dot(
                block, sel, preferred_element_type=jnp.float32
            ).astype(jnp.bfloat16)
    scaled = bias_ref[...] * math.sqrt(HD)
    high = scaled.astype(jnp.bfloat16).astype(jnp.float32)
    rest = scaled - high
    mid = rest.astype(jnp.bfloat16).astype(jnp.float32)
    low = rest - mid
    lane = lax.broadcasted_iota(jnp.int32, scaled.shape, 1) % LANES
    parts = jnp.where(lane < NB, high, jnp.where(lane < 2 * NB, mid, jnp.where(lane < 3 * NB, low, 0.0)))
    table_ref[...] = parts.astype(jnp.bfloat16)


def aggregate_kernel(src_ref, count_ref, feat_ref, gathered_ref, tiles_ref, bucket_ref, out_ref):
    rows, width = feat_ref.shape
    count = count_ref[0]
    picked = []
    masked = []
    for t in range(TILES):
        start = pl.multiple_of(src_ref[0, t] * rows, rows)
        picked.append(gathered_ref[pl.ds(start, rows), :])
        tile = tiles_ref[:, t * rows : (t + 1) * rows]
        masked.append(jnp.where(t < count, tile, jnp.zeros_like(tile)))
    total = feat_ref[...].astype(jnp.float32) + jnp.dot(
        jnp.concatenate(masked, axis=1),
        jnp.concatenate(picked, axis=0),
        preferred_element_type=jnp.float32,
    )
    mean_square = jnp.mean(total * total, axis=-1, keepdims=True)
    out_ref[:rows, :] = (total * lax.rsqrt(mean_square + 1e-06)).astype(jnp.bfloat16)
    bucket = bucket_ref[...].astype(jnp.float32)
    out_ref[rows:, :] = jnp.zeros((out_ref.shape[0] - rows, width), jnp.bfloat16)
    out_ref[rows:, :rows] = jnp.broadcast_to(bucket, (out_ref.shape[0] - rows, rows)).astype(
        jnp.bfloat16
    )


def one_hot_slab(bucket_row):
    n = bucket_row.shape[1]
    index = lax.broadcasted_iota(jnp.int32, (LANES, n), 0)
    wanted = jnp.where(index < 3 * NB, index % NB, -1).astype(jnp.float32)
    hot = jnp.where(wanted == bucket_row, 1.0, 0.0)
    return hot.T.astype(jnp.bfloat16)


def attend_kernel(
    own_ref, all_ref, wq_ref, wk_ref, wv_ref, table_ref, sel_ref, out_ref,
    k_ref, v_ref, hot_ref, q_ref, bias_ref, x0_ref, x1_ref, p0_ref, p1_ref, heads_ref,
):
    rows = out_ref.shape[0]
    blocks = all_ref.shape[0]
    keys = blocks * rows
    wide = k_ref.shape[1]
    quads = H // QUAD
    factor = math.log2(math.e) / math.sqrt(HD)

    for s in range(blocks):
        hot_ref[s * rows : (s + 1) * rows, :] = one_hot_slab(
            all_ref[s, rows : rows + 8, :rows].astype(jnp.float32)[0:1, :]
        )
    hot_q = one_hot_slab(own_ref[rows : rows + 8, :rows].astype(jnp.float32)[0:1, :])[:, :NB]
    q_ref[...] = jnp.dot(
        own_ref[:rows, :], wq_ref[...], preferred_element_type=jnp.float32
    ).astype(jnp.bfloat16)
    bias_ref[...] = jnp.dot(hot_q, table_ref[...], preferred_element_type=jnp.float32).astype(
        jnp.bfloat16
    )

    step = 4 if blocks % 4 == 0 else 1

    def project(i, carry):
        cols = pl.ds(pl.multiple_of(i * 256, 256), 256)
        for w_ref, dst in ((wk_ref, k_ref), (wv_ref, v_ref)):
            for s in range(0, blocks, step):
                block = jnp.concatenate([all_ref[s + j, :rows, :] for j in range(step)], axis=0)
                dst[s * rows : (s + step) * rows, cols] = jnp.dot(
                    block, w_ref[:, cols], preferred_element_type=jnp.float32
                ).astype(jnp.bfloat16)
        return carry

    lax.fori_loop(0, wide // 256, project, 0)

    lane_head = lax.broadcasted_iota(jnp.int32, (rows, LANES), 1) // PAD
    ones = jnp.ones((keys, LANES), jnp.bfloat16)

    def scores(m, x_ref):
        cols = pl.ds(pl.multiple_of(m * LANES, LANES), LANES)
        q = q_ref[:, cols]
        zero = jnp.zeros_like(q)
        left = jnp.concatenate([jnp.where(lane_head == h, q, zero) for h in range(QUAD)], axis=0)
        right = jnp.concatenate(
            [
                bias_ref[:, pl.ds(pl.multiple_of((m * QUAD + h) * LANES, LANES), LANES)]
                for h in range(QUAD)
            ],
            axis=0,
        )
        query = jnp.concatenate([left, right], axis=1)
        for n in range(0, keys, 256):
            key = jnp.concatenate([k_ref[n : n + 256, cols], hot_ref[n : n + 256, :]], axis=1)
            x_ref[:, n : n + 256] = lax.dot_general(
                query, key, NT, preferred_element_type=jnp.float32
            )

    def mix(m, x_ref, p_ref):
        cols = pl.ds(pl.multiple_of(m * LANES, LANES), LANES)
        for r in range(0, QUAD * rows, 16):
            x = x_ref[r : r + 16, :]
            peak = jnp.max(x, axis=-1, keepdims=True)
            p_ref[r : r + 16, :] = jnp.exp2((x - peak) * factor).astype(jnp.bfloat16)
        value = jnp.concatenate([v_ref[:, cols], ones], axis=1)
        mixed = jnp.dot(p_ref[...], value, preferred_element_type=jnp.float32)
        top = mixed[:rows, :LANES]
        total = mixed[:rows, LANES:]
        for h in range(1, QUAD):
            top = jnp.where(lane_head == h, mixed[h * rows : (h + 1) * rows, :LANES], top)
            total = jnp.where(lane_head == h, mixed[h * rows : (h + 1) * rows, LANES:], total)
        heads_ref[:, cols] = (top / total).astype(jnp.bfloat16)

    scores(0, x0_ref)

    def pair(i, carry):
        m = i * 2
        scores(m + 1, x1_ref)
        mix(m, x0_ref, p0_ref)
        scores(jnp.minimum(m + 2, quads - 1), x0_ref)
        mix(m + 1, x1_ref, p1_ref)
        return carry

    lax.fori_loop(0, quads // 2, pair, 0)

    half = 16 * HD
    for part in range(out_ref.shape[1] // half):
        out_ref[:, part * half : (part + 1) * half] = lax.dot_general(
            heads_ref[:, part * 512 : (part + 1) * 512], sel_ref[...], NT,
            preferred_element_type=jnp.float32,
        ).astype(jnp.bfloat16)


def on_device(features, tiles, tile_src, tile_count, node_bucket, w_qk, w_v, bias_table):
    rows, width = features.shape
    seq_count = lax.axis_size("seq")
    wide = H * PAD
    keys = seq_count * rows
    bf16 = jnp.bfloat16
    sel = jnp.asarray(pad_matrix(), bf16)
    params = pltpu.CompilerParams(vmem_limit_bytes=VMEM_LIMIT)

    cube = bias_table.reshape(H, NB, NB).transpose(1, 0, 2)
    cube = jnp.concatenate([cube, cube, cube, jnp.zeros((NB, H, LANES - 3 * NB), jnp.float32)], axis=2)
    cube = cube.reshape(NB, H * LANES)
    shape = jax.ShapeDtypeStruct
    wq, wk, wv, table = pl.pallas_call(
        prepare_kernel,
        out_shape=[shape((width, wide), bf16)] * 3 + [shape((NB, H * LANES), bf16)],
        in_specs=[vmem()] * 4,
        out_specs=[vmem()] * 4,
        compiler_params=params,
        cost_estimate=pl.CostEstimate(flops=2 * width * width * 3 * 512, bytes_accessed=9_000_000, transcendentals=0),
        name="prepare",
    )(w_qk, w_v, cube, sel)

    gathered = lax.all_gather(features, "group", axis=0, tiled=True)
    own = pl.pallas_call(
        aggregate_kernel,
        out_shape=shape((rows + 16, width), bf16),
        in_specs=[smem(), smem()] + [vmem()] * 4,
        out_specs=vmem(),
        compiler_params=params,
        name="aggregate",
    )(tile_src, tile_count, features, gathered, tiles, node_bucket.reshape(1, rows))

    everyone = lax.all_gather(own, "seq", axis=0, tiled=False)
    return pl.pallas_call(
        attend_kernel,
        out_shape=shape((rows, width), bf16),
        in_specs=[vmem()] * 7,
        out_specs=vmem(),
        scratch_shapes=[
            pltpu.VMEM((keys, wide), bf16),
            pltpu.VMEM((keys, wide), bf16),
            pltpu.VMEM((keys, LANES), bf16),
            pltpu.VMEM((rows, wide), bf16),
            pltpu.VMEM((rows, H * LANES), bf16),
            pltpu.VMEM((QUAD * rows, keys), jnp.float32),
            pltpu.VMEM((QUAD * rows, keys), jnp.float32),
            pltpu.VMEM((QUAD * rows, keys), bf16),
            pltpu.VMEM((QUAD * rows, keys), bf16),
            pltpu.VMEM((rows, wide), bf16),
        ],
        compiler_params=params,
        name="attend",
    )(own, everyone, wq, wk, wv, table, sel)


def solution(mesh):
    in_specs = (
        P(("group", "seq"), None),
        P(("group", "seq"), None),
        P(("group", "seq"), None),
        P(("group", "seq")),
        P(("group", "seq")),
        P(),
        P(),
        P(),
    )
    out_specs = P(("group", "seq"), None)
    return jax.shard_map(
        on_device, mesh=mesh, in_specs=in_specs, out_specs=out_specs, check_vma=False
    )
```

```python
import math

import jax
import jax.numpy as jnp
import numpy as np
from jax import lax
from jax.experimental import pallas as pl
from jax.experimental.pallas import tpu as pltpu
from jax.sharding import PartitionSpec as P

H = 32
HD = 24
NB = 16
TILES = 8
LANES = 128
PAD = 32
QUAD = LANES // PAD
WIDE = H * PAD
HALF = 16 * HD
HALF_PAD = 16 * PAD
NT = (((1,), (1,)), ((), ()))
MIB = 1024 * 1024
BF16 = jnp.bfloat16
F32 = jnp.float32


def vmem():
    return pl.BlockSpec(memory_space=pltpu.VMEM)


def smem():
    return pl.BlockSpec(memory_space=pltpu.SMEM)


def limit(mib):
    return pltpu.CompilerParams(vmem_limit_bytes=mib * MIB)


def shape(*dims, dtype=BF16):
    return jax.ShapeDtypeStruct(dims, dtype)


def cost(flops, nbytes):
    return pl.CostEstimate(flops=int(flops), bytes_accessed=int(nbytes), transcendentals=0)


def pad_matrix():
    rows = np.arange(HALF)
    cols = (rows // HD) * PAD + rows % HD
    sel = np.zeros((HALF, HALF_PAD), np.float32)
    sel[rows, cols] = 1.0
    return sel


def one_hot_slab(bucket_row):
    n = bucket_row.shape[1]
    index = lax.broadcasted_iota(jnp.int32, (LANES, n), 0)
    wanted = jnp.where(index < 3 * NB, index % NB, -1)
    hot = jnp.where(wanted == bucket_row, 1.0, 0.0)
    return hot.T.astype(BF16)


def prepare_kernel(w_qk_ref, w_v_ref, cube_ref, sel_ref, bucket_ref, wq_ref, wk_ref, wv_ref, bias_ref):
    width = w_v_ref.shape[1]
    sel = sel_ref[...]
    for src, base, dst in ((w_qk_ref, 0, wq_ref), (w_qk_ref, width, wk_ref), (w_v_ref, 0, wv_ref)):
        for part in range(width // HALF):
            block = src[:, base + part * HALF : base + (part + 1) * HALF]
            dst[:, part * HALF_PAD : (part + 1) * HALF_PAD] = jnp.dot(
                block, sel, preferred_element_type=F32
            ).astype(BF16)
    scaled = cube_ref[...] * math.sqrt(HD)
    high = scaled.astype(BF16).astype(F32)
    rest = scaled - high
    mid = rest.astype(BF16).astype(F32)
    low = rest - mid
    lane = lax.broadcasted_iota(jnp.int32, scaled.shape, 1) % LANES
    parts = jnp.where(
        lane < NB, high, jnp.where(lane < 2 * NB, mid, jnp.where(lane < 3 * NB, low, 0.0))
    )
    hot = one_hot_slab(bucket_ref[...])[:, :NB]
    bias_ref[...] = jnp.dot(hot, parts.astype(BF16), preferred_element_type=F32).astype(BF16)


def aggregate_kernel(src_ref, count_ref, me_ref, tiles_ref, *refs):
    feature_refs, out_ref, held = refs[:-2], refs[-2], refs[-1]
    rows = out_ref.shape[0]
    for d, ref in enumerate(feature_refs):
        held[d * rows : (d + 1) * rows, :] = ref[...]
    count = count_ref[0]
    me = me_ref[0]
    picked = []
    masked = []
    for t in range(TILES):
        start = pl.multiple_of((src_ref[0, t] ^ me) * rows, rows)
        picked.append(held[pl.ds(start, rows), :])
        tile = tiles_ref[:, t * rows : (t + 1) * rows]
        masked.append(jnp.where(t < count, tile, jnp.zeros_like(tile)))
    total = feature_refs[0][...].astype(F32) + jnp.dot(
        jnp.concatenate(masked, axis=1),
        jnp.concatenate(picked, axis=0),
        preferred_element_type=F32,
    )
    mean_square = jnp.mean(total * total, axis=-1, keepdims=True)
    out_ref[...] = (total * lax.rsqrt(mean_square + 1e-06)).astype(BF16)


def query_kernel(own_ref, wq_ref, bucket_ref, q_ref, hot_ref):
    rows = own_ref.shape[0]
    q_ref[...] = jnp.dot(own_ref[...], wq_ref[...], preferred_element_type=F32).astype(BF16)
    for s in range(bucket_ref.shape[0]):
        hot_ref[s * rows : (s + 1) * rows, :] = one_hot_slab(bucket_ref[s : s + 1, :])


def project_kernel(first_ref, second_ref, wk_ref, wv_ref, k_ref, v_ref):
    block = jnp.concatenate([first_ref[...], second_ref[...]], axis=0)
    for w_ref, dst in ((wk_ref, k_ref), (wv_ref, v_ref)):
        for n in range(0, WIDE, 256):
            dst[:, n : n + 256] = jnp.dot(
                block, w_ref[:, n : n + 256], preferred_element_type=F32
            ).astype(BF16)


def attend_kernel(q_ref, bias_ref, hot_ref, sel_ref, *refs):
    pairs = (len(refs) - 6) // 2
    k_refs, v_refs = refs[:pairs], refs[pairs : 2 * pairs]
    out_ref, x0_ref, x1_ref, p0_ref, p1_ref, heads_ref = refs[2 * pairs :]
    rows = out_ref.shape[0]
    span = k_refs[0].shape[0]
    quads = H // QUAD
    factor = math.log2(math.e) / math.sqrt(HD)
    lane_head = lax.broadcasted_iota(jnp.int32, (rows, LANES), 1) // PAD
    ones = jnp.ones((span, LANES), BF16)

    def scores(m, x_ref):
        cols = pl.ds(pl.multiple_of(m * LANES, LANES), LANES)
        q = q_ref[:, cols]
        zero = jnp.zeros_like(q)
        left = jnp.concatenate([jnp.where(lane_head == h, q, zero) for h in range(QUAD)], axis=0)
        right = jnp.concatenate(
            [
                bias_ref[:, pl.ds(pl.multiple_of((m * QUAD + h) * LANES, LANES), LANES)]
                for h in range(QUAD)
            ],
            axis=0,
        )
        query = jnp.concatenate([left, right], axis=1)
        for n, k_ref in enumerate(k_refs):
            part = slice(n * span, (n + 1) * span)
            key = jnp.concatenate([k_ref[:, cols], hot_ref[part, :]], axis=1)
            x_ref[:, part] = lax.dot_general(query, key, NT, preferred_element_type=F32)

    def mix(m, x_ref, p_ref):
        cols = pl.ds(pl.multiple_of(m * LANES, LANES), LANES)
        for r in range(0, QUAD * rows, 16):
            x = x_ref[r : r + 16, :]
            peak = jnp.max(x, axis=-1, keepdims=True)
            p_ref[r : r + 16, :] = jnp.exp2((x - peak) * factor).astype(BF16)
        value = jnp.concatenate(
            [jnp.concatenate([v_ref[:, cols], ones], axis=1) for v_ref in v_refs], axis=0
        )
        mixed = jnp.dot(p_ref[...], value, preferred_element_type=F32)
        top = mixed[:rows, :LANES]
        total = mixed[:rows, LANES:]
        for h in range(1, QUAD):
            top = jnp.where(lane_head == h, mixed[h * rows : (h + 1) * rows, :LANES], top)
            total = jnp.where(lane_head == h, mixed[h * rows : (h + 1) * rows, LANES:], total)
        heads_ref[:, cols] = (top / total).astype(BF16)

    scores(0, x0_ref)

    def two(i, carry):
        m = i * 2
        scores(m + 1, x1_ref)
        mix(m, x0_ref, p0_ref)
        scores(jnp.minimum(m + 2, quads - 1), x0_ref)
        mix(m + 1, x1_ref, p1_ref)
        return carry

    lax.fori_loop(0, quads // 2, two, 0)

    for part in range(out_ref.shape[1] // HALF):
        out_ref[:, part * HALF : (part + 1) * HALF] = lax.dot_general(
            heads_ref[:, part * HALF_PAD : (part + 1) * HALF_PAD], sel_ref[...], NT,
            preferred_element_type=F32,
        ).astype(BF16)


def swap(array, axis, distance):
    return lax.ppermute(array, axis, [(i, i ^ distance) for i in range(lax.axis_size(axis))])


def on_device(features, tiles, tile_src, tile_count, node_bucket, w_qk, w_v, bias_table):
    rows, width = features.shape
    groups = lax.axis_size("group")
    seq_count = lax.axis_size("seq")
    keys = seq_count * rows
    sel = jnp.asarray(pad_matrix(), BF16)
    own_bucket = node_bucket.reshape(1, rows)

    blocks = [features] + [swap(features, "group", d) for d in range(1, groups)]
    buckets = own_bucket
    step = 1
    while step < seq_count:
        buckets = jnp.concatenate([buckets, swap(buckets, "seq", step)], axis=0)
        step *= 2

    cube = bias_table.reshape(H, NB, NB).transpose(1, 0, 2)
    cube = jnp.concatenate([cube, cube, cube, jnp.zeros((NB, H, LANES - 3 * NB), F32)], axis=2)
    cube = cube.reshape(NB, H * LANES)
    wq, wk, wv, bias = pl.pallas_call(
        prepare_kernel,
        out_shape=[shape(width, WIDE)] * 3 + [shape(rows, H * LANES)],
        in_specs=[vmem()] * 5,
        out_specs=[vmem()] * 4,
        compiler_params=limit(24),
        cost_estimate=cost(6 * width * width * HALF_PAD, 10_000_000),
        name="prepare",
    )(w_qk, w_v, cube, sel, own_bucket)

    own = pl.pallas_call(
        aggregate_kernel,
        out_shape=shape(rows, width),
        in_specs=[smem()] * 3 + [vmem()] * (1 + groups),
        out_specs=vmem(),
        scratch_shapes=[pltpu.VMEM((groups * rows, width), BF16)],
        compiler_params=limit(24),
        name="aggregate",
    )(tile_src, tile_count, lax.axis_index("group").reshape(1), tiles, *blocks)

    far = [own] + [swap(own, "seq", 2 * d) for d in range(1, seq_count // 2)]
    near = [swap(block, "seq", 1) for block in far]

    q, hot = pl.pallas_call(
        query_kernel,
        out_shape=[shape(rows, WIDE), shape(keys, LANES)],
        in_specs=[vmem()] * 3,
        out_specs=[vmem()] * 2,
        compiler_params=limit(16),
        cost_estimate=cost(2 * rows * width * WIDE, 2_000_000),
        name="query",
    )(own, wq, buckets)
    k_parts = []
    v_parts = []
    for first, second in zip(far, near):
        k, v = pl.pallas_call(
            project_kernel,
            out_shape=[shape(2 * rows, WIDE)] * 2,
            in_specs=[vmem()] * 4,
            out_specs=[vmem()] * 2,
            compiler_params=limit(16),
            cost_estimate=cost(8 * rows * width * WIDE, 4_000_000),
            name="project",
        )(first, second, wk, wv)
        k_parts.append(k)
        v_parts.append(v)

    need = 2 * QUAD * rows * keys * 6 + 4 * keys * WIDE + 2 * keys * LANES
    return pl.pallas_call(
        attend_kernel,
        out_shape=shape(rows, width),
        in_specs=[vmem()] * (4 + 2 * len(k_parts)),
        out_specs=vmem(),
        scratch_shapes=[
            pltpu.VMEM((QUAD * rows, keys), F32),
            pltpu.VMEM((QUAD * rows, keys), F32),
            pltpu.VMEM((QUAD * rows, keys), BF16),
            pltpu.VMEM((QUAD * rows, keys), BF16),
            pltpu.VMEM((rows, WIDE), BF16),
        ],
        compiler_params=limit(need // MIB + 8),
        name="attend",
    )(q, bias, hot, sel, *k_parts, *v_parts)


def solution(mesh):
    in_specs = (
        P(("group", "seq"), None),
        P(("group", "seq"), None),
        P(("group", "seq"), None),
        P(("group", "seq")),
        P(("group", "seq")),
        P(),
        P(),
        P(),
    )
    out_specs = P(("group", "seq"), None)
    return jax.shard_map(
        on_device, mesh=mesh, in_specs=in_specs, out_specs=out_specs, check_vma=False
    )
```

```python
import math

import jax
import jax.numpy as jnp
import numpy as np
from jax import lax
from jax.experimental import pallas as pl
from jax.experimental.pallas import tpu as pltpu
from jax.sharding import PartitionSpec as P

H = 32
HD = 24
NB = 16
TILES = 8
LANES = 128
PAD = 32
QUAD = LANES // PAD
WIDE = H * PAD
HALF = 16 * HD
HALF_PAD = 16 * PAD
CHUNKS = 2
NT = (((1,), (1,)), ((), ()))
MIB = 1024 * 1024
BF16 = jnp.bfloat16
F32 = jnp.float32
FACTOR = math.log2(math.e) / math.sqrt(HD)
TOTAL_ROW = HD
PEAK_ROW = HD + 1


def vmem():
    return pl.BlockSpec(memory_space=pltpu.VMEM)


def smem():
    return pl.BlockSpec(memory_space=pltpu.SMEM)


def limit(mib):
    return pltpu.CompilerParams(vmem_limit_bytes=mib * MIB)


def shape(*dims, dtype=BF16):
    return jax.ShapeDtypeStruct(dims, dtype)


def cost(flops, nbytes):
    return pl.CostEstimate(flops=int(flops), bytes_accessed=int(nbytes), transcendentals=0)


def pad_matrix():
    rows = np.arange(HALF)
    sel = np.zeros((HALF_PAD, HALF), np.float32)
    sel[(rows // HD) * PAD + rows % HD, rows] = 1.0
    return sel


def one_hot_slab(bucket_row):
    n = bucket_row.shape[1]
    index = lax.broadcasted_iota(jnp.int32, (LANES, n), 0)
    wanted = jnp.where(index < 3 * NB, index % NB, -1)
    hot = jnp.where(wanted == bucket_row, 1.0, 0.0)
    return hot.T.astype(BF16)


def split_three(x):
    high = x.astype(BF16).astype(F32)
    rest = x - high
    mid = rest.astype(BF16).astype(F32)
    return high, mid, rest - mid


def weights_kernel(w_qk_ref, w_v_ref, sel_ref, wq_ref, wk_ref, wvt_ref):
    width = w_v_ref.shape[1]
    sel = sel_ref[...]
    for part in range(width // HALF):
        cols = slice(part * HALF_PAD, (part + 1) * HALF_PAD)
        for base, dst in ((0, wq_ref), (width, wk_ref)):
            block = w_qk_ref[:, base + part * HALF : base + (part + 1) * HALF]
            dst[:, cols] = lax.dot_general(block, sel, NT, preferred_element_type=F32).astype(BF16)
        block = w_v_ref[:, part * HALF : (part + 1) * HALF]
        wvt_ref[cols, :] = lax.dot_general(sel, block, NT, preferred_element_type=F32).astype(BF16)


def bias_kernel(cube_ref, own_ref, sister_ref, *refs):
    bucket_refs, bias_ref, hot_ref = refs[:-2], refs[-2], refs[-1]
    rows = own_ref.shape[1]
    high, mid, low = split_three(cube_ref[...] * math.sqrt(HD))
    lane = lax.broadcasted_iota(jnp.int32, high.shape, 1) % LANES
    parts = jnp.where(
        lane < NB, high, jnp.where(lane < 2 * NB, mid, jnp.where(lane < 3 * NB, low, 0.0))
    ).astype(BF16)
    slab = one_hot_slab(own_ref[...])
    both = jnp.concatenate([slab, one_hot_slab(sister_ref[...])], axis=0)[:, :NB]
    bias_ref[...] = jnp.dot(both, parts, preferred_element_type=F32).astype(BF16)
    hot_ref[:rows, :] = slab
    for s, ref in enumerate(bucket_refs):
        hot_ref[(s + 1) * rows : (s + 2) * rows, :] = one_hot_slab(ref[...])


def aggregate_kernel(column, src_ref, count_ref, me_ref, tiles_ref, features_ref, *refs):
    received, out_ref, held = refs[:-2], refs[-2], refs[-1]
    rows, span = out_ref.shape
    own = features_ref[:, column : column + span]
    held[:rows, :] = own
    for d, ref in enumerate(received):
        held[(d + 1) * rows : (d + 2) * rows, :] = ref[...]
    count = count_ref[0]
    me = me_ref[0]
    picked = []
    masked = []
    for t in range(TILES):
        start = pl.multiple_of((src_ref[0, t] ^ me) * rows, rows)
        picked.append(held[pl.ds(start, rows), :])
        tile = tiles_ref[:, t * rows : (t + 1) * rows]
        masked.append(jnp.where(t < count, tile, jnp.zeros_like(tile)))
    total = own.astype(F32) + jnp.dot(
        jnp.concatenate(masked, axis=1),
        jnp.concatenate(picked, axis=0),
        preferred_element_type=F32,
    )
    out_ref[...] = total.astype(BF16)


def normed(refs):
    block = jnp.concatenate([ref[...] for ref in refs], axis=1).astype(F32)
    mean_square = jnp.mean(block * block, axis=-1, keepdims=True)
    return (block * lax.rsqrt(mean_square + 1e-06)).astype(BF16)


def query_kernel(*refs):
    wq_ref, q_ref = refs[-2:]
    block = jnp.concatenate([normed(refs[:CHUNKS]), normed(refs[CHUNKS : 2 * CHUNKS])], axis=0)
    for n in range(0, WIDE, 256):
        q_ref[:, n : n + 256] = jnp.dot(
            block, wq_ref[:, n : n + 256], preferred_element_type=F32
        ).astype(BF16)


def part_kernel(first, last, q_ref, bias_ref, hot_ref, wk_ref, wvt_ref, *refs):
    block_refs, refs = refs[: 2 * CHUNKS], refs[2 * CHUNKS :]
    k_ref, vt_ref = refs[-2:]
    refs = refs[:-2]
    if not first:
        state_ref, refs = refs[0], refs[1:]
    queries = q_ref.shape[0]
    keys = k_ref.shape[0]
    block = jnp.concatenate(
        [normed(block_refs[:CHUNKS]), normed(block_refs[CHUNKS:])], axis=0
    )
    ones_row = lax.broadcasted_iota(jnp.int32, (256, keys), 0) % PAD == TOTAL_ROW
    for n in range(0, WIDE, 256):
        k_ref[:, n : n + 256] = jnp.dot(
            block, wk_ref[:, n : n + 256], preferred_element_type=F32
        ).astype(BF16)
        vt = lax.dot_general(wvt_ref[n : n + 256, :], block, NT, preferred_element_type=F32)
        vt_ref[n : n + 256, :] = jnp.where(ones_row, 1.0, vt).astype(BF16)

    lane_head = lax.broadcasted_iota(jnp.int32, (queries, LANES), 1) // PAD
    row = lax.broadcasted_iota(jnp.int32, (PAD, queries), 0)

    def quad(m, carry):
        cols = pl.ds(pl.multiple_of(m * LANES, LANES), LANES)
        q = q_ref[:, cols]
        zero = jnp.zeros_like(q)
        key = jnp.concatenate([k_ref[:, cols], hot_ref[...]], axis=1)
        for h in range(QUAD):
            head = m * QUAD + h
            bias = bias_ref[:, pl.ds(pl.multiple_of(head * LANES, LANES), LANES)]
            query = jnp.concatenate([jnp.where(lane_head == h, q, zero), bias], axis=1)
            x = lax.dot_general(key, query, NT, preferred_element_type=F32)
            peak = jnp.max(x, axis=0, keepdims=True)
            weights = jnp.exp2((x - peak) * FACTOR).astype(BF16)
            rows = pl.ds(pl.multiple_of(head * PAD, PAD), PAD)
            mixed = jnp.dot(vt_ref[rows, :], weights, preferred_element_type=F32)
            if not first:
                state = state_ref[rows, :]
                before = state[PEAK_ROW : PEAK_ROW + 1, :]
                top = jnp.maximum(before, peak)
                mixed = mixed * jnp.exp2((peak - top) * FACTOR) + state * jnp.exp2(
                    (before - top) * FACTOR
                )
                peak = top
            if not last:
                refs[0][rows, :] = jnp.where(row == PEAK_ROW, peak, mixed)
            else:
                total = mixed[TOTAL_ROW : TOTAL_ROW + 1, :]
                level = peak * FACTOR + jnp.log2(total)
                mixed = mixed / total
                own = mixed[:, : queries // 2]
                refs[0][rows, :] = jnp.where(row[:, : queries // 2] == HD, level[:, : queries // 2], own)
                high, mid, low = split_three(level[:, queries // 2 :])
                sent = mixed[:, queries // 2 :]
                for at, piece in ((HD, high), (HD + 1, mid), (HD + 2, low)):
                    sent = jnp.where(row[:, queries // 2 :] == at, piece, sent)
                refs[1][rows, :] = sent.astype(BF16)
        return carry

    lax.fori_loop(0, H // QUAD, quad, 0)


def merge_kernel(own_ref, other_ref, out_ref, turned):
    for head in range(H):
        own = own_ref[head * PAD : (head + 1) * PAD, :]
        other = other_ref[head * PAD : (head + 1) * PAD, :].astype(F32)
        level = own[HD : HD + 1, :]
        level_other = (
            other[HD : HD + 1, :] + other[HD + 1 : HD + 2, :] + other[HD + 2 : HD + 3, :]
        )
        top = jnp.maximum(level, level_other)
        share = jnp.exp2(level - top)
        share_other = jnp.exp2(level_other - top)
        mixed = (own[:HD, :] * share + other[:HD, :] * share_other) / (share + share_other)
        turned[head * HD : (head + 1) * HD, :] = mixed
    for n in range(0, H * HD, LANES):
        out_ref[:, n : n + LANES] = turned[n : n + LANES, :].T.astype(BF16)


def swap(array, axis, distance):
    return lax.ppermute(array, axis, [(i, i ^ distance) for i in range(lax.axis_size(axis))])


def on_device(features, tiles, tile_src, tile_count, node_bucket, w_qk, w_v, bias_table):
    rows, width = features.shape
    groups = lax.axis_size("group")
    chips = lax.axis_size("seq") // 2
    span = width // CHUNKS
    sel = jnp.asarray(pad_matrix(), BF16)
    own_bucket = node_bucket.reshape(1, rows)
    me = lax.axis_index("group").reshape(1)

    received = []
    for c in range(CHUNKS):
        chunk = features[:, c * span : (c + 1) * span]
        received.append([swap(chunk, "group", d) for d in range(groups - 1, 0, -1)][::-1])
    sister_bucket = swap(own_bucket, "seq", 1)
    buckets = [swap(own_bucket, "seq", 2 * d) for d in range(1, chips)]

    wq, wk, wvt = pl.pallas_call(
        weights_kernel,
        out_shape=[shape(width, WIDE)] * 2 + [shape(WIDE, width)],
        in_specs=[vmem()] * 3,
        out_specs=[vmem()] * 3,
        compiler_params=limit(24),
        cost_estimate=cost(6 * width * width * HALF_PAD, 10_000_000),
        name="weights",
    )(w_qk, w_v, sel)

    cube = bias_table.reshape(H, NB, NB).transpose(1, 0, 2)
    cube = jnp.concatenate([cube, cube, cube, jnp.zeros((NB, H, LANES - 3 * NB), F32)], axis=2)
    cube = cube.reshape(NB, H * LANES)
    bias, hot = pl.pallas_call(
        bias_kernel,
        out_shape=[shape(2 * rows, H * LANES), shape(chips * rows, LANES)],
        in_specs=[vmem()] * (2 + chips),
        out_specs=[vmem()] * 2,
        compiler_params=limit(16),
        cost_estimate=cost(2 * 2 * rows * 256 * H * LANES, 4_000_000),
        name="bias",
    )(cube, own_bucket, sister_bucket, *buckets)

    blocks = [[] for _ in range(chips)]
    sister = []
    for c in range(CHUNKS):
        own = pl.pallas_call(
            lambda *refs, c=c: aggregate_kernel(c * span, *refs),
            out_shape=shape(rows, span),
            in_specs=[smem()] * 3 + [vmem()] * (1 + groups),
            out_specs=vmem(),
            scratch_shapes=[pltpu.VMEM((groups * rows, span), BF16)],
            compiler_params=limit(16),
            cost_estimate=cost(2 * rows * TILES * 256 * span, 1_000_000),
            name="aggregate",
        )(tile_src, tile_count, me, tiles, features, *received[c])
        blocks[0].append(own)
        for d in range(chips - 1, 0, -1):
            blocks[d].append(swap(own, "seq", 2 * d))
        sister.append(swap(own, "seq", 1))

    q = pl.pallas_call(
        query_kernel,
        out_shape=shape(2 * rows, WIDE),
        in_specs=[vmem()] * (2 * CHUNKS + 1),
        out_specs=vmem(),
        compiler_params=limit(16),
        cost_estimate=cost(4 * rows * width * WIDE, 2_000_000),
        name="query",
    )(*blocks[0], *sister, wq)

    state = []
    for p in range(0, chips, 2):
        first, last = p == 0, p + 2 >= chips
        if last:
            outs = [shape(WIDE, rows, dtype=F32), shape(WIDE, rows)]
        else:
            outs = [shape(WIDE, 2 * rows, dtype=F32)]
        state = pl.pallas_call(
            lambda *refs, first=first, last=last: part_kernel(first, last, *refs),
            out_shape=outs,
            in_specs=[vmem()] * (5 + 2 * CHUNKS + len(state)),
            out_specs=[vmem()] * len(outs),
            scratch_shapes=[pltpu.VMEM((2 * rows, WIDE), BF16), pltpu.VMEM((WIDE, 2 * rows), BF16)],
            compiler_params=limit(24),
            cost_estimate=cost(8_000_000_000 // 2, 8_000_000),
            name="part",
        )(q, bias, hot[p * rows : (p + 2) * rows], wk, wvt, *blocks[p], *blocks[p + 1], *state)

    partial, payload = state
    return pl.pallas_call(
        merge_kernel,
        out_shape=shape(rows, width),
        in_specs=[vmem()] * 2,
        out_specs=vmem(),
        scratch_shapes=[pltpu.VMEM((width, rows), F32)],
        compiler_params=limit(16),
        name="merge",
    )(partial, swap(payload, "seq", 1))


def solution(mesh):
    in_specs = (
        P(("group", "seq"), None),
        P(("group", "seq"), None),
        P(("group", "seq"), None),
        P(("group", "seq")),
        P(("group", "seq")),
        P(),
        P(),
        P(),
    )
    out_specs = P(("group", "seq"), None)
    return jax.shard_map(
        on_device, mesh=mesh, in_specs=in_specs, out_specs=out_specs, check_vma=False
    )
```

```python
import math

import jax
import jax.numpy as jnp
import numpy as np
from jax import lax
from jax.experimental import pallas as pl
from jax.experimental.pallas import tpu as pltpu
from jax.sharding import PartitionSpec as P

H = 32
HD = 24
NB = 16
TILES = 8
LANES = 128
PAD = 32
QUAD = LANES // PAD
WIDE = H * PAD
HALF = 16 * HD
HALF_PAD = 16 * PAD
NT = (((1,), (1,)), ((), ()))
MIB = 1024 * 1024
BF16 = jnp.bfloat16
F32 = jnp.float32
FACTOR = math.log2(math.e) / math.sqrt(HD)


def vmem():
    return pl.BlockSpec(memory_space=pltpu.VMEM)


def smem():
    return pl.BlockSpec(memory_space=pltpu.SMEM)


def limit(mib):
    return pltpu.CompilerParams(vmem_limit_bytes=mib * MIB)


def shape(*dims, dtype=BF16):
    return jax.ShapeDtypeStruct(dims, dtype)


def cost(flops, nbytes):
    return pl.CostEstimate(flops=int(flops), bytes_accessed=int(nbytes), transcendentals=0)


def pad_matrix():
    rows = np.arange(HALF)
    cols = (rows // HD) * PAD + rows % HD
    sel = np.zeros((HALF, HALF_PAD), np.float32)
    sel[rows, cols] = 1.0
    return sel


def one_hot_slab(bucket_row):
    n = bucket_row.shape[1]
    index = lax.broadcasted_iota(jnp.int32, (LANES, n), 0)
    wanted = jnp.where(index < 3 * NB, index % NB, -1)
    hot = jnp.where(wanted == bucket_row, 1.0, 0.0)
    return hot.T.astype(BF16)


def prepare_kernel(w_qk_ref, w_v_ref, cube_ref, sel_ref, bucket_ref, wq_ref, wk_ref, wv_ref, bias_ref):
    width = w_v_ref.shape[1]
    sel = sel_ref[...]
    for src, base, dst in ((w_qk_ref, 0, wq_ref), (w_qk_ref, width, wk_ref), (w_v_ref, 0, wv_ref)):
        for part in range(width // HALF):
            block = src[:, base + part * HALF : base + (part + 1) * HALF]
            dst[:, part * HALF_PAD : (part + 1) * HALF_PAD] = jnp.dot(
                block, sel, preferred_element_type=F32
            ).astype(BF16)
    scaled = cube_ref[...] * math.sqrt(HD)
    high = scaled.astype(BF16).astype(F32)
    rest = scaled - high
    mid = rest.astype(BF16).astype(F32)
    low = rest - mid
    lane = lax.broadcasted_iota(jnp.int32, scaled.shape, 1) % LANES
    parts = jnp.where(
        lane < NB, high, jnp.where(lane < 2 * NB, mid, jnp.where(lane < 3 * NB, low, 0.0))
    )
    hot = one_hot_slab(bucket_ref[...])[:, :NB]
    bias_ref[...] = jnp.dot(hot, parts.astype(BF16), preferred_element_type=F32).astype(BF16)


def aggregate_kernel(src_ref, count_ref, me_ref, tiles_ref, *refs):
    feature_refs, out_ref, held = refs[:-4], refs[-2], refs[-1]
    rows = out_ref.shape[0]
    for d, ref in enumerate(feature_refs):
        held[d * rows : (d + 1) * rows, :] = ref[...]
    count = count_ref[0]
    me = me_ref[0]
    picked = []
    masked = []
    for t in range(TILES):
        start = pl.multiple_of((src_ref[0, t] ^ me) * rows, rows)
        picked.append(held[pl.ds(start, rows), :])
        tile = tiles_ref[:, t * rows : (t + 1) * rows]
        masked.append(jnp.where(t < count, tile, jnp.zeros_like(tile)))
    total = feature_refs[0][...].astype(F32) + jnp.dot(
        jnp.concatenate(masked, axis=1),
        jnp.concatenate(picked, axis=0),
        preferred_element_type=F32,
    )
    mean_square = jnp.mean(total * total, axis=-1, keepdims=True)
    out_ref[...] = (total * lax.rsqrt(mean_square + 1e-06)).astype(BF16)


def query_kernel(own_ref, wq_ref, q_ref):
    q_ref[...] = jnp.dot(own_ref[...], wq_ref[...], preferred_element_type=F32).astype(BF16)


def hot_kernel(bucket_ref, *hot_refs):
    rows = bucket_ref.shape[1]
    s = 0
    for hot_ref in hot_refs:
        for at in range(0, hot_ref.shape[0], rows):
            hot_ref[at : at + rows, :] = one_hot_slab(bucket_ref[s : s + 1, :])
            s += 1


def part_kernel(first, last, q_ref, bias_ref, hot_ref, wk_ref, wv_ref, *refs):
    count = hot_ref.shape[0] // q_ref.shape[0]
    block_refs, refs = refs[:count], refs[count:]
    k_ref, v_ref, x0_ref, x1_ref, p0_ref, p1_ref, t0_ref, t1_ref, heads_ref = refs[-9:]
    refs = refs[:-9]
    old_refs = ()
    if not first:
        old_refs, refs = refs[:3], refs[3:]
    rows = q_ref.shape[0]
    keys = hot_ref.shape[0]
    quads = H // QUAD
    block = jnp.concatenate([ref[...] for ref in block_refs], axis=0)
    for w_ref, dst in ((wk_ref, k_ref), (wv_ref, v_ref)):
        for n in range(0, WIDE, 256):
            dst[:, n : n + 256] = jnp.dot(
                block, w_ref[:, n : n + 256], preferred_element_type=F32
            ).astype(BF16)

    lane_head = lax.broadcasted_iota(jnp.int32, (rows, LANES), 1) // PAD
    ones = jnp.ones((keys, LANES), BF16)

    def scores(m, x_ref):
        cols = pl.ds(pl.multiple_of(m * LANES, LANES), LANES)
        q = q_ref[:, cols]
        zero = jnp.zeros_like(q)
        left = jnp.concatenate([jnp.where(lane_head == h, q, zero) for h in range(QUAD)], axis=0)
        right = jnp.concatenate(
            [
                bias_ref[:, pl.ds(pl.multiple_of((m * QUAD + h) * LANES, LANES), LANES)]
                for h in range(QUAD)
            ],
            axis=0,
        )
        query = jnp.concatenate([left, right], axis=1)
        for n in range(0, keys, 256):
            key = jnp.concatenate([k_ref[n : n + 256, cols], hot_ref[n : n + 256, :]], axis=1)
            x_ref[:, n : n + 256] = lax.dot_general(query, key, NT, preferred_element_type=F32)

    def pick(array):
        out = array[:rows, :]
        for h in range(1, QUAD):
            out = jnp.where(lane_head == h, array[h * rows : (h + 1) * rows, :], out)
        return out

    def mix(m, x_ref, p_ref, t_ref):
        cols = pl.ds(pl.multiple_of(m * LANES, LANES), LANES)
        for r in range(0, QUAD * rows, 16):
            x = x_ref[r : r + 16, :]
            peak = jnp.max(x, axis=-1, keepdims=True)
            p_ref[r : r + 16, :] = jnp.exp2((x - peak) * FACTOR).astype(BF16)
            if not (first and last):
                t_ref[r : r + 16, :] = jnp.broadcast_to(peak, (16, LANES))
        value = jnp.concatenate([v_ref[:, cols], ones], axis=1)
        mixed = jnp.dot(p_ref[...], value, preferred_element_type=F32)
        top = pick(mixed[:, :LANES])
        total = pick(mixed[:, LANES:])
        if not (first and last):
            peak = pick(t_ref[...])
        if not first:
            old_top, old_total, old_peak = (ref[:, cols] for ref in old_refs)
            best = jnp.maximum(old_peak, peak)
            new_share = jnp.exp2((peak - best) * FACTOR)
            old_share = jnp.exp2((old_peak - best) * FACTOR)
            top = top * new_share + old_top * old_share
            total = total * new_share + old_total * old_share
            peak = best
        if last:
            heads_ref[:, cols] = (top / total).astype(BF16)
        else:
            refs[0][:, cols] = top
            refs[1][:, cols] = total
            refs[2][:, cols] = peak

    scores(0, x0_ref)

    def two(i, carry):
        m = i * 2
        scores(m + 1, x1_ref)
        mix(m, x0_ref, p0_ref, t0_ref)
        scores(jnp.minimum(m + 2, quads - 1), x0_ref)
        mix(m + 1, x1_ref, p1_ref, t1_ref)
        return carry

    lax.fori_loop(0, quads // 2, two, 0)

    if last:
        sel_ref, out_ref = refs
        for part in range(out_ref.shape[1] // HALF):
            out_ref[:, part * HALF : (part + 1) * HALF] = lax.dot_general(
                heads_ref[:, part * HALF_PAD : (part + 1) * HALF_PAD], sel_ref[...], NT,
                preferred_element_type=F32,
            ).astype(BF16)


def attend_part(first, last, q, bias, hot, wk, wv, blocks, state, sel, width):
    rows = q.shape[0]
    keys = rows * len(blocks)
    if last:
        outs, extra = [shape(rows, width)], [sel]
    else:
        outs, extra = [shape(rows, WIDE, dtype=F32)] * 3, []
    operands = [q, bias, hot, wk, wv, *blocks, *state, *extra]
    tall = QUAD * rows
    need = 2 * tall * keys * 6 + 4 * keys * WIDE + 2 * tall * LANES * 4
    return pl.pallas_call(
        lambda *refs: part_kernel(first, last, *refs),
        out_shape=outs,
        in_specs=[vmem()] * len(operands),
        out_specs=[vmem()] * len(outs),
        scratch_shapes=[
            pltpu.VMEM((keys, WIDE), BF16),
            pltpu.VMEM((keys, WIDE), BF16),
            pltpu.VMEM((tall, keys), F32),
            pltpu.VMEM((tall, keys), F32),
            pltpu.VMEM((tall, keys), BF16),
            pltpu.VMEM((tall, keys), BF16),
            pltpu.VMEM((tall, LANES), F32),
            pltpu.VMEM((tall, LANES), F32),
            pltpu.VMEM((rows, WIDE), BF16),
        ],
        compiler_params=limit(need // MIB + 16),
        cost_estimate=cost(4 * keys * width * WIDE + 4 * tall * keys * 256 * (H // QUAD), 8_000_000),
        name="part",
    )(*operands)


def swap(array, axis, distance):
    return lax.ppermute(array, axis, [(i, i ^ distance) for i in range(lax.axis_size(axis))])


def on_device(features, tiles, tile_src, tile_count, node_bucket, w_qk, w_v, bias_table):
    rows, width = features.shape
    groups = lax.axis_size("group")
    seq_count = lax.axis_size("seq")
    keys = seq_count * rows
    sel = jnp.asarray(pad_matrix(), BF16)
    own_bucket = node_bucket.reshape(1, rows)

    blocks = [swap(features, "group", d) for d in range(groups - 1, 0, -1)] + [features]
    blocks = blocks[::-1]
    buckets = own_bucket
    step = 1
    while step < seq_count:
        buckets = jnp.concatenate([buckets, swap(buckets, "seq", step)], axis=0)
        step *= 2

    cube = bias_table.reshape(H, NB, NB).transpose(1, 0, 2)
    cube = jnp.concatenate([cube, cube, cube, jnp.zeros((NB, H, LANES - 3 * NB), F32)], axis=2)
    cube = cube.reshape(NB, H * LANES)
    wq, wk, wv, bias = pl.pallas_call(
        prepare_kernel,
        out_shape=[shape(width, WIDE)] * 3 + [shape(rows, H * LANES)],
        in_specs=[vmem()] * 5,
        out_specs=[vmem()] * 4,
        compiler_params=limit(24),
        cost_estimate=cost(6 * width * width * HALF_PAD, 10_000_000),
        name="prepare",
    )(w_qk, w_v, cube, sel, own_bucket)

    chips = seq_count // 2
    parts = [[0, 1]] + [[d] for d in range(2, chips)]
    hot = pl.pallas_call(
        hot_kernel,
        out_shape=[shape(2 * len(part) * rows, LANES) for part in parts],
        in_specs=[vmem()],
        out_specs=[vmem()] * len(parts),
        compiler_params=limit(16),
        cost_estimate=cost(keys * LANES, 300_000),
        name="hot",
    )(buckets)

    own = pl.pallas_call(
        aggregate_kernel,
        out_shape=shape(rows, width),
        in_specs=[smem()] * 3 + [vmem()] * (1 + groups) + [pl.BlockSpec(memory_space=pl.ANY)] * 2,
        out_specs=vmem(),
        scratch_shapes=[pltpu.VMEM((groups * rows, width), BF16)],
        compiler_params=limit(24),
        name="aggregate",
    )(tile_src, tile_count, lax.axis_index("group").reshape(1), tiles, *blocks, wv, hot[0])

    far = [own] + [None] * (chips - 1)
    for d in range(1, chips):
        far[d] = swap(own, "seq", 2 * d)
    near = [swap(own, "seq", 1)]

    q = pl.pallas_call(
        query_kernel,
        out_shape=shape(rows, WIDE),
        in_specs=[vmem()] * 2,
        out_specs=vmem(),
        compiler_params=limit(16),
        cost_estimate=cost(2 * rows * width * WIDE, 2_000_000),
        name="query",
    )(own, wq)

    state = []
    for number, part in enumerate(parts):
        blocks = []
        for d in part:
            block = far[d]
            if state:
                block, state = lax.optimization_barrier((block, state))
            if d:
                near.append(swap(block, "seq", 1))
            blocks += [block, near[d]]
        state = attend_part(
            number == 0, number == len(parts) - 1, q, bias,
            hot[number], wk, wv, blocks, state, sel, width,
        )
    return state[0]


def solution(mesh):
    in_specs = (
        P(("group", "seq"), None),
        P(("group", "seq"), None),
        P(("group", "seq"), None),
        P(("group", "seq")),
        P(("group", "seq")),
        P(),
        P(),
        P(),
    )
    out_specs = P(("group", "seq"), None)
    return jax.shard_map(
        on_device, mesh=mesh, in_specs=in_specs, out_specs=out_specs, check_vma=False
    )
```

```python
import math

import jax
import jax.numpy as jnp
import numpy as np
from jax import lax
from jax.experimental import pallas as pl
from jax.experimental.pallas import tpu as pltpu
from jax.sharding import PartitionSpec as P

H = 32
HD = 24
NB = 16
TILES = 8
LANES = 128
PAD = 32
QUAD = LANES // PAD
WIDE = H * PAD
HALF = 16 * HD
HALF_PAD = 16 * PAD
NT = (((1,), (1,)), ((), ()))
MIB = 1024 * 1024
BF16 = jnp.bfloat16
F32 = jnp.float32
FACTOR = math.log2(math.e) / math.sqrt(HD)


def vmem():
    return pl.BlockSpec(memory_space=pltpu.VMEM)


def smem():
    return pl.BlockSpec(memory_space=pltpu.SMEM)


def limit(mib):
    return pltpu.CompilerParams(vmem_limit_bytes=mib * MIB)


def shape(*dims, dtype=BF16):
    return jax.ShapeDtypeStruct(dims, dtype)


def cost(flops, nbytes):
    return pl.CostEstimate(flops=int(flops), bytes_accessed=int(nbytes), transcendentals=0)


def pad_matrix():
    rows = np.arange(HALF)
    cols = (rows // HD) * PAD + rows % HD
    sel = np.zeros((HALF, HALF_PAD), np.float32)
    sel[rows, cols] = 1.0
    return sel


def one_hot_slab(bucket_row):
    n = bucket_row.shape[1]
    index = lax.broadcasted_iota(jnp.int32, (LANES, n), 0)
    wanted = jnp.where(index < 3 * NB, index % NB, -1)
    hot = jnp.where(wanted == bucket_row, 1.0, 0.0)
    return hot.T.astype(BF16)


def stage_kernel(
    count_ref, me_ref, cube_ref, bucket_ref, features_ref, tiles_ref, *refs
):
    bias_ref, own_ref, masked_ref, hot_refs = refs[0], refs[1], refs[2], refs[3:]
    rows = features_ref.shape[0]
    me = me_ref[0]
    own_ref[...] = features_ref[...]
    for t in range(TILES):
        tile = tiles_ref[:, t * rows : (t + 1) * rows]
        masked_ref[:, t * rows : (t + 1) * rows] = jnp.where(
            t < count_ref[0], tile, jnp.zeros_like(tile)
        )
    s = 0
    for hot_ref in hot_refs:
        for at in range(0, hot_ref.shape[0], rows):
            hot_ref[at : at + rows, :] = one_hot_slab(bucket_ref[pl.ds(me ^ s, 1), :])
            s += 1
    scaled = cube_ref[...] * math.sqrt(HD)
    high = scaled.astype(BF16).astype(F32)
    rest = scaled - high
    mid = rest.astype(BF16).astype(F32)
    low = rest - mid
    lane = lax.broadcasted_iota(jnp.int32, scaled.shape, 1) % LANES
    parts = jnp.where(
        lane < NB, high, jnp.where(lane < 2 * NB, mid, jnp.where(lane < 3 * NB, low, 0.0))
    )
    hot = one_hot_slab(bucket_ref[pl.ds(me, 1), :])[:, :NB]
    bias_ref[...] = jnp.dot(hot, parts.astype(BF16), preferred_element_type=F32).astype(BF16)


def aggregate_kernel(src_ref, me_ref, masked_ref, *refs):
    feature_refs, out_ref, held = refs[:-2], refs[-2], refs[-1]
    rows = out_ref.shape[0]
    for d, ref in enumerate(feature_refs):
        held[d * rows : (d + 1) * rows, :] = ref[...]
    me = me_ref[0]
    picked = []
    for t in range(TILES):
        start = pl.multiple_of((src_ref[0, t] ^ me) * rows, rows)
        picked.append(held[pl.ds(start, rows), :])
    total = feature_refs[0][...].astype(F32) + jnp.dot(
        masked_ref[...], jnp.concatenate(picked, axis=0), preferred_element_type=F32
    )
    mean_square = jnp.mean(total * total, axis=-1, keepdims=True)
    out_ref[...] = (total * lax.rsqrt(mean_square + 1e-06)).astype(BF16)


def project(block, w_ref, base, sel, dst):
    width = block.shape[1]
    for part in range(width // HALF):
        raw = jnp.dot(
            block, w_ref[:, base + part * HALF : base + (part + 1) * HALF],
            preferred_element_type=F32,
        ).astype(BF16)
        dst[:, part * HALF_PAD : (part + 1) * HALF_PAD] = jnp.dot(
            raw, sel, preferred_element_type=F32
        ).astype(BF16)


def query_kernel(own_ref, w_qk_ref, sel_ref, q_ref):
    project(own_ref[...], w_qk_ref, 0, sel_ref[...], q_ref)


def part_kernel(first, last, q_ref, bias_ref, hot_ref, w_qk_ref, w_v_ref, sel_ref, *refs):
    count = hot_ref.shape[0] // q_ref.shape[0]
    block_refs, refs = refs[:count], refs[count:]
    k_ref, v_ref, x0_ref, x1_ref, p0_ref, p1_ref, t0_ref, t1_ref, heads_ref = refs[-9:]
    refs = refs[:-9]
    old_refs = ()
    if not first:
        old_refs, refs = refs[:3], refs[3:]
    rows = q_ref.shape[0]
    keys = hot_ref.shape[0]
    quads = H // QUAD
    block = jnp.concatenate([ref[...] for ref in block_refs], axis=0)
    sel = sel_ref[...]
    project(block, w_qk_ref, block.shape[1], sel, k_ref)
    project(block, w_v_ref, 0, sel, v_ref)

    lane_head = lax.broadcasted_iota(jnp.int32, (rows, LANES), 1) // PAD
    ones = jnp.ones((keys, LANES), BF16)

    def scores(m, x_ref):
        cols = pl.ds(pl.multiple_of(m * LANES, LANES), LANES)
        q = q_ref[:, cols]
        zero = jnp.zeros_like(q)
        left = jnp.concatenate([jnp.where(lane_head == h, q, zero) for h in range(QUAD)], axis=0)
        right = jnp.concatenate(
            [
                bias_ref[:, pl.ds(pl.multiple_of((m * QUAD + h) * LANES, LANES), LANES)]
                for h in range(QUAD)
            ],
            axis=0,
        )
        query = jnp.concatenate([left, right], axis=1)
        for n in range(0, keys, 256):
            key = jnp.concatenate([k_ref[n : n + 256, cols], hot_ref[n : n + 256, :]], axis=1)
            x_ref[:, n : n + 256] = lax.dot_general(query, key, NT, preferred_element_type=F32)

    def pick(array):
        out = array[:rows, :]
        for h in range(1, QUAD):
            out = jnp.where(lane_head == h, array[h * rows : (h + 1) * rows, :], out)
        return out

    def mix(m, x_ref, p_ref, t_ref):
        cols = pl.ds(pl.multiple_of(m * LANES, LANES), LANES)
        for r in range(0, QUAD * rows, 16):
            x = x_ref[r : r + 16, :]
            peak = jnp.max(x, axis=-1, keepdims=True)
            p_ref[r : r + 16, :] = jnp.exp2((x - peak) * FACTOR).astype(BF16)
            if not (first and last):
                t_ref[r : r + 16, :] = jnp.broadcast_to(peak, (16, LANES))
        value = jnp.concatenate([v_ref[:, cols], ones], axis=1)
        mixed = jnp.dot(p_ref[...], value, preferred_element_type=F32)
        top = pick(mixed[:, :LANES])
        total = pick(mixed[:, LANES:])
        if not (first and last):
            peak = pick(t_ref[...])
        if not first:
            old_top, old_total, old_peak = (ref[:, cols] for ref in old_refs)
            best = jnp.maximum(old_peak, peak)
            new_share = jnp.exp2((peak - best) * FACTOR)
            old_share = jnp.exp2((old_peak - best) * FACTOR)
            top = top * new_share + old_top * old_share
            total = total * new_share + old_total * old_share
            peak = best
        if last:
            heads_ref[:, cols] = (top / total).astype(BF16)
        else:
            refs[0][:, cols] = top
            refs[1][:, cols] = total
            refs[2][:, cols] = peak

    scores(0, x0_ref)

    def two(i, carry):
        m = i * 2
        scores(m + 1, x1_ref)
        mix(m, x0_ref, p0_ref, t0_ref)
        scores(jnp.minimum(m + 2, quads - 1), x0_ref)
        mix(m + 1, x1_ref, p1_ref, t1_ref)
        return carry

    lax.fori_loop(0, quads // 2, two, 0)

    if last:
        out_ref = refs[0]
        for part in range(out_ref.shape[1] // HALF):
            out_ref[:, part * HALF : (part + 1) * HALF] = lax.dot_general(
                heads_ref[:, part * HALF_PAD : (part + 1) * HALF_PAD], sel, NT,
                preferred_element_type=F32,
            ).astype(BF16)


def attend_part(first, last, q, bias, hot, w_qk, w_v, sel, blocks, state):
    rows = q.shape[0]
    keys = rows * len(blocks)
    if last:
        outs = [shape(*blocks[0].shape)]
    else:
        outs = [shape(rows, WIDE, dtype=F32)] * 3
    operands = [q, bias, hot, w_qk, w_v, sel, *blocks, *state]
    tall = QUAD * rows
    need = 2 * tall * keys * 6 + 4 * keys * WIDE + 2 * tall * LANES * 4
    return pl.pallas_call(
        lambda *refs: part_kernel(first, last, *refs),
        out_shape=outs,
        in_specs=[vmem()] * len(operands),
        out_specs=[vmem()] * len(outs),
        scratch_shapes=[
            pltpu.VMEM((keys, WIDE), BF16),
            pltpu.VMEM((keys, WIDE), BF16),
            pltpu.VMEM((tall, keys), F32),
            pltpu.VMEM((tall, keys), F32),
            pltpu.VMEM((tall, keys), BF16),
            pltpu.VMEM((tall, keys), BF16),
            pltpu.VMEM((tall, LANES), F32),
            pltpu.VMEM((tall, LANES), F32),
            pltpu.VMEM((rows, WIDE), BF16),
        ],
        compiler_params=limit(need // MIB + 16),
        cost_estimate=cost(0, 0),
        name="part",
    )(*operands)


def swap(array, axis, distance):
    return lax.ppermute(array, axis, [(i, i ^ distance) for i in range(lax.axis_size(axis))])


def forward(array, axis, pairs):
    return lax.ppermute(array, axis, [(2 * a + c, 2 * b + c) for a, b in pairs for c in range(2)])


def after(value, *others):
    return lax.optimization_barrier((value, others))[0]


def on_device(features, tiles, tile_src, tile_count, node_bucket, w_qk, w_v, bias_table):
    rows, width = features.shape
    groups = lax.axis_size("group")
    seq_count = lax.axis_size("seq")
    chips = seq_count // 2
    sel = jnp.asarray(pad_matrix(), BF16)
    my_group = lax.axis_index("group").reshape(1)
    my_seq = lax.axis_index("seq").reshape(1)

    received = [swap(features, "group", d) for d in range(groups - 1, 0, -1)][::-1]

    at = jnp.arange(seq_count)[:, None] == my_seq[None, :]
    buckets = jnp.where(at, node_bucket[None, :], 0)
    step = 1
    while step < seq_count:
        buckets = buckets + swap(buckets, "seq", step)
        step *= 2

    cube = bias_table.reshape(H, NB, NB).transpose(1, 0, 2)
    cube = jnp.concatenate([cube, cube, cube, jnp.zeros((NB, H, LANES - 3 * NB), F32)], axis=2)
    cube = cube.reshape(NB, H * LANES)
    bias, own_features, masked, *hot = pl.pallas_call(
        stage_kernel,
        out_shape=[shape(rows, H * LANES), shape(rows, width), shape(rows, TILES * rows)]
        + [shape(2 * rows, LANES)] * chips,
        in_specs=[smem()] * 2 + [vmem()] * 4,
        out_specs=[vmem()] * (3 + chips),
        compiler_params=limit(16),
        cost_estimate=cost(0, 0),
        name="stage",
    )(tile_count, my_seq, cube, buckets, features, tiles)

    own = pl.pallas_call(
        aggregate_kernel,
        out_shape=shape(rows, width),
        in_specs=[smem()] * 2 + [vmem()] * (1 + groups),
        out_specs=vmem(),
        scratch_shapes=[pltpu.VMEM((groups * rows, width), BF16)],
        compiler_params=limit(16),
        cost_estimate=cost(0, 0),
        name="aggregate",
    )(tile_src, my_group, masked, own_features, *received)

    far = [own] + [None] * (chips - 1)
    far[1] = swap(own, "seq", 2)
    if chips == 4:
        middle = [(1, 2), (2, 1)]
        outward = [(1, 0), (2, 3)]
        across = forward(own, "seq", middle)
    else:
        for d in range(2, chips):
            far[d] = swap(own, "seq", 2 * d)
    near = [swap(own, "seq", 1)]

    q = pl.pallas_call(
        query_kernel,
        out_shape=shape(rows, WIDE),
        in_specs=[vmem()] * 3,
        out_specs=vmem(),
        compiler_params=limit(16),
        cost_estimate=cost(0, 0),
        name="query",
    )(own, w_qk, sel)

    state = []
    for d in range(chips):
        if chips == 4:
            chip = my_seq[0] // 2
            inner = (chip == 1) | (chip == 2)
            if d == 1:
                crossed = forward(far[1], "seq", middle)
                passed = forward(across, "seq", outward)
            if d == 2:
                crossed, passed = after((crossed, passed), *state)
                ended = forward(crossed, "seq", outward)
                far[2] = jnp.where(inner, crossed, passed)
            if d == 3:
                far[3] = jnp.where(inner, across, after(ended, *state))
        block = far[d]
        if d:
            block = after(block, *state)
            near.append(swap(block, "seq", 1))
        state = attend_part(
            d == 0, d == chips - 1, q, bias, hot[d], w_qk, w_v, sel, [block, near[d]], state
        )
    return state[0]


def solution(mesh):
    in_specs = (
        P(("group", "seq"), None),
        P(("group", "seq"), None),
        P(("group", "seq"), None),
        P(("group", "seq")),
        P(("group", "seq")),
        P(),
        P(),
        P(),
    )
    out_specs = P(("group", "seq"), None)
    return jax.shard_map(
        on_device, mesh=mesh, in_specs=in_specs, out_specs=out_specs, check_vma=False
    )
```

```python
import math

import jax
import jax.numpy as jnp
from jax import lax
from jax.experimental import pallas as pl
from jax.experimental.pallas import tpu as pltpu
from jax.sharding import PartitionSpec as P

H = 32
HD = 24
NB = 16
TILES = 8
LANES = 128
PAD = 32
QUAD = LANES // PAD
WIDE = H * PAD
HALF = 16 * HD
HALF_PAD = 16 * PAD
EXTRA = 8
NT = (((1,), (1,)), ((), ()))
MIB = 1024 * 1024
BF16 = jnp.bfloat16
F32 = jnp.float32
FACTOR = math.log2(math.e) / math.sqrt(HD)


def vmem():
    return pl.BlockSpec(memory_space=pltpu.VMEM)


def smem():
    return pl.BlockSpec(memory_space=pltpu.SMEM)


def limit(mib):
    return pltpu.CompilerParams(vmem_limit_bytes=mib * MIB)


def shape(*dims, dtype=BF16):
    return jax.ShapeDtypeStruct(dims, dtype)


def one_hot_slab(bucket_row):
    n = bucket_row.shape[1]
    index = lax.broadcasted_iota(jnp.int32, (LANES, n), 0)
    wanted = jnp.where(index < 3 * NB, index % NB, -1).astype(F32)
    hot = jnp.where(wanted == bucket_row, 1.0, 0.0)
    return hot.T.astype(BF16)


def stage_kernel(
    count_ref, me_ref, src_ref, cube_ref, bucket_ref, features_ref, tiles_ref,
    bias_ref, own_ref, masked_ref, sel_ref, extra_ref, from_ref, tiles_held, sems,
):
    rows = own_ref.shape[0]
    copies = [
        pltpu.make_async_copy(tiles_ref, tiles_held, sems.at[0]),
        pltpu.make_async_copy(features_ref, own_ref, sems.at[1]),
    ]
    for copy in copies:
        copy.start()
    for t in range(TILES):
        from_ref[t : t + 1, :] = jnp.full((1, LANES), src_ref[0, t] ^ me_ref[0], jnp.int32)
    width = own_ref.shape[1]
    extra = jnp.concatenate(
        [bucket_ref[...].astype(F32), jnp.zeros((1, width - rows), F32)], axis=1
    )
    extra_ref[...] = jnp.broadcast_to(extra, (EXTRA, width))
    take = lax.broadcasted_iota(jnp.int32, sel_ref.shape, 0)
    column = lax.broadcasted_iota(jnp.int32, sel_ref.shape, 1)
    wanted = jnp.where(column % PAD < HD, column // PAD * HD + column % PAD, -1)
    sel_ref[...] = jnp.where(take == wanted, 1.0, 0.0).astype(BF16)
    scaled = cube_ref[...] * math.sqrt(HD)
    high = scaled.astype(BF16).astype(F32)
    rest = scaled - high
    mid = rest.astype(BF16).astype(F32)
    low = rest - mid
    lane = lax.broadcasted_iota(jnp.int32, scaled.shape, 1) % LANES
    parts = jnp.where(
        lane < NB, high, jnp.where(lane < 2 * NB, mid, jnp.where(lane < 3 * NB, low, 0.0))
    )
    hot = one_hot_slab(bucket_ref[...].astype(F32))[:, :NB]
    bias_ref[...] = jnp.dot(hot, parts.astype(BF16), preferred_element_type=F32).astype(BF16)
    for copy in copies:
        copy.wait()
    for t in range(TILES):
        tile = tiles_held[:, t * rows : (t + 1) * rows]
        masked_ref[:, t * rows : (t + 1) * rows] = jnp.where(
            t < count_ref[0], tile, jnp.zeros_like(tile)
        )


def aggregate_kernel(from_ref, extra_ref, masked_ref, *refs):
    feature_refs, out_ref, held = refs[:-2], refs[-2], refs[-1]
    rows = feature_refs[0].shape[0]
    for d, ref in enumerate(feature_refs):
        held[d * rows : (d + 1) * rows, :] = ref[...]
    picked = []
    for t in range(TILES):
        start = pl.multiple_of(from_ref[t, 0] * rows, rows)
        picked.append(held[pl.ds(start, rows), :])
    total = feature_refs[0][...].astype(F32) + jnp.dot(
        masked_ref[...], jnp.concatenate(picked, axis=0), preferred_element_type=F32
    )
    mean_square = jnp.mean(total * total, axis=-1, keepdims=True)
    out_ref[...] = jnp.concatenate(
        [total * lax.rsqrt(mean_square + 1e-06), extra_ref[...]], axis=0
    ).astype(BF16)


def project(block, w_ref, base, sel, dst):
    width = block.shape[1]
    for part in range(width // HALF):
        raw = jnp.dot(
            block, w_ref[:, base + part * HALF : base + (part + 1) * HALF],
            preferred_element_type=F32,
        ).astype(BF16)
        dst[:, part * HALF_PAD : (part + 1) * HALF_PAD] = jnp.dot(
            raw, sel, preferred_element_type=F32
        ).astype(BF16)


def query_kernel(own_ref, w_qk_ref, sel_ref, q_ref):
    project(own_ref[...][: q_ref.shape[0], :], w_qk_ref, 0, sel_ref[...], q_ref)


def part_kernel(count, first, last, q_ref, bias_ref, w_qk_ref, w_v_ref, sel_ref, *refs):
    block_refs, refs = refs[:count], refs[count:]
    hot_ref, k_ref, v_ref, x0_ref, x1_ref, p0_ref, p1_ref, t0_ref, t1_ref, heads_ref = refs[-10:]
    refs = refs[:-10]
    old_refs = ()
    if not first:
        old_refs, refs = refs[:3], refs[3:]
    rows = q_ref.shape[0]
    keys = hot_ref.shape[0]
    quads = H // QUAD
    arrived = [ref[...] for ref in block_refs]
    for s, item in enumerate(arrived):
        bucket = item[rows:, :rows].astype(F32)[:1, :]
        hot_ref[s * rows : (s + 1) * rows, :] = one_hot_slab(bucket)
    block = jnp.concatenate([item[:rows, :] for item in arrived], axis=0)
    sel = sel_ref[...]
    project(block, w_qk_ref, block.shape[1], sel, k_ref)
    project(block, w_v_ref, 0, sel, v_ref)

    lane_head = lax.broadcasted_iota(jnp.int32, (rows, LANES), 1) // PAD
    ones = jnp.ones((keys, LANES), BF16)

    def scores(m, x_ref):
        cols = pl.ds(pl.multiple_of(m * LANES, LANES), LANES)
        q = q_ref[:, cols]
        zero = jnp.zeros_like(q)
        left = jnp.concatenate([jnp.where(lane_head == h, q, zero) for h in range(QUAD)], axis=0)
        right = jnp.concatenate(
            [
                bias_ref[:, pl.ds(pl.multiple_of((m * QUAD + h) * LANES, LANES), LANES)]
                for h in range(QUAD)
            ],
            axis=0,
        )
        query = jnp.concatenate([left, right], axis=1)
        for n in range(0, keys, 256):
            key = jnp.concatenate([k_ref[n : n + 256, cols], hot_ref[n : n + 256, :]], axis=1)
            x_ref[:, n : n + 256] = lax.dot_general(query, key, NT, preferred_element_type=F32)

    def pick(array):
        out = array[:rows, :]
        for h in range(1, QUAD):
            out = jnp.where(lane_head == h, array[h * rows : (h + 1) * rows, :], out)
        return out

    def mix(m, x_ref, p_ref, t_ref):
        cols = pl.ds(pl.multiple_of(m * LANES, LANES), LANES)
        for r in range(0, QUAD * rows, 16):
            x = x_ref[r : r + 16, :]
            peak = jnp.max(x, axis=-1, keepdims=True)
            p_ref[r : r + 16, :] = jnp.exp2((x - peak) * FACTOR).astype(BF16)
            if not (first and last):
                t_ref[r : r + 16, :] = jnp.broadcast_to(peak, (16, LANES))
        value = jnp.concatenate([v_ref[:, cols], ones], axis=1)
        mixed = jnp.dot(p_ref[...], value, preferred_element_type=F32)
        top = pick(mixed[:, :LANES])
        total = pick(mixed[:, LANES:])
        if not (first and last):
            peak = pick(t_ref[...])
        if not first:
            old_top, old_total, old_peak = (ref[:, cols] for ref in old_refs)
            best = jnp.maximum(old_peak, peak)
            new_share = jnp.exp2((peak - best) * FACTOR)
            old_share = jnp.exp2((old_peak - best) * FACTOR)
            top = top * new_share + old_top * old_share
            total = total * new_share + old_total * old_share
            peak = best
        if last:
            heads_ref[:, cols] = (top / total).astype(BF16)
        else:
            refs[0][:, cols] = top
            refs[1][:, cols] = total
            refs[2][:, cols] = peak

    scores(0, x0_ref)

    def two(i, carry):
        m = i * 2
        scores(m + 1, x1_ref)
        mix(m, x0_ref, p0_ref, t0_ref)
        scores(jnp.minimum(m + 2, quads - 1), x0_ref)
        mix(m + 1, x1_ref, p1_ref, t1_ref)
        return carry

    lax.fori_loop(0, quads // 2, two, 0)

    if last:
        out_ref = refs[0]
        for part in range(out_ref.shape[1] // HALF):
            out_ref[:, part * HALF : (part + 1) * HALF] = lax.dot_general(
                heads_ref[:, part * HALF_PAD : (part + 1) * HALF_PAD], sel, NT,
                preferred_element_type=F32,
            ).astype(BF16)


def attend_part(first, last, q, bias, w_qk, w_v, sel, blocks, state):
    rows = q.shape[0]
    keys = rows * len(blocks)
    if last:
        outs = [shape(rows, blocks[0].shape[1])]
    else:
        outs = [shape(rows, WIDE, dtype=F32)] * 3
    operands = [q, bias, w_qk, w_v, sel, *blocks, *state]
    tall = QUAD * rows
    need = 2 * tall * keys * 6 + 4 * keys * WIDE + 2 * tall * LANES * 4
    return pl.pallas_call(
        lambda *refs: part_kernel(len(blocks), first, last, *refs),
        out_shape=outs,
        in_specs=[vmem()] * len(operands),
        out_specs=[vmem()] * len(outs),
        scratch_shapes=[
            pltpu.VMEM((keys, LANES), BF16),
            pltpu.VMEM((keys, WIDE), BF16),
            pltpu.VMEM((keys, WIDE), BF16),
            pltpu.VMEM((tall, keys), F32),
            pltpu.VMEM((tall, keys), F32),
            pltpu.VMEM((tall, keys), BF16),
            pltpu.VMEM((tall, keys), BF16),
            pltpu.VMEM((tall, LANES), F32),
            pltpu.VMEM((tall, LANES), F32),
            pltpu.VMEM((rows, WIDE), BF16),
        ],
        compiler_params=limit(need // MIB + 16),
        cost_estimate=pl.CostEstimate(flops=1000, bytes_accessed=1000, transcendentals=0),
        name="part",
    )(*operands)


def swap(array, axis, distance):
    return lax.ppermute(array, axis, [(i, i ^ distance) for i in range(lax.axis_size(axis))])


def after(value, *others):
    return lax.optimization_barrier((value, others))[0]


def on_device(features, tiles, tile_src, tile_count, node_bucket, w_qk, w_v, bias_table):
    rows, width = features.shape
    groups = lax.axis_size("group")
    seq_count = lax.axis_size("seq")
    chips = seq_count // 2
    any_space = pl.BlockSpec(memory_space=pl.ANY)

    received = [swap(features, "group", d) for d in range(groups - 1, 0, -1)][::-1]
    own_bucket = node_bucket.reshape(1, rows)

    cube = bias_table.reshape(H, NB, NB).transpose(1, 0, 2)
    cube = jnp.concatenate([cube, cube, cube, jnp.zeros((NB, H, LANES - 3 * NB), F32)], axis=2)
    cube = cube.reshape(NB, H * LANES)
    bias, own_features, masked, sel, extra, source = pl.pallas_call(
        stage_kernel,
        out_shape=[
            shape(rows, H * LANES), shape(rows, width), shape(rows, TILES * rows),
            shape(HALF, HALF_PAD), shape(EXTRA, width, dtype=F32),
            shape(TILES, LANES, dtype=jnp.int32),
        ],
        in_specs=[smem()] * 3 + [vmem(), vmem(), any_space, any_space],
        out_specs=[vmem()] * 6,
        scratch_shapes=[pltpu.VMEM((rows, TILES * rows), BF16), pltpu.SemaphoreType.DMA((2,))],
        compiler_params=limit(16),
        cost_estimate=pl.CostEstimate(flops=1000, bytes_accessed=1000, transcendentals=0),
        name="stage",
    )(tile_count, lax.axis_index("group").reshape(1), tile_src, cube, own_bucket, features, tiles)

    own = pl.pallas_call(
        aggregate_kernel,
        out_shape=shape(rows + EXTRA, width),
        in_specs=[vmem()] * (3 + groups),
        out_specs=vmem(),
        scratch_shapes=[pltpu.VMEM((groups * rows, width), BF16)],
        compiler_params=limit(16),
        cost_estimate=pl.CostEstimate(flops=1000, bytes_accessed=1000, transcendentals=0),
        name="aggregate",
    )(source, extra, masked, own_features, *received)

    far = [own] + [None] * (chips - 1)
    top = 1
    while 2 * top < chips:
        top *= 2
    far[top] = swap(own, "seq", 2 * top)
    step = 1
    while step < top:
        far[step] = swap(own, "seq", 2 * step)
        step *= 2
    for d in range(3, chips):
        if far[d] is None:
            far[d] = swap(far[d & (d - 1)], "seq", 2 * (d & -d))
    q = pl.pallas_call(
        query_kernel,
        out_shape=shape(rows, WIDE),
        in_specs=[vmem()] * 3,
        out_specs=vmem(),
        compiler_params=limit(16),
        cost_estimate=pl.CostEstimate(flops=1000, bytes_accessed=1000, transcendentals=0),
        name="query",
    )(own, w_qk, sel)

    parts = [[0], [1, top]] if top > 1 else [[0, 1]]
    parts += [[d] for d in range(2, chips) if d != top]
    state = []
    for number, part in enumerate(parts):
        blocks = []
        for d in part:
            block = far[d]
            if d:
                block = after(block, *state)
                near = swap(block, "seq", 1)
            else:
                near = swap(own, "seq", 1)
            blocks += [block, near]
        state = attend_part(
            number == 0, number == len(parts) - 1, q, bias, w_qk, w_v, sel, blocks, state
        )
    return state[0]


def solution(mesh):
    in_specs = (
        P(("group", "seq"), None),
        P(("group", "seq"), None),
        P(("group", "seq"), None),
        P(("group", "seq")),
        P(("group", "seq")),
        P(),
        P(),
        P(),
    )
    out_specs = P(("group", "seq"), None)
    return jax.shard_map(
        on_device, mesh=mesh, in_specs=in_specs, out_specs=out_specs, check_vma=False
    )
```

```python
import math

import jax
import jax.numpy as jnp
from jax import lax
from jax.experimental import pallas as pl
from jax.experimental.pallas import tpu as pltpu
from jax.sharding import PartitionSpec as P

H = 32
HD = 24
NB = 16
TILES = 8
LANES = 128
SET = 16
HALF = SET * HD
SLABS = HALF // LANES
SAFE = 1e30
EXTRA = 8
SHIFT = 3 * NB
NT = (((1,), (1,)), ((), ()))
MIB = 1024 * 1024
BF16 = jnp.bfloat16
F32 = jnp.float32
FACTOR = math.log2(math.e) / math.sqrt(HD)


def vmem():
    return pl.BlockSpec(memory_space=pltpu.VMEM)


def smem():
    return pl.BlockSpec(memory_space=pltpu.SMEM)


def limit(mib):
    return pltpu.CompilerParams(vmem_limit_bytes=mib * MIB)


def shape(*dims, dtype=BF16):
    return jax.ShapeDtypeStruct(dims, dtype)


def one_hot_slab(bucket_row):
    n = bucket_row.shape[1]
    index = lax.broadcasted_iota(jnp.int32, (LANES, n), 0)
    wanted = jnp.where(index < 3 * NB, index % NB, -1).astype(F32)
    hot = jnp.where((wanted == bucket_row) | ((index >= SHIFT) & (index < SHIFT + 3)), 1.0, 0.0)
    return hot.T.astype(BF16)


def stage_kernel(
    count_ref, me_ref, src_ref, cube_ref, bucket_ref, features_ref, tiles_ref,
    bias_ref, own_ref, masked_ref, extra_ref, from_ref, tiles_held, sems,
):
    rows = own_ref.shape[0]
    copies = [
        pltpu.make_async_copy(tiles_ref, tiles_held, sems.at[0]),
        pltpu.make_async_copy(features_ref, own_ref, sems.at[1]),
    ]
    for copy in copies:
        copy.start()
    for t in range(TILES):
        from_ref[t : t + 1, :] = jnp.full((1, LANES), src_ref[0, t] ^ me_ref[0], jnp.int32)
    width = own_ref.shape[1]
    extra = jnp.concatenate(
        [bucket_ref[...].astype(F32), jnp.zeros((1, width - rows), F32)], axis=1
    )
    extra_ref[...] = jnp.broadcast_to(extra, (EXTRA, width))
    scaled = cube_ref[...] * math.sqrt(HD)
    high = scaled.astype(BF16).astype(F32)
    rest = scaled - high
    mid = rest.astype(BF16).astype(F32)
    low = rest - mid
    lane = lax.broadcasted_iota(jnp.int32, scaled.shape, 1) % LANES
    parts = jnp.where(
        lane < NB, high, jnp.where(lane < 2 * NB, mid, jnp.where(lane < 3 * NB, low, 0.0))
    )
    hot = one_hot_slab(bucket_ref[...].astype(F32))[:, :NB]
    bias_ref[...] = jnp.dot(hot, parts.astype(BF16), preferred_element_type=F32).astype(BF16)
    for copy in copies:
        copy.wait()
    for t in range(TILES):
        tile = tiles_held[:, t * rows : (t + 1) * rows]
        masked_ref[:, t * rows : (t + 1) * rows] = jnp.where(
            t < count_ref[0], tile, jnp.zeros_like(tile)
        )


def aggregate_kernel(from_ref, extra_ref, masked_ref, *refs):
    feature_refs, out_ref, held = refs[:-2], refs[-2], refs[-1]
    rows = feature_refs[0].shape[0]
    for d, ref in enumerate(feature_refs):
        held[d * rows : (d + 1) * rows, :] = ref[...]
    picked = []
    for t in range(TILES):
        start = pl.multiple_of(from_ref[t, 0] * rows, rows)
        picked.append(held[pl.ds(start, rows), :])
    total = feature_refs[0][...].astype(F32) + jnp.dot(
        masked_ref[...], jnp.concatenate(picked, axis=0), preferred_element_type=F32
    )
    mean_square = jnp.mean(total * total, axis=-1, keepdims=True)
    out_ref[...] = jnp.concatenate(
        [total * lax.rsqrt(mean_square + 1e-06), extra_ref[...]], axis=0
    ).astype(BF16)


def slab_heads(slab):
    return slab * LANES // HD, ((slab + 1) * LANES - 1) // HD


def part_kernel(count, first, last, w_qk_ref, w_v_ref, *refs):
    block_refs, refs = refs[:count], refs[count:]
    hot_ref, k_ref, v_ref, p_ref, *refs_back = refs[-5:]
    top_ref = refs_back[0]
    refs = refs[:-5]
    if first:
        bias_ref, q_ref, shifted_ref, *outs = refs
    else:
        q_ref, bias_ref, *refs = refs
        old_refs, outs = (refs[:2], refs[2:]) if len(refs) in (3, 5) else (refs[:3], refs[3:])
    rows = q_ref.shape[0]
    keys = hot_ref.shape[0]
    width = w_v_ref.shape[0]
    arrived = [ref[...] for ref in block_refs]
    for s, item in enumerate(arrived):
        bucket = item[rows:, :rows].astype(F32)[:1, :]
        hot_ref[s * rows : (s + 1) * rows, :] = one_hot_slab(bucket)
    block = jnp.concatenate([item[:rows, :] for item in arrived], axis=0)
    if first:
        for n in range(0, width, 256):
            q_ref[:, n : n + 256] = jnp.dot(
                block[:rows, :], w_qk_ref[:, n : n + 256], preferred_element_type=F32
            ).astype(BF16)
    for n in range(0, width, 256):
        k_ref[:, n : n + 256] = jnp.dot(
            block, w_qk_ref[:, width + n : width + n + 256], preferred_element_type=F32
        ).astype(BF16)
        v_ref[:, n : n + 256] = jnp.dot(
            block, w_v_ref[:, n : n + 256], preferred_element_type=F32
        ).astype(BF16)

    lane = lax.broadcasted_iota(jnp.int32, (rows, LANES), 1)
    ones = jnp.ones((keys, LANES), BF16)

    def scores(half, slab):
        cols = pl.ds(pl.multiple_of(half * HALF + slab * LANES, LANES), LANES)
        begin, end = slab_heads(slab)
        q = q_ref[:, cols]
        zero = jnp.zeros_like(q)
        lefts, rights = [], []
        for h in range(begin, end + 1):
            inside = (lane >= h * HD - slab * LANES) & (lane < (h + 1) * HD - slab * LANES)
            lefts.append(jnp.where(inside, q, zero))
            if h * HD >= slab * LANES:
                at = pl.multiple_of((half * SET + h) * LANES, LANES)
                rights.append(bias_ref[:, pl.ds(at, LANES)])
            else:
                rights.append(zero)
        query = jnp.concatenate(
            [jnp.concatenate(lefts, axis=0), jnp.concatenate(rights, axis=0)], axis=1
        )
        key = jnp.concatenate([k_ref[:, cols], hot_ref[...]], axis=1)
        return lax.dot_general(query, key, NT, preferred_element_type=F32)

    def weigh(half, local):
        carried = None
        for slab in range(SLABS):
            begin, end = slab_heads(slab)
            x = scores(half, slab)
            for h in range(begin, end + 1):
                own = x[(h - begin) * rows : (h - begin + 1) * rows, :]
                if h * HD < slab * LANES:
                    own = own + carried
                if (h + 1) * HD > (slab + 1) * LANES:
                    carried = own
                    continue
                if local:
                    peak = jnp.max(own, axis=-1, keepdims=True)
                    own = own - peak
                    keep_peak(half, h, peak)
                p_ref[h * rows : (h + 1) * rows, :] = jnp.exp2(own * FACTOR).astype(BF16)

    def keep_peak(half, h, peak):
        if first:
            at = pl.ds(pl.multiple_of((half * SET + h) * LANES, LANES), LANES)
            high = (-peak).astype(BF16).astype(F32)
            rest = -peak - high
            mid = rest.astype(BF16).astype(F32)
            low = rest - mid
            mark = jnp.where(
                lane == SHIFT, high, jnp.where(lane == SHIFT + 1, mid, jnp.where(lane == SHIFT + 2, low, 0.0))
            )
            shifted_ref[:, at] = bias_ref[:, at] + mark.astype(BF16)
        else:
            top_ref[h * rows : (h + 1) * rows, :] = jnp.broadcast_to(peak, (rows, LANES))

    def pick(array, slab, base):
        begin, end = slab_heads(slab)
        out = array[(begin - base) * rows : (begin - base + 1) * rows, :]
        for h in range(begin + 1, end + 1):
            piece = array[(h - base) * rows : (h - base + 1) * rows, :]
            out = jnp.where(lane >= h * HD - slab * LANES, piece, out)
        return out

    def mix(half, slab):
        cols = pl.ds(pl.multiple_of(half * HALF + slab * LANES, LANES), LANES)
        begin, end = slab_heads(slab)
        value = jnp.concatenate([v_ref[:, cols], ones], axis=1)
        mixed = jnp.dot(
            p_ref[begin * rows : (end + 1) * rows, :], value, preferred_element_type=F32
        )
        return cols, pick(mixed[:, :LANES], slab, begin), pick(mixed[:, LANES:], slab, begin)

    def fast(half, largest):
        weigh(half, first)
        for slab in range(SLABS):
            cols, top, total = mix(half, slab)
            if not first:
                top = top + old_refs[0][:, cols]
                total = total + old_refs[1][:, cols]
            largest = jnp.maximum(largest, total)
            if last:
                outs[0][:, cols] = (top / total).astype(BF16)
            else:
                outs[0][:, cols] = top
                outs[1][:, cols] = total
                if not first:
                    outs[2][:, cols] = jnp.zeros_like(top)
        return largest

    largest = lax.fori_loop(0, width // HALF, fast, jnp.zeros((rows, LANES), F32))
    if first:
        return
    fine = jnp.max(largest) < SAFE
    if len(old_refs) == 3:
        fine = fine & (jnp.max(old_refs[2][...]) == 0.0)

    @pl.when(jnp.logical_not(fine))
    def _():
        def careful(half, carry):
            weigh(half, True)
            for slab in range(SLABS):
                cols, top, total = mix(half, slab)
                peak = pick(top_ref[...], slab, 0)
                old = old_refs[2][:, cols] if len(old_refs) == 3 else jnp.zeros_like(top)
                best = jnp.maximum(old, peak)
                share = jnp.exp2((peak - best) * FACTOR)
                old_share = jnp.exp2((old - best) * FACTOR)
                top = top * share + old_refs[0][:, cols] * old_share
                total = total * share + old_refs[1][:, cols] * old_share
                if last:
                    outs[0][:, cols] = (top / total).astype(BF16)
                else:
                    outs[0][:, cols] = top
                    outs[1][:, cols] = total
                    outs[2][:, cols] = best
            return carry

        lax.fori_loop(0, width // HALF, careful, 0)


def attend_part(first, last, w_qk, w_v, blocks, inputs):
    width = w_v.shape[0]
    rows = blocks[0].shape[0] - EXTRA
    keys = rows * len(blocks)
    state = shape(rows, width, dtype=F32)
    if first:
        outs = [shape(rows, width), shape(rows, H * LANES), state, state]
    elif last:
        outs = [shape(rows, width)]
    else:
        outs = [state] * 3
    operands = [w_qk, w_v, *blocks, *inputs]
    tall = SET * rows
    need = 8 * tall * keys * 2 + 4 * keys * width + 4 * tall * LANES
    return pl.pallas_call(
        lambda *refs: part_kernel(len(blocks), first, last, *refs),
        out_shape=outs,
        in_specs=[vmem()] * len(operands),
        out_specs=[vmem()] * len(outs),
        scratch_shapes=[
            pltpu.VMEM((keys, LANES), BF16),
            pltpu.VMEM((keys, width), BF16),
            pltpu.VMEM((keys, width), BF16),
            pltpu.VMEM((tall, keys), BF16),
            pltpu.VMEM((tall, LANES), F32),
        ],
        compiler_params=limit(need // MIB + 12),
        cost_estimate=pl.CostEstimate(flops=1000, bytes_accessed=1000, transcendentals=0),
        name="part",
    )(*operands)


def swap(array, axis, distance):
    return lax.ppermute(array, axis, [(i, i ^ distance) for i in range(lax.axis_size(axis))])


def after(value, *others):
    return lax.optimization_barrier((value, others))[0]


def on_device(features, tiles, tile_src, tile_count, node_bucket, w_qk, w_v, bias_table):
    rows, width = features.shape
    groups = lax.axis_size("group")
    seq_count = lax.axis_size("seq")
    chips = seq_count // 2
    any_space = pl.BlockSpec(memory_space=pl.ANY)

    received = [swap(features, "group", d) for d in range(groups - 1, 0, -1)][::-1]
    own_bucket = node_bucket.reshape(1, rows)

    cube = bias_table.reshape(H, NB, NB).transpose(1, 0, 2)
    cube = jnp.concatenate([cube, cube, cube, jnp.zeros((NB, H, LANES - 3 * NB), F32)], axis=2)
    cube = cube.reshape(NB, H * LANES)
    bias, own_features, masked, extra, source = pl.pallas_call(
        stage_kernel,
        out_shape=[
            shape(rows, H * LANES), shape(rows, width), shape(rows, TILES * rows),
            shape(EXTRA, width, dtype=F32),
            shape(TILES, LANES, dtype=jnp.int32),
        ],
        in_specs=[smem()] * 3 + [vmem(), vmem(), any_space, any_space],
        out_specs=[vmem()] * 5,
        scratch_shapes=[pltpu.VMEM((rows, TILES * rows), BF16), pltpu.SemaphoreType.DMA((2,))],
        compiler_params=limit(16),
        cost_estimate=pl.CostEstimate(flops=1000, bytes_accessed=1000, transcendentals=0),
        name="stage",
    )(tile_count, lax.axis_index("group").reshape(1), tile_src, cube, own_bucket, features, tiles)

    own = pl.pallas_call(
        aggregate_kernel,
        out_shape=shape(rows + EXTRA, width),
        in_specs=[vmem()] * (3 + groups),
        out_specs=vmem(),
        scratch_shapes=[pltpu.VMEM((groups * rows, width), BF16)],
        compiler_params=limit(16),
        cost_estimate=pl.CostEstimate(flops=1000, bytes_accessed=1000, transcendentals=0),
        name="aggregate",
    )(source, extra, masked, own_features, *received)

    far = [own] + [None] * (chips - 1)
    top = 1
    while 2 * top < chips:
        top *= 2
    far[top] = swap(own, "seq", 2 * top)
    step = 1
    while step < top:
        far[step] = swap(own, "seq", 2 * step)
        step *= 2
    for d in range(3, chips):
        if far[d] is None:
            far[d] = swap(far[d & (d - 1)], "seq", 2 * (d & -d))
    parts = [[0], [1, top]] if top > 1 else [[0, 1]]
    parts += [[d] for d in range(2, chips) if d != top]
    queries, state = [], [bias]
    for number, part in enumerate(parts):
        blocks = []
        for d in part:
            block = far[d]
            if d:
                block = after(block, *state)
                near = swap(block, "seq", 1)
            else:
                near = swap(own, "seq", 1)
            blocks += [block, near]
        state = attend_part(
            number == 0, number == len(parts) - 1, w_qk, w_v, blocks, [*queries, *state]
        )
        if number == 0:
            queries, state = state[:2], state[2:]
    return state[0]


def solution(mesh):
    in_specs = (
        P(("group", "seq"), None),
        P(("group", "seq"), None),
        P(("group", "seq"), None),
        P(("group", "seq")),
        P(("group", "seq")),
        P(),
        P(),
        P(),
    )
    out_specs = P(("group", "seq"), None)
    return jax.shard_map(
        on_device, mesh=mesh, in_specs=in_specs, out_specs=out_specs, check_vma=False
    )
```

```python
import math

import jax
import jax.numpy as jnp
from jax import lax
from jax.experimental import pallas as pl
from jax.experimental.pallas import tpu as pltpu
from jax.sharding import PartitionSpec as P

H = 32
HD = 24
NB = 16
TILES = 8
LANES = 128
SET = 16
HALF = SET * HD
SLABS = HALF // LANES
SAFE = 1e30
EXTRA = 8
SHIFT = 3 * NB
NT = (((1,), (1,)), ((), ()))
MIB = 1024 * 1024
BF16 = jnp.bfloat16
F32 = jnp.float32
FACTOR = math.log2(math.e) / math.sqrt(HD)


def vmem():
    return pl.BlockSpec(memory_space=pltpu.VMEM)


def smem():
    return pl.BlockSpec(memory_space=pltpu.SMEM)


def limit(mib):
    return pltpu.CompilerParams(vmem_limit_bytes=mib * MIB)


def shape(*dims, dtype=BF16):
    return jax.ShapeDtypeStruct(dims, dtype)


def one_hot_slab(bucket_row):
    n = bucket_row.shape[1]
    index = lax.broadcasted_iota(jnp.int32, (LANES, n), 0)
    wanted = jnp.where(index < 3 * NB, index % NB, -1).astype(F32)
    hot = jnp.where((wanted == bucket_row) | ((index >= SHIFT) & (index < SHIFT + 3)), 1.0, 0.0)
    return hot.T.astype(BF16)


def split_three(x):
    high = x.astype(BF16).astype(F32)
    mid = (x - high).astype(BF16).astype(F32)
    return high, mid, x - high - mid


def stage_kernel(
    count_ref, me_ref, src_ref, table_ref, bucket_ref, features_ref, tiles_ref,
    bias_ref, own_ref, masked_ref, extra_ref, from_ref, tiles_held, sems,
):
    rows = own_ref.shape[0]
    copies = [
        pltpu.make_async_copy(tiles_ref, tiles_held, sems.at[0]),
        pltpu.make_async_copy(features_ref, own_ref, sems.at[1]),
    ]
    for copy in copies:
        copy.start()
    for t in range(TILES):
        from_ref[t : t + 1, :] = jnp.full((1, LANES), src_ref[0, t] ^ me_ref[0], jnp.int32)
    width = own_ref.shape[1]
    extra = jnp.concatenate(
        [bucket_ref[...].astype(F32), jnp.zeros((1, width - rows), F32)], axis=1
    )
    extra_ref[...] = jnp.broadcast_to(extra, (EXTRA, width))
    table = table_ref[...] * math.sqrt(HD)
    at = lax.broadcasted_iota(jnp.int32, (NB, NB * NB), 1) // NB
    mine = at == lax.broadcasted_iota(jnp.int32, (NB, NB * NB), 0)
    key = lax.broadcasted_iota(jnp.int32, (NB * NB, LANES), 0) % NB
    column = lax.broadcasted_iota(jnp.int32, (NB * NB, LANES), 1)
    cube = jnp.zeros((H * NB, LANES), F32)
    for number, piece in enumerate(split_three(table)):
        spread = [jnp.where(mine, piece[h : h + 1, :], 0.0) for h in range(H)]
        place = jnp.where(column == key + number * NB, 1.0, 0.0).astype(BF16)
        cube = cube + jnp.dot(
            jnp.concatenate(spread, axis=0).astype(BF16), place, preferred_element_type=F32
        )
    cube = cube.astype(BF16)
    hot = one_hot_slab(bucket_ref[...].astype(F32))[:, :NB]
    for h in range(H):
        bias_ref[:, h * LANES : (h + 1) * LANES] = jnp.dot(
            hot, cube[h * NB : (h + 1) * NB, :], preferred_element_type=F32
        ).astype(BF16)
    for copy in copies:
        copy.wait()
    for t in range(TILES):
        tile = tiles_held[:, t * rows : (t + 1) * rows]
        masked_ref[:, t * rows : (t + 1) * rows] = jnp.where(
            t < count_ref[0], tile, jnp.zeros_like(tile)
        )


def aggregate_kernel(from_ref, extra_ref, masked_ref, *refs):
    feature_refs, out_ref, held = refs[:-2], refs[-2], refs[-1]
    rows = feature_refs[0].shape[0]
    for d, ref in enumerate(feature_refs):
        held[d * rows : (d + 1) * rows, :] = ref[...]
    picked = []
    for t in range(TILES):
        start = pl.multiple_of(from_ref[t, 0] * rows, rows)
        picked.append(held[pl.ds(start, rows), :])
    total = feature_refs[0][...].astype(F32) + jnp.dot(
        masked_ref[...], jnp.concatenate(picked, axis=0), preferred_element_type=F32
    )
    mean_square = jnp.mean(total * total, axis=-1, keepdims=True)
    out_ref[...] = jnp.concatenate(
        [total * lax.rsqrt(mean_square + 1e-06), extra_ref[...]], axis=0
    ).astype(BF16)


def slab_heads(slab):
    return slab * LANES // HD, ((slab + 1) * LANES - 1) // HD


def part_kernel(count, first, last, w_qk_ref, w_v_ref, *refs):
    block_refs, refs = refs[:count], refs[count:]
    hot_ref, k_ref, v_ref, p_ref, *refs_back = refs[-5:]
    top_ref = refs_back[0]
    refs = refs[:-5]
    if first:
        bias_ref, q_ref, shifted_ref, *outs = refs
    else:
        q_ref, bias_ref, *refs = refs
        old_refs, outs = (refs[:2], refs[2:]) if len(refs) in (3, 5) else (refs[:3], refs[3:])
    rows = q_ref.shape[0]
    keys = hot_ref.shape[0]
    width = w_v_ref.shape[0]
    arrived = [ref[...] for ref in block_refs]
    for s, item in enumerate(arrived):
        bucket = item[rows:, :rows].astype(F32)[:1, :]
        hot_ref[s * rows : (s + 1) * rows, :] = one_hot_slab(bucket)
    block = jnp.concatenate([item[:rows, :] for item in arrived], axis=0)
    if first:
        for n in range(0, width, 256):
            q_ref[:, n : n + 256] = jnp.dot(
                block[:rows, :], w_qk_ref[:, n : n + 256], preferred_element_type=F32
            ).astype(BF16)
    for n in range(0, width, 256):
        k_ref[:, n : n + 256] = jnp.dot(
            block, w_qk_ref[:, width + n : width + n + 256], preferred_element_type=F32
        ).astype(BF16)
        v_ref[:, n : n + 256] = jnp.dot(
            block, w_v_ref[:, n : n + 256], preferred_element_type=F32
        ).astype(BF16)

    lane = lax.broadcasted_iota(jnp.int32, (rows, LANES), 1)
    ones = jnp.ones((keys, LANES), BF16)

    def scores(half, slab):
        cols = pl.ds(pl.multiple_of(half * HALF + slab * LANES, LANES), LANES)
        begin, end = slab_heads(slab)
        q = q_ref[:, cols]
        zero = jnp.zeros_like(q)
        lefts, rights = [], []
        for h in range(begin, end + 1):
            inside = (lane >= h * HD - slab * LANES) & (lane < (h + 1) * HD - slab * LANES)
            lefts.append(jnp.where(inside, q, zero))
            if h * HD >= slab * LANES:
                at = pl.multiple_of((half * SET + h) * LANES, LANES)
                rights.append(bias_ref[:, pl.ds(at, LANES)])
            else:
                rights.append(zero)
        query = jnp.concatenate(
            [jnp.concatenate(lefts, axis=0), jnp.concatenate(rights, axis=0)], axis=1
        )
        key = jnp.concatenate([k_ref[:, cols], hot_ref[...]], axis=1)
        return lax.dot_general(query, key, NT, preferred_element_type=F32)

    def weigh(half, local):
        carried = None
        for slab in range(SLABS):
            begin, end = slab_heads(slab)
            x = scores(half, slab)
            for h in range(begin, end + 1):
                own = x[(h - begin) * rows : (h - begin + 1) * rows, :]
                if h * HD < slab * LANES:
                    own = own + carried
                if (h + 1) * HD > (slab + 1) * LANES:
                    carried = own
                    continue
                if local:
                    peak = jnp.max(own, axis=-1, keepdims=True)
                    own = own - peak
                    keep_peak(half, h, peak)
                p_ref[h * rows : (h + 1) * rows, :] = jnp.exp2(own * FACTOR).astype(BF16)

    def keep_peak(half, h, peak):
        if first:
            at = pl.ds(pl.multiple_of((half * SET + h) * LANES, LANES), LANES)
            mark = jnp.zeros((rows, LANES), F32)
            for number, piece in enumerate(split_three(-peak)):
                mark = jnp.where(lane == SHIFT + number, piece, mark)
            shifted_ref[:, at] = bias_ref[:, at] + mark.astype(BF16)
        else:
            top_ref[h * rows : (h + 1) * rows, :] = jnp.broadcast_to(peak, (rows, LANES))

    def pick(array, slab, base):
        begin, end = slab_heads(slab)
        out = array[(begin - base) * rows : (begin - base + 1) * rows, :]
        for h in range(begin + 1, end + 1):
            piece = array[(h - base) * rows : (h - base + 1) * rows, :]
            out = jnp.where(lane >= h * HD - slab * LANES, piece, out)
        return out

    def mix(half, slab):
        cols = pl.ds(pl.multiple_of(half * HALF + slab * LANES, LANES), LANES)
        begin, end = slab_heads(slab)
        value = jnp.concatenate([v_ref[:, cols], ones], axis=1)
        mixed = jnp.dot(
            p_ref[begin * rows : (end + 1) * rows, :], value, preferred_element_type=F32
        )
        return cols, pick(mixed[:, :LANES], slab, begin), pick(mixed[:, LANES:], slab, begin)

    def fast(half, largest):
        weigh(half, first)
        for slab in range(SLABS):
            cols, top, total = mix(half, slab)
            if not first:
                top = top + old_refs[0][:, cols]
                total = total + old_refs[1][:, cols]
            largest = jnp.maximum(largest, total)
            if last:
                outs[0][:, cols] = (top / total).astype(BF16)
            else:
                outs[0][:, cols] = top
                outs[1][:, cols] = total
                if not first:
                    outs[2][:, cols] = jnp.zeros_like(top)
        return largest

    largest = lax.fori_loop(0, width // HALF, fast, jnp.zeros((rows, LANES), F32))
    if first:
        return
    fine = jnp.max(largest) < SAFE
    if len(old_refs) == 3:
        fine = fine & (jnp.max(old_refs[2][...]) == 0.0)

    @pl.when(jnp.logical_not(fine))
    def _():
        def careful(half, carry):
            weigh(half, True)
            for slab in range(SLABS):
                cols, top, total = mix(half, slab)
                peak = pick(top_ref[...], slab, 0)
                old = old_refs[2][:, cols] if len(old_refs) == 3 else jnp.zeros_like(top)
                best = jnp.maximum(old, peak)
                share = jnp.exp2((peak - best) * FACTOR)
                old_share = jnp.exp2((old - best) * FACTOR)
                top = top * share + old_refs[0][:, cols] * old_share
                total = total * share + old_refs[1][:, cols] * old_share
                if last:
                    outs[0][:, cols] = (top / total).astype(BF16)
                else:
                    outs[0][:, cols] = top
                    outs[1][:, cols] = total
                    outs[2][:, cols] = best
            return carry

        lax.fori_loop(0, width // HALF, careful, 0)


def attend_part(first, last, w_qk, w_v, blocks, inputs):
    width = w_v.shape[0]
    rows = blocks[0].shape[0] - EXTRA
    keys = rows * len(blocks)
    state = shape(rows, width, dtype=F32)
    if first:
        outs = [shape(rows, width), shape(rows, H * LANES), state, state]
    elif last:
        outs = [shape(rows, width)]
    else:
        outs = [state] * 3
    operands = [w_qk, w_v, *blocks, *inputs]
    tall = SET * rows
    need = 2 * tall * keys + 4 * keys * width + 4 * tall * LANES
    return pl.pallas_call(
        lambda *refs: part_kernel(len(blocks), first, last, *refs),
        out_shape=outs,
        in_specs=[vmem()] * len(operands),
        out_specs=[vmem()] * len(outs),
        scratch_shapes=[
            pltpu.VMEM((keys, LANES), BF16),
            pltpu.VMEM((keys, width), BF16),
            pltpu.VMEM((keys, width), BF16),
            pltpu.VMEM((tall, keys), BF16),
            pltpu.VMEM((tall, LANES), F32),
        ],
        compiler_params=limit(need // MIB + 8),
        cost_estimate=pl.CostEstimate(flops=10**9, bytes_accessed=4_000_000, transcendentals=0),
        name="part",
    )(*operands)


def swap(array, axis, distance):
    return lax.ppermute(array, axis, [(i, i ^ distance) for i in range(lax.axis_size(axis))])


def after(value, *others):
    return lax.optimization_barrier((value, others))[0]


def on_device(features, tiles, tile_src, tile_count, node_bucket, w_qk, w_v, bias_table):
    rows, width = features.shape
    groups = lax.axis_size("group")
    seq_count = lax.axis_size("seq")
    chips = seq_count // 2
    any_space = pl.BlockSpec(memory_space=pl.ANY)

    received = [swap(features, "group", d) for d in range(groups - 1, 0, -1)][::-1]
    own_bucket = node_bucket.reshape(1, rows)

    bias, own_features, masked, extra, source = pl.pallas_call(
        stage_kernel,
        out_shape=[
            shape(rows, H * LANES), shape(rows, width), shape(rows, TILES * rows),
            shape(EXTRA, width, dtype=F32),
            shape(TILES, LANES, dtype=jnp.int32),
        ],
        in_specs=[smem()] * 3 + [vmem(), vmem(), any_space, any_space],
        out_specs=[vmem()] * 5,
        scratch_shapes=[pltpu.VMEM((rows, TILES * rows), BF16), pltpu.SemaphoreType.DMA((2,))],
        compiler_params=limit(8),
        cost_estimate=pl.CostEstimate(flops=10**9, bytes_accessed=4_000_000, transcendentals=0),
        name="stage",
    )(tile_count, lax.axis_index("group").reshape(1), tile_src, bias_table, own_bucket, features, tiles)

    own = pl.pallas_call(
        aggregate_kernel,
        out_shape=shape(rows + EXTRA, width),
        in_specs=[vmem()] * (3 + groups),
        out_specs=vmem(),
        scratch_shapes=[pltpu.VMEM((groups * rows, width), BF16)],
        compiler_params=limit(8),
        cost_estimate=pl.CostEstimate(flops=10**9, bytes_accessed=4_000_000, transcendentals=0),
        name="aggregate",
    )(source, extra, masked, own_features, *received)

    far = [own] + [None] * (chips - 1)
    top = 1
    while 2 * top < chips:
        top *= 2
    far[top] = swap(own, "seq", 2 * top)
    step = 1
    while step < top:
        far[step] = swap(own, "seq", 2 * step)
        step *= 2
    for d in range(3, chips):
        if far[d] is None:
            far[d] = swap(far[d & (d - 1)], "seq", 2 * (d & -d))
    parts = [[0], [1, top]] if top > 1 else [[0, 1]]
    parts += [[d] for d in range(2, chips) if d != top]
    queries, state = [], [bias]
    for number, part in enumerate(parts):
        blocks = []
        for d in part:
            block = far[d]
            if d:
                block = after(block, *state)
                near = swap(block, "seq", 1)
            else:
                near = swap(own, "seq", 1)
            blocks += [block, near]
        state = attend_part(
            number == 0, number == len(parts) - 1, w_qk, w_v, blocks, [*queries, *state]
        )
        if number == 0:
            queries, state = state[:2], state[2:]
    return state[0]


def solution(mesh):
    in_specs = (
        P(("group", "seq"), None),
        P(("group", "seq"), None),
        P(("group", "seq"), None),
        P(("group", "seq")),
        P(("group", "seq")),
        P(),
        P(),
        P(),
    )
    out_specs = P(("group", "seq"), None)
    return jax.shard_map(
        on_device, mesh=mesh, in_specs=in_specs, out_specs=out_specs, check_vma=False
    )
```

```python
import math

import jax
import jax.numpy as jnp
from jax import lax
from jax.experimental import pallas as pl
from jax.experimental.pallas import tpu as pltpu
from jax.sharding import PartitionSpec as P

H = 32
HD = 24
NB = 16
TILES = 8
LANES = 128
SET = 16
HALF = SET * HD
SLABS = HALF // LANES
SAFE = 1e30
TINY = pl.CostEstimate(flops=1000, bytes_accessed=1000, transcendentals=0)
EXTRA = 8
EARLY = 3 * LANES
SHIFT = 3 * NB
NT = (((1,), (1,)), ((), ()))
MIB = 1024 * 1024
BF16 = jnp.bfloat16
F32 = jnp.float32
FACTOR = math.log2(math.e) / math.sqrt(HD)


def vmem():
    return pl.BlockSpec(memory_space=pltpu.VMEM)


def smem():
    return pl.BlockSpec(memory_space=pltpu.SMEM)


def limit(mib):
    return pltpu.CompilerParams(vmem_limit_bytes=mib * MIB)


def shape(*dims, dtype=BF16):
    return jax.ShapeDtypeStruct(dims, dtype)


def one_hot_slab(bucket_row):
    n = bucket_row.shape[1]
    index = lax.broadcasted_iota(jnp.int32, (LANES, n), 0)
    wanted = jnp.where(index < 3 * NB, index % NB, -1).astype(F32)
    hot = jnp.where((wanted == bucket_row) | ((index >= SHIFT) & (index < SHIFT + 3)), 1.0, 0.0)
    return hot.T.astype(BF16)


def split_three(x):
    high = x.astype(BF16).astype(F32)
    mid = (x - high).astype(BF16).astype(F32)
    return high, mid, x - high - mid


def stage_kernel(bucket_ref, table_ref, bias_ref):
    table = table_ref[...] * math.sqrt(HD)
    at = lax.broadcasted_iota(jnp.int32, (NB, NB * NB), 1) // NB
    mine = at == lax.broadcasted_iota(jnp.int32, (NB, NB * NB), 0)
    key = lax.broadcasted_iota(jnp.int32, (NB * NB, LANES), 0) % NB
    column = lax.broadcasted_iota(jnp.int32, (NB * NB, LANES), 1)
    cube = jnp.zeros((H * NB, LANES), F32)
    for number, piece in enumerate(split_three(table)):
        spread = [jnp.where(mine, piece[h : h + 1, :], 0.0) for h in range(H)]
        place = jnp.where(column == key + number * NB, 1.0, 0.0).astype(BF16)
        cube = cube + jnp.dot(
            jnp.concatenate(spread, axis=0).astype(BF16), place, preferred_element_type=F32
        )
    cube = cube.astype(BF16)
    hot = one_hot_slab(bucket_ref[...].astype(F32))[:, :NB]
    for h in range(H):
        bias_ref[:, h * LANES : (h + 1) * LANES] = jnp.dot(
            hot, cube[h * NB : (h + 1) * NB, :], preferred_element_type=F32
        ).astype(BF16)


def aggregate(count_ref, me_ref, src_ref, tiles_ref, feature_refs, held):
    rows = feature_refs[0].shape[0]
    for d, ref in enumerate(feature_refs):
        held[d * rows : (d + 1) * rows, :] = ref[...]
    picked, masked = [], []
    for t in range(TILES):
        start = pl.multiple_of((src_ref[0, t] ^ me_ref[0]) * rows, rows)
        picked.append(held[pl.ds(start, rows), :])
        tile = tiles_ref[:, t * rows : (t + 1) * rows]
        masked.append(jnp.where(t < count_ref[0], tile, jnp.zeros_like(tile)))
    return feature_refs[0][...].astype(F32) + jnp.dot(
        jnp.concatenate(masked, axis=1),
        jnp.concatenate(picked, axis=0),
        preferred_element_type=F32,
    )


def early_kernel(count_ref, me_ref, src_ref, tiles_ref, *refs):
    *feature_refs, out_ref, square_ref, held = refs
    total = aggregate(count_ref, me_ref, src_ref, tiles_ref, feature_refs, held)
    out_ref[...] = total.astype(BF16)
    square = jnp.sum(total * total, axis=-1, keepdims=True)
    square_ref[...] = jnp.broadcast_to(square, square_ref.shape)


def late_kernel(count_ref, me_ref, src_ref, tiles_ref, bucket_ref, square_ref, *refs):
    *feature_refs, out_ref, held = refs
    total = aggregate(count_ref, me_ref, src_ref, tiles_ref, feature_refs, held)
    rows, span = total.shape
    width = span + EARLY
    square = jnp.sum(total * total, axis=-1, keepdims=True) + square_ref[...]
    scale = lax.rsqrt(square * (1.0 / width) + 1e-06)
    turned = scale.T[:EXTRA, :]
    row = lax.broadcasted_iota(jnp.int32, (EXTRA, rows), 0)
    below = jnp.where(row == 0, bucket_ref[...].astype(F32), 0.0)
    for number, piece in enumerate(split_three(turned)):
        below = jnp.where(row == number + 1, piece, below)
    below = jnp.concatenate([below, jnp.zeros((EXTRA, span - rows), F32)], axis=1)
    out_ref[...] = jnp.concatenate([total * scale[:, :1], below], axis=0).astype(BF16)


def slab_heads(slab):
    return slab * LANES // HD, ((slab + 1) * LANES - 1) // HD


def part_kernel(count, first, last, w_qk_ref, w_v_ref, *refs):
    block_refs, refs = refs[: 2 * count], refs[2 * count :]
    hot_ref, k_ref, v_ref, p_ref, *refs_back = refs[-5:]
    top_ref = refs_back[0]
    refs = refs[:-5]
    if first:
        bias_ref, q_ref, shifted_ref, *outs = refs
    else:
        q_ref, bias_ref, *refs = refs
        old_refs, outs = (refs[:2], refs[2:]) if len(refs) in (3, 5) else (refs[:3], refs[3:])
    rows = q_ref.shape[0]
    keys = hot_ref.shape[0]
    width = w_v_ref.shape[0]
    early = jnp.concatenate([ref[...] for ref in block_refs[::2]], axis=0)
    late, scale = [], []
    for s, ref in enumerate(block_refs[1::2]):
        item = ref[...]
        below = item[rows:, :rows].astype(F32)
        hot_ref[s * rows : (s + 1) * rows, :] = one_hot_slab(below[:1, :])
        scale.append(jnp.broadcast_to(below[1:2, :] + below[2:3, :] + below[3:4, :], (rows, rows)).T)
        late.append(item[:rows, :])
    late = jnp.concatenate(late, axis=0)
    scale = jnp.concatenate(scale, axis=0)
    scale = jnp.concatenate([scale, scale], axis=1)

    def project(n, w_ref, base, count):
        cols = slice(base + n, base + n + 256)
        one = jnp.dot(early[:count, :], w_ref[:EARLY, cols], preferred_element_type=F32)
        two = jnp.dot(late[:count, :], w_ref[EARLY:, cols], preferred_element_type=F32)
        return (one * scale[:count, :] + two).astype(BF16)

    for n in range(0, width, 256):
        if first:
            q_ref[:, n : n + 256] = project(n, w_qk_ref, 0, rows)
        k_ref[:, n : n + 256] = project(n, w_qk_ref, width, keys)
        v_ref[:, n : n + 256] = project(n, w_v_ref, 0, keys)

    lane = lax.broadcasted_iota(jnp.int32, (rows, LANES), 1)
    ones = jnp.ones((keys, LANES), BF16)

    def scores(half, slab):
        cols = pl.ds(pl.multiple_of(half * HALF + slab * LANES, LANES), LANES)
        begin, end = slab_heads(slab)
        q = q_ref[:, cols]
        zero = jnp.zeros_like(q)
        lefts, rights = [], []
        for h in range(begin, end + 1):
            inside = (lane >= h * HD - slab * LANES) & (lane < (h + 1) * HD - slab * LANES)
            lefts.append(jnp.where(inside, q, zero))
            if h * HD >= slab * LANES:
                at = pl.multiple_of((half * SET + h) * LANES, LANES)
                rights.append(bias_ref[:, pl.ds(at, LANES)])
            else:
                rights.append(zero)
        query = jnp.concatenate(
            [jnp.concatenate(lefts, axis=0), jnp.concatenate(rights, axis=0)], axis=1
        )
        key = jnp.concatenate([k_ref[:, cols], hot_ref[...]], axis=1)
        return lax.dot_general(query, key, NT, preferred_element_type=F32)

    def weigh(half, local):
        carried = None
        for slab in range(SLABS):
            begin, end = slab_heads(slab)
            x = scores(half, slab)
            for h in range(begin, end + 1):
                own = x[(h - begin) * rows : (h - begin + 1) * rows, :]
                if h * HD < slab * LANES:
                    own = own + carried
                if (h + 1) * HD > (slab + 1) * LANES:
                    carried = own
                    continue
                if local:
                    peak = jnp.max(own, axis=-1, keepdims=True)
                    own = own - peak
                    keep_peak(half, h, peak)
                p_ref[h * rows : (h + 1) * rows, :] = jnp.exp2(own * FACTOR).astype(BF16)

    def keep_peak(half, h, peak):
        if first:
            at = pl.ds(pl.multiple_of((half * SET + h) * LANES, LANES), LANES)
            mark = jnp.zeros((rows, LANES), F32)
            for number, piece in enumerate(split_three(-peak)):
                mark = jnp.where(lane == SHIFT + number, piece, mark)
            shifted_ref[:, at] = bias_ref[:, at] + mark.astype(BF16)
        else:
            top_ref[h * rows : (h + 1) * rows, :] = jnp.broadcast_to(peak, (rows, LANES))

    def pick(array, slab, base):
        begin, end = slab_heads(slab)
        out = array[(begin - base) * rows : (begin - base + 1) * rows, :]
        for h in range(begin + 1, end + 1):
            piece = array[(h - base) * rows : (h - base + 1) * rows, :]
            out = jnp.where(lane >= h * HD - slab * LANES, piece, out)
        return out

    def mix(half, slab):
        cols = pl.ds(pl.multiple_of(half * HALF + slab * LANES, LANES), LANES)
        begin, end = slab_heads(slab)
        value = jnp.concatenate([v_ref[:, cols], ones], axis=1)
        mixed = jnp.dot(
            p_ref[begin * rows : (end + 1) * rows, :], value, preferred_element_type=F32
        )
        return cols, pick(mixed[:, :LANES], slab, begin), pick(mixed[:, LANES:], slab, begin)

    def fast(half, largest):
        weigh(half, first)
        for slab in range(SLABS):
            cols, top, total = mix(half, slab)
            if not first:
                top = top + old_refs[0][:, cols]
                total = total + old_refs[1][:, cols]
            largest = jnp.maximum(largest, total)
            if last:
                outs[0][:, cols] = (top / total).astype(BF16)
            else:
                outs[0][:, cols] = top
                outs[1][:, cols] = total
                if not first:
                    outs[2][:, cols] = jnp.zeros_like(top)
        return largest

    largest = lax.fori_loop(0, width // HALF, fast, jnp.zeros((rows, LANES), F32))
    if first:
        return
    fine = jnp.max(largest) < SAFE
    if len(old_refs) == 3:
        fine = fine & (jnp.max(old_refs[2][...]) == 0.0)

    @pl.when(jnp.logical_not(fine))
    def _():
        def careful(half, carry):
            weigh(half, True)
            for slab in range(SLABS):
                cols, top, total = mix(half, slab)
                peak = pick(top_ref[...], slab, 0)
                old = old_refs[2][:, cols] if len(old_refs) == 3 else jnp.zeros_like(top)
                best = jnp.maximum(old, peak)
                share = jnp.exp2((peak - best) * FACTOR)
                old_share = jnp.exp2((old - best) * FACTOR)
                top = top * share + old_refs[0][:, cols] * old_share
                total = total * share + old_refs[1][:, cols] * old_share
                if last:
                    outs[0][:, cols] = (top / total).astype(BF16)
                else:
                    outs[0][:, cols] = top
                    outs[1][:, cols] = total
                    outs[2][:, cols] = best
            return carry

        lax.fori_loop(0, width // HALF, careful, 0)


def attend_part(first, last, w_qk, w_v, blocks, inputs):
    width = w_v.shape[0]
    rows = blocks[0][0].shape[0]
    keys = rows * len(blocks)
    state = shape(rows, width, dtype=F32)
    if first:
        outs = [shape(rows, width), shape(rows, H * LANES), state, state]
    elif last:
        outs = [shape(rows, width)]
    else:
        outs = [state] * 3
    operands = [w_qk, w_v, *(piece for block in blocks for piece in block), *inputs]
    tall = SET * rows
    need = 2 * tall * keys + 4 * keys * width + 4 * tall * LANES
    return pl.pallas_call(
        lambda *refs: part_kernel(len(blocks), first, last, *refs),
        out_shape=outs,
        in_specs=[vmem()] * len(operands),
        out_specs=[vmem()] * len(outs),
        scratch_shapes=[
            pltpu.VMEM((keys, LANES), BF16),
            pltpu.VMEM((keys, width), BF16),
            pltpu.VMEM((keys, width), BF16),
            pltpu.VMEM((tall, keys), BF16),
            pltpu.VMEM((tall, LANES), F32),
        ],
        compiler_params=limit(need // MIB + 8),
        cost_estimate=pl.CostEstimate(flops=10**9, bytes_accessed=4_000_000, transcendentals=0),
        name="part",
    )(*operands)


def swap(array, axis, distance):
    return lax.ppermute(array, axis, [(i, i ^ distance) for i in range(lax.axis_size(axis))])


def after(value, *others):
    return lax.optimization_barrier((value, others))[0]


def on_device(features, tiles, tile_src, tile_count, node_bucket, w_qk, w_v, bias_table):
    rows, width = features.shape
    groups = lax.axis_size("group")
    seq_count = lax.axis_size("seq")
    chips = seq_count // 2
    own_bucket = node_bucket.reshape(1, rows)
    me = lax.axis_index("group").reshape(1)

    def gather(piece):
        return [piece] + [swap(piece, "group", d) for d in range(1, groups)]

    def hop(pieces, distance):
        return [swap(piece, "seq", distance) for piece in pieces]

    first_columns = gather(features[:, :EARLY])
    other_columns = gather(features[:, EARLY:])
    early, square = pl.pallas_call(
        early_kernel,
        out_shape=[shape(rows, EARLY), shape(rows, LANES, dtype=F32)],
        in_specs=[smem()] * 3 + [vmem()] * (1 + groups),
        out_specs=[vmem()] * 2,
        scratch_shapes=[pltpu.VMEM((groups * rows, EARLY), BF16)],
        compiler_params=limit(8),
        cost_estimate=pl.CostEstimate(flops=10**9, bytes_accessed=4_000_000, transcendentals=0),
        name="early",
    )(tile_count, me, tile_src, tiles, *first_columns)
    late = pl.pallas_call(
        late_kernel,
        out_shape=shape(rows + EXTRA, width - EARLY),
        in_specs=[smem()] * 3 + [vmem()] * (3 + groups),
        out_specs=vmem(),
        scratch_shapes=[pltpu.VMEM((groups * rows, width - EARLY), BF16)],
        compiler_params=limit(8),
        cost_estimate=pl.CostEstimate(flops=10**9, bytes_accessed=4_000_000, transcendentals=0),
        name="late",
    )(tile_count, me, tile_src, tiles, own_bucket, square, *other_columns)
    far = [[early, late]] + [None] * (chips - 1)
    top = 1
    while 2 * top < chips:
        top *= 2
    far[top] = hop(far[0], 2 * top)
    step = 1
    while step < top:
        far[step] = hop(far[0], 2 * step)
        step *= 2
    sister = hop(far[0], 1)

    bias = pl.pallas_call(
        stage_kernel,
        out_shape=shape(rows, H * LANES),
        in_specs=[vmem()] * 2,
        out_specs=vmem(),
        compiler_params=limit(8),
        cost_estimate=pl.CostEstimate(flops=10**9, bytes_accessed=4_000_000, transcendentals=0),
        name="stage",
    )(own_bucket, after(bias_table, sister[0], far[1][0], far[top][0]))

    parts = [[0], [1, top]] if top > 1 else [[0, 1]]
    parts += [[d] for d in range(2, chips) if d != top]
    queries, state = [], [bias]
    for number, part in enumerate(parts):
        if number == 1:
            for d in range(3, chips):
                if far[d] is None:
                    far[d] = hop([after(piece, *state) for piece in far[d & (d - 1)]], 2 * (d & -d))
        blocks = []
        for d in part:
            pieces = [after(piece, *state) for piece in far[d]] if d else far[0]
            blocks += [pieces, hop(pieces, 1) if d else sister]
        state = attend_part(
            number == 0, number == len(parts) - 1, w_qk, w_v, blocks, [*queries, *state]
        )
        if number == 0:
            queries, state = state[:2], state[2:]
    return state[0]


def solution(mesh):
    in_specs = (
        P(("group", "seq"), None),
        P(("group", "seq"), None),
        P(("group", "seq"), None),
        P(("group", "seq")),
        P(("group", "seq")),
        P(),
        P(),
        P(),
    )
    out_specs = P(("group", "seq"), None)
    return jax.shard_map(
        on_device, mesh=mesh, in_specs=in_specs, out_specs=out_specs, check_vma=False
    )
```

```python
import math

import jax
import jax.numpy as jnp
from jax import lax
from jax.experimental import pallas as pl
from jax.experimental.pallas import tpu as pltpu
from jax.sharding import PartitionSpec as P

H = 32
HD = 24
NB = 16
TILES = 8
LANES = 128
SET = 16
HALF = SET * HD
SLABS = HALF // LANES
SAFE = 1e30
EXTRA = 8
SHIFT = 3 * NB
NT = (((1,), (1,)), ((), ()))
MIB = 1024 * 1024
BF16 = jnp.bfloat16
F32 = jnp.float32
FACTOR = math.log2(math.e) / math.sqrt(HD)


def vmem():
    return pl.BlockSpec(memory_space=pltpu.VMEM)


def smem():
    return pl.BlockSpec(memory_space=pltpu.SMEM)


def limit(mib):
    return pltpu.CompilerParams(vmem_limit_bytes=mib * MIB)


def shape(*dims, dtype=BF16):
    return jax.ShapeDtypeStruct(dims, dtype)


def one_hot_slab(bucket_row):
    n = bucket_row.shape[1]
    index = lax.broadcasted_iota(jnp.int32, (LANES, n), 0)
    wanted = jnp.where(index < 3 * NB, index % NB, -1).astype(F32)
    hot = jnp.where((wanted == bucket_row) | ((index >= SHIFT) & (index < SHIFT + 3)), 1.0, 0.0)
    return hot.T.astype(BF16)


def split_three(x):
    high = x.astype(BF16).astype(F32)
    mid = (x - high).astype(BF16).astype(F32)
    return high, mid, x - high - mid


def stage_kernel(
    count_ref, me_ref, src_ref, table_ref, bucket_ref, features_ref, tiles_ref,
    bias_ref, own_ref, masked_ref, extra_ref, from_ref, tiles_held, sems,
):
    rows = own_ref.shape[0]
    copies = [
        pltpu.make_async_copy(tiles_ref, tiles_held, sems.at[0]),
        pltpu.make_async_copy(features_ref, own_ref, sems.at[1]),
    ]
    for copy in copies:
        copy.start()
    for t in range(TILES):
        from_ref[t : t + 1, :] = jnp.full((1, LANES), src_ref[0, t] ^ me_ref[0], jnp.int32)
    width = own_ref.shape[1]
    extra = jnp.concatenate(
        [bucket_ref[...].astype(F32), jnp.zeros((1, width - rows), F32)], axis=1
    )
    extra_ref[...] = jnp.broadcast_to(extra, (EXTRA, width))
    table = table_ref[...] * math.sqrt(HD)
    at = lax.broadcasted_iota(jnp.int32, (NB, NB * NB), 1) // NB
    mine = at == lax.broadcasted_iota(jnp.int32, (NB, NB * NB), 0)
    key = lax.broadcasted_iota(jnp.int32, (NB * NB, LANES), 0) % NB
    column = lax.broadcasted_iota(jnp.int32, (NB * NB, LANES), 1)
    cube = jnp.zeros((H * NB, LANES), F32)
    for number, piece in enumerate(split_three(table)):
        spread = [jnp.where(mine, piece[h : h + 1, :], 0.0) for h in range(H)]
        place = jnp.where(column == key + number * NB, 1.0, 0.0).astype(BF16)
        cube = cube + jnp.dot(
            jnp.concatenate(spread, axis=0).astype(BF16), place, preferred_element_type=F32
        )
    cube = cube.astype(BF16)
    hot = one_hot_slab(bucket_ref[...].astype(F32))[:, :NB]
    for h in range(H):
        bias_ref[:, h * LANES : (h + 1) * LANES] = jnp.dot(
            hot, cube[h * NB : (h + 1) * NB, :], preferred_element_type=F32
        ).astype(BF16)
    for copy in copies:
        copy.wait()
    for t in range(TILES):
        tile = tiles_held[:, t * rows : (t + 1) * rows]
        masked_ref[:, t * rows : (t + 1) * rows] = jnp.where(
            t < count_ref[0], tile, jnp.zeros_like(tile)
        )


def aggregate_kernel(from_ref, extra_ref, masked_ref, *refs):
    feature_refs, out_ref, held = refs[:-2], refs[-2], refs[-1]
    rows = feature_refs[0].shape[0]
    for d, ref in enumerate(feature_refs):
        held[d * rows : (d + 1) * rows, :] = ref[...]
    picked = []
    for t in range(TILES):
        start = pl.multiple_of(from_ref[t, 0] * rows, rows)
        picked.append(held[pl.ds(start, rows), :])
    total = feature_refs[0][...].astype(F32) + jnp.dot(
        masked_ref[...], jnp.concatenate(picked, axis=0), preferred_element_type=F32
    )
    mean_square = jnp.mean(total * total, axis=-1, keepdims=True)
    out_ref[...] = jnp.concatenate(
        [total * lax.rsqrt(mean_square + 1e-06), extra_ref[...]], axis=0
    ).astype(BF16)


def slab_heads(slab):
    return slab * LANES // HD, ((slab + 1) * LANES - 1) // HD


def part_kernel(count, first, last, w_qk_ref, w_v_ref, *refs):
    block_refs, refs = refs[:count], refs[count:]
    hot_ref, k_ref, v_ref, p_refs, *refs_back = *refs[-6:-3], refs[-3:-1], refs[-1]
    top_ref = refs_back[0]
    refs = refs[:-6]
    if first:
        bias_ref, q_ref, shifted_ref, *outs = refs
    else:
        q_ref, bias_ref, *refs = refs
        old_refs, outs = (refs[:2], refs[2:]) if len(refs) in (3, 5) else (refs[:3], refs[3:])
    rows = q_ref.shape[0]
    keys = hot_ref.shape[0]
    width = w_v_ref.shape[0]
    arrived = [ref[...] for ref in block_refs]
    for s, item in enumerate(arrived):
        bucket = item[rows:, :rows].astype(F32)[:1, :]
        hot_ref[s * rows : (s + 1) * rows, :] = one_hot_slab(bucket)
    block = jnp.concatenate([item[:rows, :] for item in arrived], axis=0)
    if first:
        for n in range(0, width, 256):
            q_ref[:, n : n + 256] = jnp.dot(
                block[:rows, :], w_qk_ref[:, n : n + 256], preferred_element_type=F32
            ).astype(BF16)
    for n in range(0, width, 256):
        k_ref[:, n : n + 256] = jnp.dot(
            block, w_qk_ref[:, width + n : width + n + 256], preferred_element_type=F32
        ).astype(BF16)
        v_ref[:, n : n + 256] = jnp.dot(
            block, w_v_ref[:, n : n + 256], preferred_element_type=F32
        ).astype(BF16)

    lane = lax.broadcasted_iota(jnp.int32, (rows, LANES), 1)
    ones = jnp.ones((keys, LANES), BF16)

    def span(start, size):
        return pl.ds(start if isinstance(start, int) else pl.multiple_of(start, LANES), size)

    def scores(half, slab):
        cols = span(half * HALF + slab * LANES, LANES)
        begin, end = slab_heads(slab)
        q = q_ref[:, cols]
        zero = jnp.zeros_like(q)
        lefts, rights = [], []
        for h in range(begin, end + 1):
            inside = (lane >= h * HD - slab * LANES) & (lane < (h + 1) * HD - slab * LANES)
            lefts.append(jnp.where(inside, q, zero))
            if h * HD >= slab * LANES:
                rights.append(bias_ref[:, span((half * SET + h) * LANES, LANES)])
            else:
                rights.append(zero)
        query = jnp.concatenate(
            [jnp.concatenate(lefts, axis=0), jnp.concatenate(rights, axis=0)], axis=1
        )
        key = jnp.concatenate([k_ref[:, cols], hot_ref[...]], axis=1)
        return lax.dot_general(query, key, NT, preferred_element_type=F32)

    def weigh(half, slab, x, carried, p_ref, local):
        begin, end = slab_heads(slab)
        for h in range(begin, end + 1):
            own = x[(h - begin) * rows : (h - begin + 1) * rows, :]
            if h * HD < slab * LANES:
                own = own + carried
            if (h + 1) * HD > (slab + 1) * LANES:
                return own
            if local:
                peak = jnp.max(own, axis=-1, keepdims=True)
                own = own - peak
                keep_peak(half, h, peak)
            p_ref[h * rows : (h + 1) * rows, :] = jnp.exp2(own * FACTOR).astype(BF16)
        return None

    def keep_peak(half, h, peak):
        if first:
            at = span((half * SET + h) * LANES, LANES)
            mark = jnp.zeros((rows, LANES), F32)
            for number, piece in enumerate(split_three(-peak)):
                mark = jnp.where(lane == SHIFT + number, piece, mark)
            shifted_ref[:, at] = bias_ref[:, at] + mark.astype(BF16)
        else:
            top_ref[h * rows : (h + 1) * rows, :] = jnp.broadcast_to(peak, (rows, LANES))

    def pick(array, slab, base):
        begin, end = slab_heads(slab)
        out = array[(begin - base) * rows : (begin - base + 1) * rows, :]
        for h in range(begin + 1, end + 1):
            piece = array[(h - base) * rows : (h - base + 1) * rows, :]
            out = jnp.where(lane >= h * HD - slab * LANES, piece, out)
        return out

    def mix(half, slab, p_ref):
        cols = span(half * HALF + slab * LANES, LANES)
        begin, end = slab_heads(slab)
        value = jnp.concatenate([v_ref[:, cols], ones], axis=1)
        mixed = jnp.dot(
            p_ref[begin * rows : (end + 1) * rows, :], value, preferred_element_type=F32
        )
        return cols, pick(mixed[:, :LANES], slab, begin), pick(mixed[:, LANES:], slab, begin)

    def add(half, slab, p_ref):
        cols, top, total = mix(half, slab, p_ref)
        if not first:
            top = top + old_refs[0][:, cols]
            total = total + old_refs[1][:, cols]
        if last:
            outs[0][:, cols] = (top / total).astype(BF16)
        else:
            outs[0][:, cols] = top
            outs[1][:, cols] = total
            if not first:
                outs[2][:, cols] = jnp.zeros_like(top)
        return total

    steps = [divmod(step, SLABS) for step in range(width // LANES)]
    largest = jnp.zeros((rows, LANES), F32)
    x = scores(*steps[0])
    carried = None
    for number, (half, slab) in enumerate(steps):
        ahead = scores(*steps[number + 1]) if number + 1 < len(steps) else None
        carried = weigh(half, slab, x, carried, p_refs[half % 2], first)
        if number:
            before = steps[number - 1]
            largest = jnp.maximum(largest, add(*before, p_refs[before[0] % 2]))
        x = ahead
    largest = jnp.maximum(largest, add(*steps[-1], p_refs[steps[-1][0] % 2]))
    if first:
        return
    fine = jnp.max(largest) < SAFE
    if len(old_refs) == 3:
        fine = fine & (jnp.max(old_refs[2][...]) == 0.0)

    @pl.when(jnp.logical_not(fine))
    def _():
        def careful(half, carry):
            left = None
            for slab in range(SLABS):
                left = weigh(half, slab, scores(half, slab), left, p_refs[0], True)
            for slab in range(SLABS):
                cols, top, total = mix(half, slab, p_refs[0])
                peak = pick(top_ref[...], slab, 0)
                old = old_refs[2][:, cols] if len(old_refs) == 3 else jnp.zeros_like(top)
                best = jnp.maximum(old, peak)
                share = jnp.exp2((peak - best) * FACTOR)
                old_share = jnp.exp2((old - best) * FACTOR)
                top = top * share + old_refs[0][:, cols] * old_share
                total = total * share + old_refs[1][:, cols] * old_share
                if last:
                    outs[0][:, cols] = (top / total).astype(BF16)
                else:
                    outs[0][:, cols] = top
                    outs[1][:, cols] = total
                    outs[2][:, cols] = best
            return carry

        lax.fori_loop(0, width // HALF, careful, 0)


def attend_part(first, last, w_qk, w_v, blocks, inputs):
    width = w_v.shape[0]
    rows = blocks[0].shape[0] - EXTRA
    keys = rows * len(blocks)
    state = shape(rows, width, dtype=F32)
    if first:
        outs = [shape(rows, width), shape(rows, H * LANES), state, state]
    elif last:
        outs = [shape(rows, width)]
    else:
        outs = [state] * 3
    operands = [w_qk, w_v, *blocks, *inputs]
    tall = SET * rows
    need = 4 * tall * keys + 4 * keys * width + 4 * tall * LANES
    return pl.pallas_call(
        lambda *refs: part_kernel(len(blocks), first, last, *refs),
        out_shape=outs,
        in_specs=[vmem()] * len(operands),
        out_specs=[vmem()] * len(outs),
        scratch_shapes=[
            pltpu.VMEM((keys, LANES), BF16),
            pltpu.VMEM((keys, width), BF16),
            pltpu.VMEM((keys, width), BF16),
            pltpu.VMEM((tall, keys), BF16),
            pltpu.VMEM((tall, keys), BF16),
            pltpu.VMEM((tall, LANES), F32),
        ],
        compiler_params=limit(need // MIB + 8),
        cost_estimate=pl.CostEstimate(flops=10**9, bytes_accessed=4_000_000, transcendentals=0),
        name="part",
    )(*operands)


def swap(array, axis, distance):
    return lax.ppermute(array, axis, [(i, i ^ distance) for i in range(lax.axis_size(axis))])


def after(value, *others):
    return lax.optimization_barrier((value, others))[0]


def on_device(features, tiles, tile_src, tile_count, node_bucket, w_qk, w_v, bias_table):
    rows, width = features.shape
    groups = lax.axis_size("group")
    seq_count = lax.axis_size("seq")
    chips = seq_count // 2
    any_space = pl.BlockSpec(memory_space=pl.ANY)

    received = [swap(features, "group", d) for d in range(groups - 1, 0, -1)][::-1]
    own_bucket = node_bucket.reshape(1, rows)

    bias, own_features, masked, extra, source = pl.pallas_call(
        stage_kernel,
        out_shape=[
            shape(rows, H * LANES), shape(rows, width), shape(rows, TILES * rows),
            shape(EXTRA, width, dtype=F32),
            shape(TILES, LANES, dtype=jnp.int32),
        ],
        in_specs=[smem()] * 3 + [vmem(), vmem(), any_space, any_space],
        out_specs=[vmem()] * 5,
        scratch_shapes=[pltpu.VMEM((rows, TILES * rows), BF16), pltpu.SemaphoreType.DMA((2,))],
        compiler_params=limit(8),
        cost_estimate=pl.CostEstimate(flops=10**9, bytes_accessed=4_000_000, transcendentals=0),
        name="stage",
    )(tile_count, lax.axis_index("group").reshape(1), tile_src, bias_table, own_bucket, features, tiles)

    own = pl.pallas_call(
        aggregate_kernel,
        out_shape=shape(rows + EXTRA, width),
        in_specs=[vmem()] * (3 + groups),
        out_specs=vmem(),
        scratch_shapes=[pltpu.VMEM((groups * rows, width), BF16)],
        compiler_params=limit(8),
        cost_estimate=pl.CostEstimate(flops=10**9, bytes_accessed=4_000_000, transcendentals=0),
        name="aggregate",
    )(source, extra, masked, own_features, *received)

    far = [own] + [None] * (chips - 1)
    top = 1
    while 2 * top < chips:
        top *= 2
    far[top] = swap(own, "seq", 2 * top)
    step = 1
    while step < top:
        far[step] = swap(own, "seq", 2 * step)
        step *= 2
    for d in range(3, chips):
        if far[d] is None:
            far[d] = swap(far[d & (d - 1)], "seq", 2 * (d & -d))
    parts = [[0], [1, top]] if top > 1 else [[0, 1]]
    parts += [[d] for d in range(2, chips) if d != top]
    queries, state = [], [bias]
    for number, part in enumerate(parts):
        blocks = []
        for d in part:
            block = far[d]
            if d:
                block = after(block, *state)
                near = swap(block, "seq", 1)
            else:
                near = swap(own, "seq", 1)
            blocks += [block, near]
        state = attend_part(
            number == 0, number == len(parts) - 1, w_qk, w_v, blocks, [*queries, *state]
        )
        if number == 0:
            queries, state = state[:2], state[2:]
    return state[0]


def solution(mesh):
    in_specs = (
        P(("group", "seq"), None),
        P(("group", "seq"), None),
        P(("group", "seq"), None),
        P(("group", "seq")),
        P(("group", "seq")),
        P(),
        P(),
        P(),
    )
    out_specs = P(("group", "seq"), None)
    return jax.shard_map(
        on_device, mesh=mesh, in_specs=in_specs, out_specs=out_specs, check_vma=False
    )
```

```python
import math

import jax
import jax.numpy as jnp
from jax import lax
from jax.experimental import pallas as pl
from jax.experimental.pallas import tpu as pltpu
from jax.sharding import PartitionSpec as P

H = 32
HD = 24
NB = 16
TILES = 8
LANES = 128
SET = 16
HALF = SET * HD
SLABS = HALF // LANES
SAFE = 1e30
EXTRA = 8
SHIFT = 3 * NB
NT = (((1,), (1,)), ((), ()))
MIB = 1024 * 1024
BF16 = jnp.bfloat16
F32 = jnp.float32
FACTOR = math.log2(math.e) / math.sqrt(HD)


def vmem():
    return pl.BlockSpec(memory_space=pltpu.VMEM)


def smem():
    return pl.BlockSpec(memory_space=pltpu.SMEM)


def limit(mib):
    return pltpu.CompilerParams(vmem_limit_bytes=mib * MIB)


def shape(*dims, dtype=BF16):
    return jax.ShapeDtypeStruct(dims, dtype)


def one_hot_slab(bucket_row):
    n = bucket_row.shape[1]
    index = lax.broadcasted_iota(jnp.int32, (LANES, n), 0)
    wanted = jnp.where(index < 3 * NB, index % NB, -1).astype(F32)
    hot = jnp.where((wanted == bucket_row) | ((index >= SHIFT) & (index < SHIFT + 3)), 1.0, 0.0)
    return hot.T.astype(BF16)


def split_three(x):
    high = x.astype(BF16).astype(F32)
    mid = (x - high).astype(BF16).astype(F32)
    return high, mid, x - high - mid


def stage_kernel(
    count_ref, me_ref, src_ref, table_ref, bucket_ref, features_ref, tiles_ref,
    bias_ref, own_ref, masked_ref, extra_ref, from_ref, tiles_held, sems,
):
    rows = own_ref.shape[0]
    copies = [
        pltpu.make_async_copy(tiles_ref, tiles_held, sems.at[0]),
        pltpu.make_async_copy(features_ref, own_ref, sems.at[1]),
    ]
    for copy in copies:
        copy.start()
    for t in range(TILES):
        from_ref[t : t + 1, :] = jnp.full((1, LANES), src_ref[0, t] ^ me_ref[0], jnp.int32)
    width = own_ref.shape[1]
    extra = jnp.concatenate(
        [bucket_ref[...].astype(F32), jnp.zeros((1, width - rows), F32)], axis=1
    )
    extra_ref[...] = jnp.broadcast_to(extra, (EXTRA, width))
    table = table_ref[...] * math.sqrt(HD)
    at = lax.broadcasted_iota(jnp.int32, (NB, NB * NB), 1) // NB
    mine = at == lax.broadcasted_iota(jnp.int32, (NB, NB * NB), 0)
    key = lax.broadcasted_iota(jnp.int32, (NB * NB, LANES), 0) % NB
    column = lax.broadcasted_iota(jnp.int32, (NB * NB, LANES), 1)
    cube = jnp.zeros((H * NB, LANES), F32)
    for number, piece in enumerate(split_three(table)):
        spread = [jnp.where(mine, piece[h : h + 1, :], 0.0) for h in range(H)]
        place = jnp.where(column == key + number * NB, 1.0, 0.0).astype(BF16)
        cube = cube + jnp.dot(
            jnp.concatenate(spread, axis=0).astype(BF16), place, preferred_element_type=F32
        )
    cube = cube.astype(BF16)
    hot = one_hot_slab(bucket_ref[...].astype(F32))[:, :NB]
    for h in range(H):
        bias_ref[:, h * LANES : (h + 1) * LANES] = jnp.dot(
            hot, cube[h * NB : (h + 1) * NB, :], preferred_element_type=F32
        ).astype(BF16)
    for copy in copies:
        copy.wait()
    for t in range(TILES):
        tile = tiles_held[:, t * rows : (t + 1) * rows]
        masked_ref[:, t * rows : (t + 1) * rows] = jnp.where(
            t < count_ref[0], tile, jnp.zeros_like(tile)
        )


def aggregate_kernel(from_ref, extra_ref, masked_ref, *refs):
    feature_refs, out_ref, held = refs[:-2], refs[-2], refs[-1]
    rows = feature_refs[0].shape[0]
    for d, ref in enumerate(feature_refs):
        held[d * rows : (d + 1) * rows, :] = ref[...]
    picked = []
    for t in range(TILES):
        start = pl.multiple_of(from_ref[t, 0] * rows, rows)
        picked.append(held[pl.ds(start, rows), :])
    total = feature_refs[0][...].astype(F32) + jnp.dot(
        masked_ref[...], jnp.concatenate(picked, axis=0), preferred_element_type=F32
    )
    mean_square = jnp.mean(total * total, axis=-1, keepdims=True)
    out_ref[...] = jnp.concatenate(
        [total * lax.rsqrt(mean_square + 1e-06), extra_ref[...]], axis=0
    ).astype(BF16)


def slab_heads(slab):
    return slab * LANES // HD, ((slab + 1) * LANES - 1) // HD


def part_kernel(count, first, last, w_qk_ref, w_v_ref, *refs):
    block_refs, refs = refs[:count], refs[count:]
    hot_ref, k_ref, v_ref, p_refs, *refs_back = *refs[-6:-3], refs[-3:-1], refs[-1]
    top_ref = refs_back[0]
    refs = refs[:-6]
    if first:
        bias_ref, q_ref, shifted_ref, *outs = refs
    else:
        q_ref, bias_ref, *refs = refs
        old_refs, outs = (refs[:2], refs[2:]) if len(refs) in (3, 5) else (refs[:3], refs[3:])
    rows = q_ref.shape[0]
    keys = hot_ref.shape[0]
    width = w_v_ref.shape[0]
    arrived = [ref[...] for ref in block_refs]
    for s, item in enumerate(arrived):
        bucket = item[rows:, :rows].astype(F32)[:1, :]
        hot_ref[s * rows : (s + 1) * rows, :] = one_hot_slab(bucket)
    block = jnp.concatenate([item[:rows, :] for item in arrived], axis=0)
    if first:
        for n in range(0, width, 256):
            q_ref[:, n : n + 256] = jnp.dot(
                block[:rows, :], w_qk_ref[:, n : n + 256], preferred_element_type=F32
            ).astype(BF16)
    for n in range(0, width, 256):
        k_ref[:, n : n + 256] = jnp.dot(
            block, w_qk_ref[:, width + n : width + n + 256], preferred_element_type=F32
        ).astype(BF16)
        v_ref[:, n : n + 256] = jnp.dot(
            block, w_v_ref[:, n : n + 256], preferred_element_type=F32
        ).astype(BF16)

    lane = lax.broadcasted_iota(jnp.int32, (rows, LANES), 1)
    ones = jnp.ones((keys, LANES), BF16)

    def span(start, size):
        return pl.ds(start if isinstance(start, int) else pl.multiple_of(start, LANES), size)

    def scores(half, slab):
        cols = span(half * HALF + slab * LANES, LANES)
        begin, end = slab_heads(slab)
        q = q_ref[:, cols]
        zero = jnp.zeros_like(q)
        lefts, rights = [], []
        for h in range(begin, end + 1):
            inside = (lane >= h * HD - slab * LANES) & (lane < (h + 1) * HD - slab * LANES)
            lefts.append(jnp.where(inside, q, zero))
            if h * HD >= slab * LANES:
                rights.append(bias_ref[:, span((half * SET + h) * LANES, LANES)])
            else:
                rights.append(zero)
        query = jnp.concatenate(
            [jnp.concatenate(lefts, axis=0), jnp.concatenate(rights, axis=0)], axis=1
        )
        key = jnp.concatenate([k_ref[:, cols], hot_ref[...]], axis=1)
        return lax.dot_general(query, key, NT, preferred_element_type=F32)

    def weigh(half, slab, x, carried, p_ref, local):
        begin, end = slab_heads(slab)
        for h in range(begin, end + 1):
            own = x[(h - begin) * rows : (h - begin + 1) * rows, :]
            if h * HD < slab * LANES:
                own = own + carried
            if (h + 1) * HD > (slab + 1) * LANES:
                return own
            if local:
                peak = jnp.max(own, axis=-1, keepdims=True)
                own = own - peak
                keep_peak(half, h, peak)
            p_ref[h * rows : (h + 1) * rows, :] = jnp.exp2(own * FACTOR).astype(BF16)
        return None

    def keep_peak(half, h, peak):
        if first:
            at = span((half * SET + h) * LANES, LANES)
            mark = jnp.zeros((rows, LANES), F32)
            for number, piece in enumerate(split_three(-peak)):
                mark = jnp.where(lane == SHIFT + number, piece, mark)
            shifted_ref[:, at] = bias_ref[:, at] + mark.astype(BF16)
        else:
            top_ref[h * rows : (h + 1) * rows, :] = jnp.broadcast_to(peak, (rows, LANES))

    def pick(array, slab, base):
        begin, end = slab_heads(slab)
        out = array[(begin - base) * rows : (begin - base + 1) * rows, :]
        for h in range(begin + 1, end + 1):
            piece = array[(h - base) * rows : (h - base + 1) * rows, :]
            out = jnp.where(lane >= h * HD - slab * LANES, piece, out)
        return out

    def mix(half, slab, p_ref):
        cols = span(half * HALF + slab * LANES, LANES)
        begin, end = slab_heads(slab)
        value = jnp.concatenate([v_ref[:, cols], ones], axis=1)
        mixed = jnp.dot(
            p_ref[begin * rows : (end + 1) * rows, :], value, preferred_element_type=F32
        )
        return cols, pick(mixed[:, :LANES], slab, begin), pick(mixed[:, LANES:], slab, begin)

    def add(half, slab, p_ref):
        cols, top, total = mix(half, slab, p_ref)
        if not first:
            top = top + old_refs[0][:, cols]
            total = total + old_refs[1][:, cols]
        if last:
            outs[0][:, cols] = (top / total).astype(BF16)
        else:
            outs[0][:, cols] = top
            outs[1][:, cols] = total
            if not first:
                outs[2][:, cols] = jnp.zeros_like(top)
        return total

    steps = [divmod(step, SLABS) for step in range(width // LANES)]
    largest = jnp.zeros((rows, LANES), F32)
    x = scores(*steps[0])
    carried = None
    for number, (half, slab) in enumerate(steps):
        ahead = scores(*steps[number + 1]) if number + 1 < len(steps) else None
        carried = weigh(half, slab, x, carried, p_refs[half % 2], first)
        if number:
            before = steps[number - 1]
            largest = jnp.maximum(largest, add(*before, p_refs[before[0] % 2]))
        x = ahead
    largest = jnp.maximum(largest, add(*steps[-1], p_refs[steps[-1][0] % 2]))
    if first:
        return
    fine = jnp.max(largest) < SAFE
    if len(old_refs) == 3:
        fine = fine & (jnp.max(old_refs[2][...]) == 0.0)

    @pl.when(jnp.logical_not(fine))
    def _():
        def careful(half, carry):
            left = None
            for slab in range(SLABS):
                left = weigh(half, slab, scores(half, slab), left, p_refs[0], True)
            for slab in range(SLABS):
                cols, top, total = mix(half, slab, p_refs[0])
                peak = pick(top_ref[...], slab, 0)
                old = old_refs[2][:, cols] if len(old_refs) == 3 else jnp.zeros_like(top)
                best = jnp.maximum(old, peak)
                share = jnp.exp2((peak - best) * FACTOR)
                old_share = jnp.exp2((old - best) * FACTOR)
                top = top * share + old_refs[0][:, cols] * old_share
                total = total * share + old_refs[1][:, cols] * old_share
                if last:
                    outs[0][:, cols] = (top / total).astype(BF16)
                else:
                    outs[0][:, cols] = top
                    outs[1][:, cols] = total
                    outs[2][:, cols] = best
            return carry

        lax.fori_loop(0, width // HALF, careful, 0)


def attend_part(first, last, w_qk, w_v, blocks, inputs):
    width = w_v.shape[0]
    rows = inputs[0].shape[0]
    keys = rows * len(blocks)
    state = shape(rows, width, dtype=F32)
    if first:
        outs = [shape(rows, width), shape(rows, H * LANES), state, state]
    elif last:
        outs = [shape(rows, width)]
    else:
        outs = [state] * 3
    operands = [w_qk, w_v, *blocks, *inputs]
    tall = SET * rows
    need = 4 * tall * keys + 4 * keys * width + 4 * tall * LANES
    return pl.pallas_call(
        lambda *refs: part_kernel(len(blocks), first, last, *refs),
        out_shape=outs,
        in_specs=[vmem()] * len(operands),
        out_specs=[vmem()] * len(outs),
        scratch_shapes=[
            pltpu.VMEM((keys, LANES), BF16),
            pltpu.VMEM((keys, width), BF16),
            pltpu.VMEM((keys, width), BF16),
            pltpu.VMEM((tall, keys), BF16),
            pltpu.VMEM((tall, keys), BF16),
            pltpu.VMEM((tall, LANES), F32),
        ],
        compiler_params=limit(need // MIB + 8),
        cost_estimate=pl.CostEstimate(flops=10**9, bytes_accessed=4_000_000, transcendentals=0),
        name="part",
    )(*operands)


def swap(array, axis, distance):
    return lax.ppermute(array, axis, [(i, i ^ distance) for i in range(lax.axis_size(axis))])


def after(value, *others):
    return lax.optimization_barrier((value, others))[0]


def on_device(features, tiles, tile_src, tile_count, node_bucket, w_qk, w_v, bias_table):
    rows, width = features.shape
    groups = lax.axis_size("group")
    seq_count = lax.axis_size("seq")
    chips = seq_count // 2
    any_space = pl.BlockSpec(memory_space=pl.ANY)

    received = [swap(features, "group", d) for d in range(groups - 1, 0, -1)][::-1]
    own_bucket = node_bucket.reshape(1, rows)

    bias, own_features, masked, extra, source = pl.pallas_call(
        stage_kernel,
        out_shape=[
            shape(rows, H * LANES), shape(rows, width), shape(rows, TILES * rows),
            shape(EXTRA, width, dtype=F32),
            shape(TILES, LANES, dtype=jnp.int32),
        ],
        in_specs=[smem()] * 3 + [vmem(), vmem(), any_space, any_space],
        out_specs=[vmem()] * 5,
        scratch_shapes=[pltpu.VMEM((rows, TILES * rows), BF16), pltpu.SemaphoreType.DMA((2,))],
        compiler_params=limit(8),
        cost_estimate=pl.CostEstimate(flops=10**9, bytes_accessed=4_000_000, transcendentals=0),
        name="stage",
    )(tile_count, lax.axis_index("group").reshape(1), tile_src, bias_table, own_bucket, features, tiles)

    own = pl.pallas_call(
        aggregate_kernel,
        out_shape=shape(rows + EXTRA, width),
        in_specs=[vmem()] * (3 + groups),
        out_specs=vmem(),
        scratch_shapes=[pltpu.VMEM((groups * rows, width), BF16)],
        compiler_params=limit(8),
        cost_estimate=pl.CostEstimate(flops=10**9, bytes_accessed=4_000_000, transcendentals=0),
        name="aggregate",
    )(source, extra, masked, own_features, *received)

    far = [own] + [None] * (chips - 1)
    top = 1
    while 2 * top < chips:
        top *= 2
    far[top] = swap(own, "seq", 2 * top)
    step = 1
    while step < top:
        far[step] = swap(own, "seq", 2 * step)
        step *= 2
    for d in range(3, chips):
        if far[d] is None:
            far[d] = swap(far[d & (d - 1)], "seq", 2 * (d & -d))
    parts = [[0], [1, top]] if top > 1 else [[0, 1]]
    parts += [[d] for d in range(2, chips) if d != top]
    queries, state = [], [bias]
    for number, part in enumerate(parts):
        blocks = [swap(after(own, *state), "seq", 1)] if number == 1 else []
        for d in part:
            block = far[d]
            if d:
                block = after(block, *state)
                blocks += [block, swap(block, "seq", 1)]
            else:
                blocks.append(block)
        state = attend_part(
            number == 0, number == len(parts) - 1, w_qk, w_v, blocks, [*queries, *state]
        )
        if number == 0:
            queries, state = state[:2], state[2:]
    return state[0]


def solution(mesh):
    in_specs = (
        P(("group", "seq"), None),
        P(("group", "seq"), None),
        P(("group", "seq"), None),
        P(("group", "seq")),
        P(("group", "seq")),
        P(),
        P(),
        P(),
    )
    out_specs = P(("group", "seq"), None)
    return jax.shard_map(
        on_device, mesh=mesh, in_specs=in_specs, out_specs=out_specs, check_vma=False
    )
```

```python
import math

import jax
import jax.numpy as jnp
from jax import lax
from jax.experimental import pallas as pl
from jax.experimental.pallas import tpu as pltpu
from jax.sharding import PartitionSpec as P

H = 32
HD = 24
NB = 16
TILES = 8
LANES = 128
SET = 16
HALF = SET * HD
SLABS = HALF // LANES
SAFE = 1e30
EXTRA = 8
SHIFT = 3 * NB
NT = (((1,), (1,)), ((), ()))
MIB = 1024 * 1024
BF16 = jnp.bfloat16
F32 = jnp.float32
FACTOR = math.log2(math.e) / math.sqrt(HD)


def vmem():
    return pl.BlockSpec(memory_space=pltpu.VMEM)


def smem():
    return pl.BlockSpec(memory_space=pltpu.SMEM)


def limit(mib):
    return pltpu.CompilerParams(vmem_limit_bytes=mib * MIB)


def shape(*dims, dtype=BF16):
    return jax.ShapeDtypeStruct(dims, dtype)


def one_hot_slab(bucket_row):
    n = bucket_row.shape[1]
    index = lax.broadcasted_iota(jnp.int32, (LANES, n), 0)
    wanted = jnp.where(index < 3 * NB, index % NB, -1).astype(F32)
    hot = jnp.where((wanted == bucket_row) | ((index >= SHIFT) & (index < SHIFT + 3)), 1.0, 0.0)
    return hot.T.astype(BF16)


def split_three(x):
    high = x.astype(BF16).astype(F32)
    mid = (x - high).astype(BF16).astype(F32)
    return high, mid, x - high - mid


def stage_kernel(
    count_ref, me_ref, src_ref, table_ref, bucket_ref, features_ref, tiles_ref,
    bias_ref, own_ref, masked_ref, extra_ref, from_ref, tiles_held, sems,
):
    rows = own_ref.shape[0]
    copies = [
        pltpu.make_async_copy(tiles_ref, tiles_held, sems.at[0]),
        pltpu.make_async_copy(features_ref, own_ref, sems.at[1]),
    ]
    for copy in copies:
        copy.start()
    for t in range(TILES):
        from_ref[t : t + 1, :] = jnp.full((1, LANES), src_ref[0, t] ^ me_ref[0], jnp.int32)
    width = own_ref.shape[1]
    extra = jnp.concatenate(
        [bucket_ref[...].astype(F32), jnp.zeros((1, width - rows), F32)], axis=1
    )
    extra_ref[...] = jnp.broadcast_to(extra, (EXTRA, width))
    table = table_ref[...] * math.sqrt(HD)
    at = lax.broadcasted_iota(jnp.int32, (NB, NB * NB), 1) // NB
    mine = at == lax.broadcasted_iota(jnp.int32, (NB, NB * NB), 0)
    key = lax.broadcasted_iota(jnp.int32, (NB * NB, LANES), 0) % NB
    column = lax.broadcasted_iota(jnp.int32, (NB * NB, LANES), 1)
    cube = jnp.zeros((H * NB, LANES), F32)
    for number, piece in enumerate(split_three(table)):
        spread = [jnp.where(mine, piece[h : h + 1, :], 0.0) for h in range(H)]
        place = jnp.where(column == key + number * NB, 1.0, 0.0).astype(BF16)
        cube = cube + jnp.dot(
            jnp.concatenate(spread, axis=0).astype(BF16), place, preferred_element_type=F32
        )
    cube = cube.astype(BF16)
    hot = one_hot_slab(bucket_ref[...].astype(F32))[:, :NB]
    for h in range(H):
        bias_ref[:, h * LANES : (h + 1) * LANES] = jnp.dot(
            hot, cube[h * NB : (h + 1) * NB, :], preferred_element_type=F32
        ).astype(BF16)
    for copy in copies:
        copy.wait()
    for t in range(TILES):
        tile = tiles_held[:, t * rows : (t + 1) * rows]
        masked_ref[:, t * rows : (t + 1) * rows] = jnp.where(
            t < count_ref[0], tile, jnp.zeros_like(tile)
        )


def aggregate_kernel(from_ref, extra_ref, masked_ref, *refs):
    feature_refs, out_ref, short_ref, held = refs[:-3], refs[-3], refs[-2], refs[-1]
    rows = feature_refs[0].shape[0]
    for d, ref in enumerate(feature_refs):
        held[d * rows : (d + 1) * rows, :] = ref[...]
    picked = []
    for t in range(TILES):
        start = pl.multiple_of(from_ref[t, 0] * rows, rows)
        picked.append(held[pl.ds(start, rows), :])
    total = feature_refs[0][...].astype(F32) + jnp.dot(
        masked_ref[...], jnp.concatenate(picked, axis=0), preferred_element_type=F32
    )
    mean_square = jnp.mean(total * total, axis=-1, keepdims=True)
    result = jnp.concatenate(
        [total * lax.rsqrt(mean_square + 1e-06), extra_ref[...]], axis=0
    ).astype(BF16)
    out_ref[...] = result
    short_ref[...] = result[: short_ref.shape[0], :]


def slab_heads(slab):
    return slab * LANES // HD, ((slab + 1) * LANES - 1) // HD


def part_kernel(count, first, last, w_qk_ref, w_v_ref, *refs):
    block_refs, refs = refs[:count], refs[count:]
    hot_ref, k_ref, v_ref, p_refs, *refs_back = *refs[-6:-3], refs[-3:-1], refs[-1]
    top_ref = refs_back[0]
    refs = refs[:-6]
    if last:
        *refs, held_ref, sems = refs
    if first:
        bias_ref, q_ref, shifted_ref, *outs = refs
    else:
        q_ref, bias_ref, *refs = refs
        old_refs, outs = (refs[:2], refs[2:]) if len(refs) in (3, 5) else (refs[:3], refs[3:])
    rows = q_ref.shape[0]
    keys = hot_ref.shape[0]
    width = w_v_ref.shape[0]
    arrived = [ref[...] for ref in block_refs]
    for s, item in enumerate(arrived):
        bucket = item[rows:, :rows].astype(F32)[:1, :]
        hot_ref[s * rows : (s + 1) * rows, :] = one_hot_slab(bucket)
    block = jnp.concatenate([item[:rows, :] for item in arrived], axis=0)
    if first:
        for n in range(0, width, 256):
            q_ref[:, n : n + 256] = jnp.dot(
                block[:rows, :], w_qk_ref[:, n : n + 256], preferred_element_type=F32
            ).astype(BF16)
    for n in range(0, width, 256):
        k_ref[:, n : n + 256] = jnp.dot(
            block, w_qk_ref[:, width + n : width + n + 256], preferred_element_type=F32
        ).astype(BF16)
        v_ref[:, n : n + 256] = jnp.dot(
            block, w_v_ref[:, n : n + 256], preferred_element_type=F32
        ).astype(BF16)

    lane = lax.broadcasted_iota(jnp.int32, (rows, LANES), 1)
    ones = jnp.ones((keys, LANES), BF16)

    def span(start, size):
        return pl.ds(start if isinstance(start, int) else pl.multiple_of(start, LANES), size)

    def scores(half, slab):
        cols = span(half * HALF + slab * LANES, LANES)
        begin, end = slab_heads(slab)
        q = q_ref[:, cols]
        zero = jnp.zeros_like(q)
        lefts, rights = [], []
        for h in range(begin, end + 1):
            inside = (lane >= h * HD - slab * LANES) & (lane < (h + 1) * HD - slab * LANES)
            lefts.append(jnp.where(inside, q, zero))
            if h * HD >= slab * LANES:
                rights.append(bias_ref[:, span((half * SET + h) * LANES, LANES)])
            else:
                rights.append(zero)
        query = jnp.concatenate(
            [jnp.concatenate(lefts, axis=0), jnp.concatenate(rights, axis=0)], axis=1
        )
        key = jnp.concatenate([k_ref[:, cols], hot_ref[...]], axis=1)
        return lax.dot_general(query, key, NT, preferred_element_type=F32)

    def weigh(half, slab, x, carried, p_ref, local):
        begin, end = slab_heads(slab)
        for h in range(begin, end + 1):
            own = x[(h - begin) * rows : (h - begin + 1) * rows, :]
            if h * HD < slab * LANES:
                own = own + carried
            if (h + 1) * HD > (slab + 1) * LANES:
                return own
            if local:
                peak = jnp.max(own, axis=-1, keepdims=True)
                own = own - peak
                keep_peak(half, h, peak)
            p_ref[h * rows : (h + 1) * rows, :] = jnp.exp2(own * FACTOR).astype(BF16)
        return None

    def keep_peak(half, h, peak):
        if first:
            at = span((half * SET + h) * LANES, LANES)
            mark = jnp.zeros((rows, LANES), F32)
            for number, piece in enumerate(split_three(-peak)):
                mark = jnp.where(lane == SHIFT + number, piece, mark)
            shifted_ref[:, at] = bias_ref[:, at] + mark.astype(BF16)
        else:
            top_ref[h * rows : (h + 1) * rows, :] = jnp.broadcast_to(peak, (rows, LANES))

    def pick(array, slab, base):
        begin, end = slab_heads(slab)
        out = array[(begin - base) * rows : (begin - base + 1) * rows, :]
        for h in range(begin + 1, end + 1):
            piece = array[(h - base) * rows : (h - base + 1) * rows, :]
            out = jnp.where(lane >= h * HD - slab * LANES, piece, out)
        return out

    def mix(half, slab, p_ref):
        cols = span(half * HALF + slab * LANES, LANES)
        begin, end = slab_heads(slab)
        value = jnp.concatenate([v_ref[:, cols], ones], axis=1)
        mixed = jnp.dot(
            p_ref[begin * rows : (end + 1) * rows, :], value, preferred_element_type=F32
        )
        return cols, pick(mixed[:, :LANES], slab, begin), pick(mixed[:, LANES:], slab, begin)

    def add(half, slab, p_ref):
        cols, top, total = mix(half, slab, p_ref)
        if not first:
            top = top + old_refs[0][:, cols]
            total = total + old_refs[1][:, cols]
        if last:
            held_ref[:, cols] = (top / total).astype(BF16)
            send(half * SLABS + slab).start()
        else:
            outs[0][:, cols] = top
            outs[1][:, cols] = total
            if not first:
                outs[2][:, cols] = jnp.zeros_like(top)
        return total

    def send(step):
        cols = pl.ds(step * LANES, LANES)
        return pltpu.make_async_copy(held_ref.at[:, cols], outs[0].at[:, cols], sems.at[step])

    steps = [divmod(step, SLABS) for step in range(width // LANES)]
    largest = jnp.zeros((rows, LANES), F32)
    x = scores(*steps[0])
    carried = None
    for number, (half, slab) in enumerate(steps):
        ahead = scores(*steps[number + 1]) if number + 1 < len(steps) else None
        carried = weigh(half, slab, x, carried, p_refs[half % 2], first)
        if number:
            before = steps[number - 1]
            largest = jnp.maximum(largest, add(*before, p_refs[before[0] % 2]))
        x = ahead
    largest = jnp.maximum(largest, add(*steps[-1], p_refs[steps[-1][0] % 2]))
    if last:
        for step in range(len(steps)):
            send(step).wait()
    if first:
        return
    fine = jnp.max(largest) < SAFE
    if len(old_refs) == 3:
        fine = fine & (jnp.max(old_refs[2][...]) == 0.0)

    @pl.when(jnp.logical_not(fine))
    def _():
        def careful(half, carry):
            left = None
            for slab in range(SLABS):
                left = weigh(half, slab, scores(half, slab), left, p_refs[0], True)
            for slab in range(SLABS):
                cols, top, total = mix(half, slab, p_refs[0])
                peak = pick(top_ref[...], slab, 0)
                old = old_refs[2][:, cols] if len(old_refs) == 3 else jnp.zeros_like(top)
                best = jnp.maximum(old, peak)
                share = jnp.exp2((peak - best) * FACTOR)
                old_share = jnp.exp2((old - best) * FACTOR)
                top = top * share + old_refs[0][:, cols] * old_share
                total = total * share + old_refs[1][:, cols] * old_share
                if last:
                    held_ref[:, cols] = (top / total).astype(BF16)
                else:
                    outs[0][:, cols] = top
                    outs[1][:, cols] = total
                    outs[2][:, cols] = best
            return carry

        lax.fori_loop(0, width // HALF, careful, 0)
        if last:
            for step in range(len(steps)):
                send(step).start()
            for step in range(len(steps)):
                send(step).wait()


def attend_part(first, last, w_qk, w_v, blocks, inputs):
    width = w_v.shape[0]
    rows = inputs[0].shape[0]
    keys = rows * len(blocks)
    state = shape(rows, width, dtype=F32)
    if first:
        outs = [shape(rows, width), shape(rows, H * LANES), state, state]
    elif last:
        outs = [shape(rows, width)]
    else:
        outs = [state] * 3
    operands = [w_qk, w_v, *blocks, *inputs]
    tall = SET * rows
    need = 4 * tall * keys + 4 * keys * width + 4 * tall * LANES
    return pl.pallas_call(
        lambda *refs: part_kernel(len(blocks), first, last, *refs),
        out_shape=outs,
        in_specs=[vmem()] * len(operands),
        out_specs=[pl.BlockSpec(memory_space=pl.ANY) if last else vmem()] * len(outs),
        scratch_shapes=(
            [pltpu.VMEM((rows, width), BF16), pltpu.SemaphoreType.DMA((width // LANES,))] if last else []
        )
        + [
            pltpu.VMEM((keys, LANES), BF16),
            pltpu.VMEM((keys, width), BF16),
            pltpu.VMEM((keys, width), BF16),
            pltpu.VMEM((tall, keys), BF16),
            pltpu.VMEM((tall, keys), BF16),
            pltpu.VMEM((tall, LANES), F32),
        ],
        compiler_params=limit(need // MIB + 8),
        cost_estimate=pl.CostEstimate(
            flops=1000 if not last else 10**9, bytes_accessed=1000 if not last else 4_000_000, transcendentals=0
        ),
        name="part",
    )(*operands)


def swap(array, axis, distance):
    return lax.ppermute(array, axis, [(i, i ^ distance) for i in range(lax.axis_size(axis))])


def after(value, *others):
    return lax.optimization_barrier((value, others))[0]


def on_device(features, tiles, tile_src, tile_count, node_bucket, w_qk, w_v, bias_table):
    rows, width = features.shape
    groups = lax.axis_size("group")
    seq_count = lax.axis_size("seq")
    chips = seq_count // 2
    any_space = pl.BlockSpec(memory_space=pl.ANY)

    received = [swap(features, "group", d) for d in range(groups - 1, 0, -1)][::-1]
    own_bucket = node_bucket.reshape(1, rows)

    bias, own_features, masked, extra, source = pl.pallas_call(
        stage_kernel,
        out_shape=[
            shape(rows, H * LANES), shape(rows, width), shape(rows, TILES * rows),
            shape(EXTRA, width, dtype=F32),
            shape(TILES, LANES, dtype=jnp.int32),
        ],
        in_specs=[smem()] * 3 + [vmem(), vmem(), any_space, any_space],
        out_specs=[vmem()] * 5,
        scratch_shapes=[pltpu.VMEM((rows, TILES * rows), BF16), pltpu.SemaphoreType.DMA((2,))],
        compiler_params=limit(8),
        cost_estimate=pl.CostEstimate(flops=10**9, bytes_accessed=4_000_000, transcendentals=0),
        name="stage",
    )(tile_count, lax.axis_index("group").reshape(1), tile_src, bias_table, own_bucket, features, tiles)

    own, short = pl.pallas_call(
        aggregate_kernel,
        out_shape=[shape(rows + EXTRA, width), shape(rows + EXTRA // 2, width)],
        in_specs=[vmem()] * (3 + groups),
        out_specs=[vmem()] * 2,
        scratch_shapes=[pltpu.VMEM((groups * rows, width), BF16)],
        compiler_params=limit(8),
        cost_estimate=pl.CostEstimate(flops=10**9, bytes_accessed=4_000_000, transcendentals=0),
        name="aggregate",
    )(source, extra, masked, own_features, *received)

    far = [short] + [None] * (chips - 1)
    top = 1
    while 2 * top < chips:
        top *= 2
    far[top] = swap(own, "seq", 2 * top)
    step = 1
    while step < top:
        far[step] = swap(short, "seq", 2 * step)
        step *= 2
    for d in range(3, chips):
        if far[d] is None:
            far[d] = swap(far[d & (d - 1)], "seq", 2 * (d & -d))
    parts = [[0], [1, top]] if top > 1 else [[0, 1]]
    parts += [[d] for d in range(2, chips) if d != top]
    queries, state = [], [bias]
    for number, part in enumerate(parts):
        blocks = []
        for d in part:
            block = far[d]
            if d:
                block = after(block, *state)
                near = swap(block, "seq", 1)
            else:
                near = swap(short, "seq", 1)
            blocks += [block, near]
        state = attend_part(
            number == 0, number == len(parts) - 1, w_qk, w_v, blocks, [*queries, *state]
        )
        if number == 0:
            queries, state = state[:2], state[2:]
    return state[0]


def solution(mesh):
    in_specs = (
        P(("group", "seq"), None),
        P(("group", "seq"), None),
        P(("group", "seq"), None),
        P(("group", "seq")),
        P(("group", "seq")),
        P(),
        P(),
        P(),
    )
    out_specs = P(("group", "seq"), None)
    return jax.shard_map(
        on_device, mesh=mesh, in_specs=in_specs, out_specs=out_specs, check_vma=False
    )
```

```python
import math

import jax
import jax.numpy as jnp
from jax import lax
from jax.experimental import pallas as pl
from jax.experimental.pallas import tpu as pltpu
from jax.sharding import PartitionSpec as P

H = 32
HD = 24
NB = 16
TILES = 8
LANES = 128
SET = 16
HALF = SET * HD
SLABS = HALF // LANES
SAFE = 1e30
EXTRA = 8
SHIFT = 3 * NB
NT = (((1,), (1,)), ((), ()))
MIB = 1024 * 1024
BF16 = jnp.bfloat16
F32 = jnp.float32
FACTOR = math.log2(math.e) / math.sqrt(HD)


def vmem():
    return pl.BlockSpec(memory_space=pltpu.VMEM)


def smem():
    return pl.BlockSpec(memory_space=pltpu.SMEM)


def limit(mib):
    return pltpu.CompilerParams(vmem_limit_bytes=mib * MIB)


def shape(*dims, dtype=BF16):
    return jax.ShapeDtypeStruct(dims, dtype)


def one_hot_slab(bucket_row):
    n = bucket_row.shape[1]
    index = lax.broadcasted_iota(jnp.int32, (LANES, n), 0)
    wanted = jnp.where(index < 3 * NB, index % NB, -1).astype(F32)
    hot = jnp.where((wanted == bucket_row) | ((index >= SHIFT) & (index < SHIFT + 3)), 1.0, 0.0)
    return hot.T.astype(BF16)


def split_three(x):
    high = x.astype(BF16).astype(F32)
    mid = (x - high).astype(BF16).astype(F32)
    return high, mid, x - high - mid


def stage_kernel(
    count_ref, me_ref, src_ref, table_ref, bucket_ref, features_ref, tiles_ref,
    bias_ref, own_ref, masked_ref, extra_ref, from_ref, tiles_held, sems,
):
    rows = own_ref.shape[0]
    copies = [
        pltpu.make_async_copy(tiles_ref, tiles_held, sems.at[0]),
        pltpu.make_async_copy(features_ref, own_ref, sems.at[1]),
    ]
    for copy in copies:
        copy.start()
    for t in range(TILES):
        from_ref[t : t + 1, :] = jnp.full((1, LANES), src_ref[0, t] ^ me_ref[0], jnp.int32)
    width = own_ref.shape[1]
    extra = jnp.concatenate(
        [bucket_ref[...].astype(F32), jnp.zeros((1, width - rows), F32)], axis=1
    )
    extra_ref[...] = jnp.broadcast_to(extra, (EXTRA, width))
    table = table_ref[...] * math.sqrt(HD)
    at = lax.broadcasted_iota(jnp.int32, (NB, NB * NB), 1) // NB
    mine = at == lax.broadcasted_iota(jnp.int32, (NB, NB * NB), 0)
    key = lax.broadcasted_iota(jnp.int32, (NB * NB, LANES), 0) % NB
    column = lax.broadcasted_iota(jnp.int32, (NB * NB, LANES), 1)
    cube = jnp.zeros((H * NB, LANES), F32)
    for number, piece in enumerate(split_three(table)):
        spread = [jnp.where(mine, piece[h : h + 1, :], 0.0) for h in range(H)]
        place = jnp.where(column == key + number * NB, 1.0, 0.0).astype(BF16)
        cube = cube + jnp.dot(
            jnp.concatenate(spread, axis=0).astype(BF16), place, preferred_element_type=F32
        )
    cube = cube.astype(BF16)
    hot = one_hot_slab(bucket_ref[...].astype(F32))[:, :NB]
    for h in range(H):
        bias_ref[:, h * LANES : (h + 1) * LANES] = jnp.dot(
            hot, cube[h * NB : (h + 1) * NB, :], preferred_element_type=F32
        ).astype(BF16)
    for copy in copies:
        copy.wait()
    for t in range(TILES):
        tile = tiles_held[:, t * rows : (t + 1) * rows]
        masked_ref[:, t * rows : (t + 1) * rows] = jnp.where(
            t < count_ref[0], tile, jnp.zeros_like(tile)
        )


def aggregate_kernel(from_ref, extra_ref, masked_ref, *refs):
    feature_refs, out_ref, short_ref, held = refs[:-3], refs[-3], refs[-2], refs[-1]
    rows = feature_refs[0].shape[0]
    for d, ref in enumerate(feature_refs):
        held[d * rows : (d + 1) * rows, :] = ref[...]
    picked = []
    for t in range(TILES):
        start = pl.multiple_of(from_ref[t, 0] * rows, rows)
        picked.append(held[pl.ds(start, rows), :])
    total = feature_refs[0][...].astype(F32) + jnp.dot(
        masked_ref[...], jnp.concatenate(picked, axis=0), preferred_element_type=F32
    )
    mean_square = jnp.mean(total * total, axis=-1, keepdims=True)
    result = jnp.concatenate(
        [total * lax.rsqrt(mean_square + 1e-06), extra_ref[...]], axis=0
    ).astype(BF16)
    out_ref[...] = result
    short_ref[...] = result[: short_ref.shape[0], :]


def slab_heads(slab):
    return slab * LANES // HD, ((slab + 1) * LANES - 1) // HD


def project_blocks(block_refs, rows, w_qk_ref, w_v_ref, hot_ref, k_ref, v_ref):
    width = w_v_ref.shape[0]
    arrived = [ref[...] for ref in block_refs]
    for s, item in enumerate(arrived):
        bucket = item[rows:, :rows].astype(F32)[:1, :]
        hot_ref[s * rows : (s + 1) * rows, :] = one_hot_slab(bucket)
    block = jnp.concatenate([item[:rows, :] for item in arrived], axis=0)
    for n in range(0, width, 256):
        k_ref[:, n : n + 256] = jnp.dot(
            block, w_qk_ref[:, width + n : width + n + 256], preferred_element_type=F32
        ).astype(BF16)
        v_ref[:, n : n + 256] = jnp.dot(
            block, w_v_ref[:, n : n + 256], preferred_element_type=F32
        ).astype(BF16)
    return block


def project_kernel(w_qk_ref, w_v_ref, *refs):
    *block_refs, hot_ref, k_ref, v_ref = refs
    rows = hot_ref.shape[0] // len(block_refs)
    project_blocks(block_refs, rows, w_qk_ref, w_v_ref, hot_ref, k_ref, v_ref)


def part_kernel(count, first, last, w_qk_ref, w_v_ref, *refs):
    block_refs, refs = refs[:count], refs[count:]
    hot_refs, k_refs, v_refs = ([ref] for ref in refs[-6:-3])
    p_refs, top_ref = refs[-3:-1], refs[-1]
    refs = refs[:-6]
    if first:
        bias_ref, q_ref, shifted_ref, *outs = refs
    else:
        ready, (q_ref, bias_ref, *refs) = refs[:3], refs[3:]
        old_refs, outs = (refs[:2], refs[2:]) if len(refs) in (3, 5) else (refs[:3], refs[3:])
    rows = q_ref.shape[0]
    width = w_v_ref.shape[0]
    block = project_blocks(
        block_refs, rows, w_qk_ref, w_v_ref, hot_refs[0], k_refs[0], v_refs[0]
    )
    if first:
        for n in range(0, width, 256):
            q_ref[:, n : n + 256] = jnp.dot(
                block[:rows, :], w_qk_ref[:, n : n + 256], preferred_element_type=F32
            ).astype(BF16)
    else:
        for some, ref in zip((hot_refs, k_refs, v_refs), ready):
            some.insert(0, ref)
    keys = sum(ref.shape[0] for ref in hot_refs)

    def every(some, cols=slice(None)):
        return jnp.concatenate([ref[:, cols] for ref in some], axis=0)

    lane = lax.broadcasted_iota(jnp.int32, (rows, LANES), 1)
    ones = jnp.ones((keys, LANES), BF16)

    def span(start, size):
        return pl.ds(start if isinstance(start, int) else pl.multiple_of(start, LANES), size)

    def scores(half, slab):
        cols = span(half * HALF + slab * LANES, LANES)
        begin, end = slab_heads(slab)
        q = q_ref[:, cols]
        zero = jnp.zeros_like(q)
        lefts, rights = [], []
        for h in range(begin, end + 1):
            inside = (lane >= h * HD - slab * LANES) & (lane < (h + 1) * HD - slab * LANES)
            lefts.append(jnp.where(inside, q, zero))
            if h * HD >= slab * LANES:
                rights.append(bias_ref[:, span((half * SET + h) * LANES, LANES)])
            else:
                rights.append(zero)
        query = jnp.concatenate(
            [jnp.concatenate(lefts, axis=0), jnp.concatenate(rights, axis=0)], axis=1
        )
        key = jnp.concatenate([every(k_refs, cols), every(hot_refs)], axis=1)
        return lax.dot_general(query, key, NT, preferred_element_type=F32)

    def weigh(half, slab, x, carried, p_ref, local):
        begin, end = slab_heads(slab)
        for h in range(begin, end + 1):
            own = x[(h - begin) * rows : (h - begin + 1) * rows, :]
            if h * HD < slab * LANES:
                own = own + carried
            if (h + 1) * HD > (slab + 1) * LANES:
                return own
            if local:
                peak = jnp.max(own, axis=-1, keepdims=True)
                own = own - peak
                keep_peak(half, h, peak)
            p_ref[h * rows : (h + 1) * rows, :] = jnp.exp2(own * FACTOR).astype(BF16)
        return None

    def keep_peak(half, h, peak):
        if first:
            at = span((half * SET + h) * LANES, LANES)
            mark = jnp.zeros((rows, LANES), F32)
            for number, piece in enumerate(split_three(-peak)):
                mark = jnp.where(lane == SHIFT + number, piece, mark)
            shifted_ref[:, at] = bias_ref[:, at] + mark.astype(BF16)
        else:
            top_ref[h * rows : (h + 1) * rows, :] = jnp.broadcast_to(peak, (rows, LANES))

    def pick(array, slab, base):
        begin, end = slab_heads(slab)
        out = array[(begin - base) * rows : (begin - base + 1) * rows, :]
        for h in range(begin + 1, end + 1):
            piece = array[(h - base) * rows : (h - base + 1) * rows, :]
            out = jnp.where(lane >= h * HD - slab * LANES, piece, out)
        return out

    def mix(half, slab, p_ref):
        cols = span(half * HALF + slab * LANES, LANES)
        begin, end = slab_heads(slab)
        value = jnp.concatenate([every(v_refs, cols), ones], axis=1)
        mixed = jnp.dot(
            p_ref[begin * rows : (end + 1) * rows, :], value, preferred_element_type=F32
        )
        return cols, pick(mixed[:, :LANES], slab, begin), pick(mixed[:, LANES:], slab, begin)

    def add(half, slab, p_ref):
        cols, top, total = mix(half, slab, p_ref)
        if not first:
            top = top + old_refs[0][:, cols]
            total = total + old_refs[1][:, cols]
        if last:
            outs[0][:, cols] = (top / total).astype(BF16)
        else:
            outs[0][:, cols] = top
            outs[1][:, cols] = total
            if not first:
                outs[2][:, cols] = jnp.zeros_like(top)
        return total

    steps = [divmod(step, SLABS) for step in range(width // LANES)]
    largest = jnp.zeros((rows, LANES), F32)
    x = scores(*steps[0])
    carried = None
    for number, (half, slab) in enumerate(steps):
        ahead = scores(*steps[number + 1]) if number + 1 < len(steps) else None
        carried = weigh(half, slab, x, carried, p_refs[half % 2], first)
        if number:
            before = steps[number - 1]
            largest = jnp.maximum(largest, add(*before, p_refs[before[0] % 2]))
        x = ahead
    largest = jnp.maximum(largest, add(*steps[-1], p_refs[steps[-1][0] % 2]))
    if first:
        return
    fine = jnp.max(largest) < SAFE
    if len(old_refs) == 3:
        fine = fine & (jnp.max(old_refs[2][...]) == 0.0)

    @pl.when(jnp.logical_not(fine))
    def _():
        def careful(half, carry):
            left = None
            for slab in range(SLABS):
                left = weigh(half, slab, scores(half, slab), left, p_refs[0], True)
            for slab in range(SLABS):
                cols, top, total = mix(half, slab, p_refs[0])
                peak = pick(top_ref[...], slab, 0)
                old = old_refs[2][:, cols] if len(old_refs) == 3 else jnp.zeros_like(top)
                best = jnp.maximum(old, peak)
                share = jnp.exp2((peak - best) * FACTOR)
                old_share = jnp.exp2((old - best) * FACTOR)
                top = top * share + old_refs[0][:, cols] * old_share
                total = total * share + old_refs[1][:, cols] * old_share
                if last:
                    outs[0][:, cols] = (top / total).astype(BF16)
                else:
                    outs[0][:, cols] = top
                    outs[1][:, cols] = total
                    outs[2][:, cols] = best
            return carry

        lax.fori_loop(0, width // HALF, careful, 0)


def attend_part(first, last, w_qk, w_v, blocks, inputs):
    width = w_v.shape[0]
    rows = inputs[0].shape[0]
    ready = []
    if not first:
        near, blocks = blocks[::2], blocks[1::2]
        count = rows * len(near)
        ready = pl.pallas_call(
            project_kernel,
            out_shape=[shape(count, LANES), shape(count, width), shape(count, width)],
            in_specs=[vmem()] * (2 + len(near)),
            out_specs=[vmem()] * 3,
            compiler_params=limit(8),
            cost_estimate=pl.CostEstimate(flops=1000, bytes_accessed=1000, transcendentals=0),
            name="project",
        )(w_qk, w_v, *near)
    count = rows * len(blocks)
    keys = count + sum(item.shape[0] for item in ready[:1])
    state = shape(rows, width, dtype=F32)
    if first:
        outs = [shape(rows, width), shape(rows, H * LANES), state, state]
    elif last:
        outs = [shape(rows, width)]
    else:
        outs = [state] * 3
    operands = [w_qk, w_v, *blocks, *ready, *inputs]
    tall = SET * rows
    need = 4 * tall * keys + 4 * keys * width + 4 * tall * LANES
    return pl.pallas_call(
        lambda *refs: part_kernel(len(blocks), first, last, *refs),
        out_shape=outs,
        in_specs=[vmem()] * len(operands),
        out_specs=[vmem()] * len(outs),
        scratch_shapes=[
            pltpu.VMEM((count, LANES), BF16),
            pltpu.VMEM((count, width), BF16),
            pltpu.VMEM((count, width), BF16),
            pltpu.VMEM((tall, keys), BF16),
            pltpu.VMEM((tall, keys), BF16),
            pltpu.VMEM((tall, LANES), F32),
        ],
        compiler_params=limit(need // MIB + 8),
        cost_estimate=pl.CostEstimate(
            flops=1000 if not last else 10**9, bytes_accessed=1000 if not last else 4_000_000, transcendentals=0
        ),
        name="part",
    )(*operands)


def swap(array, axis, distance):
    return lax.ppermute(array, axis, [(i, i ^ distance) for i in range(lax.axis_size(axis))])


def after(value, *others):
    return lax.optimization_barrier((value, others))[0]


def on_device(features, tiles, tile_src, tile_count, node_bucket, w_qk, w_v, bias_table):
    rows, width = features.shape
    groups = lax.axis_size("group")
    seq_count = lax.axis_size("seq")
    chips = seq_count // 2
    any_space = pl.BlockSpec(memory_space=pl.ANY)

    received = [swap(features, "group", d) for d in range(groups - 1, 0, -1)][::-1]
    own_bucket = node_bucket.reshape(1, rows)

    bias, own_features, masked, extra, source = pl.pallas_call(
        stage_kernel,
        out_shape=[
            shape(rows, H * LANES), shape(rows, width), shape(rows, TILES * rows),
            shape(EXTRA, width, dtype=F32),
            shape(TILES, LANES, dtype=jnp.int32),
        ],
        in_specs=[smem()] * 3 + [vmem(), vmem(), any_space, any_space],
        out_specs=[vmem()] * 5,
        scratch_shapes=[pltpu.VMEM((rows, TILES * rows), BF16), pltpu.SemaphoreType.DMA((2,))],
        compiler_params=limit(8),
        cost_estimate=pl.CostEstimate(flops=10**9, bytes_accessed=4_000_000, transcendentals=0),
        name="stage",
    )(tile_count, lax.axis_index("group").reshape(1), tile_src, bias_table, own_bucket, features, tiles)

    own, short = pl.pallas_call(
        aggregate_kernel,
        out_shape=[shape(rows + EXTRA, width), shape(rows + EXTRA // 2, width)],
        in_specs=[vmem()] * (3 + groups),
        out_specs=[vmem()] * 2,
        scratch_shapes=[pltpu.VMEM((groups * rows, width), BF16)],
        compiler_params=limit(8),
        cost_estimate=pl.CostEstimate(flops=10**9, bytes_accessed=4_000_000, transcendentals=0),
        name="aggregate",
    )(source, extra, masked, own_features, *received)

    far = [short] + [None] * (chips - 1)
    top = 1
    while 2 * top < chips:
        top *= 2
    far[top] = swap(own, "seq", 2 * top)
    step = 1
    while step < top:
        far[step] = swap(short, "seq", 2 * step)
        step *= 2
    for d in range(3, chips):
        if far[d] is None:
            far[d] = swap(far[d & (d - 1)], "seq", 2 * (d & -d))
    parts = [[0], [1, top]] if top > 1 else [[0, 1]]
    parts += [[d] for d in range(2, chips) if d != top]
    queries, state = [], [bias]
    for number, part in enumerate(parts):
        blocks = []
        for d in part:
            block = far[d]
            if d:
                block = after(block, *state)
                near = swap(block, "seq", 1)
            else:
                near = swap(short, "seq", 1)
            blocks += [block, near]
        state = attend_part(
            number == 0, number == len(parts) - 1, w_qk, w_v, blocks, [*queries, *state]
        )
        if number == 0:
            queries, state = state[:2], state[2:]
    return state[0]


def solution(mesh):
    in_specs = (
        P(("group", "seq"), None),
        P(("group", "seq"), None),
        P(("group", "seq"), None),
        P(("group", "seq")),
        P(("group", "seq")),
        P(),
        P(),
        P(),
    )
    out_specs = P(("group", "seq"), None)
    return jax.shard_map(
        on_device, mesh=mesh, in_specs=in_specs, out_specs=out_specs, check_vma=False
    )
```

```python
import math

import jax
import jax.numpy as jnp
from jax import lax
from jax.experimental import pallas as pl
from jax.experimental.pallas import tpu as pltpu
from jax.sharding import PartitionSpec as P

H = 32
HD = 24
NB = 16
TILES = 8
LANES = 128
SET = 16
HALF = SET * HD
SLABS = HALF // LANES
SAFE = 1e30
EXTRA = 8
SHIFT = 3 * NB
NT = (((1,), (1,)), ((), ()))
MIB = 1024 * 1024
BF16 = jnp.bfloat16
F32 = jnp.float32
FACTOR = math.log2(math.e) / math.sqrt(HD)


def vmem():
    return pl.BlockSpec(memory_space=pltpu.VMEM)


def smem():
    return pl.BlockSpec(memory_space=pltpu.SMEM)


def limit(mib):
    return pltpu.CompilerParams(vmem_limit_bytes=mib * MIB)


def shape(*dims, dtype=BF16):
    return jax.ShapeDtypeStruct(dims, dtype)


def one_hot_slab(bucket_row):
    n = bucket_row.shape[1]
    index = lax.broadcasted_iota(jnp.int32, (LANES, n), 0)
    wanted = jnp.where(index < 3 * NB, index % NB, -1).astype(F32)
    hot = jnp.where((wanted == bucket_row) | ((index >= SHIFT) & (index < SHIFT + 3)), 1.0, 0.0)
    return hot.T.astype(BF16)


def split_three(x):
    high = x.astype(BF16).astype(F32)
    mid = (x - high).astype(BF16).astype(F32)
    return high, mid, x - high - mid


def stage_kernel(
    count_ref, me_ref, src_ref, table_ref, bucket_ref, features_ref, tiles_ref,
    bias_ref, own_ref, masked_ref, extra_ref, from_ref, tiles_held, sems,
):
    rows = own_ref.shape[0]
    copies = [
        pltpu.make_async_copy(tiles_ref, tiles_held, sems.at[0]),
        pltpu.make_async_copy(features_ref, own_ref, sems.at[1]),
    ]
    for copy in copies:
        copy.start()
    for t in range(TILES):
        from_ref[t : t + 1, :] = jnp.full((1, LANES), src_ref[0, t] ^ me_ref[0], jnp.int32)
    width = own_ref.shape[1]
    extra = jnp.concatenate(
        [bucket_ref[...].astype(F32), jnp.zeros((1, width - rows), F32)], axis=1
    )
    extra_ref[...] = jnp.broadcast_to(extra, (EXTRA, width))
    table = table_ref[...] * math.sqrt(HD)
    at = lax.broadcasted_iota(jnp.int32, (NB, NB * NB), 1) // NB
    mine = at == lax.broadcasted_iota(jnp.int32, (NB, NB * NB), 0)
    key = lax.broadcasted_iota(jnp.int32, (NB * NB, LANES), 0) % NB
    column = lax.broadcasted_iota(jnp.int32, (NB * NB, LANES), 1)
    cube = jnp.zeros((H * NB, LANES), F32)
    for number, piece in enumerate(split_three(table)):
        spread = [jnp.where(mine, piece[h : h + 1, :], 0.0) for h in range(H)]
        place = jnp.where(column == key + number * NB, 1.0, 0.0).astype(BF16)
        cube = cube + jnp.dot(
            jnp.concatenate(spread, axis=0).astype(BF16), place, preferred_element_type=F32
        )
    cube = cube.astype(BF16)
    hot = one_hot_slab(bucket_ref[...].astype(F32))[:, :NB]
    for h in range(H):
        bias_ref[:, h * LANES : (h + 1) * LANES] = jnp.dot(
            hot, cube[h * NB : (h + 1) * NB, :], preferred_element_type=F32
        ).astype(BF16)
    for copy in copies:
        copy.wait()
    for t in range(TILES):
        tile = tiles_held[:, t * rows : (t + 1) * rows]
        masked_ref[:, t * rows : (t + 1) * rows] = jnp.where(
            t < count_ref[0], tile, jnp.zeros_like(tile)
        )


def aggregate_kernel(order, from_ref, extra_ref, masked_ref, *refs):
    feature_refs, out_ref, short_ref, held = refs[:-3], refs[-3], refs[-2], refs[-1]
    rows = feature_refs[0].shape[0]
    for d, ref in zip([0, *order], feature_refs):
        held[d * rows : (d + 1) * rows, :] = ref[...]
    picked = []
    for t in range(TILES):
        start = pl.multiple_of(from_ref[t, 0] * rows, rows)
        picked.append(held[pl.ds(start, rows), :])
    total = feature_refs[0][...].astype(F32) + jnp.dot(
        masked_ref[...], jnp.concatenate(picked, axis=0), preferred_element_type=F32
    )
    mean_square = jnp.mean(total * total, axis=-1, keepdims=True)
    result = jnp.concatenate(
        [total * lax.rsqrt(mean_square + 1e-06), extra_ref[...]], axis=0
    ).astype(BF16)
    out_ref[...] = result
    short_ref[...] = result[: short_ref.shape[0], :]


def slab_heads(slab):
    return slab * LANES // HD, ((slab + 1) * LANES - 1) // HD


def project_blocks(block_refs, rows, w_qk_ref, w_v_ref, hot_ref, k_ref, v_ref):
    width = w_v_ref.shape[0]
    arrived = [ref[...] for ref in block_refs]
    for s, item in enumerate(arrived):
        bucket = item[rows:, :rows].astype(F32)[:1, :]
        hot_ref[s * rows : (s + 1) * rows, :] = one_hot_slab(bucket)
    block = jnp.concatenate([item[:rows, :] for item in arrived], axis=0)
    for n in range(0, width, 256):
        k_ref[:, n : n + 256] = jnp.dot(
            block, w_qk_ref[:, width + n : width + n + 256], preferred_element_type=F32
        ).astype(BF16)
        v_ref[:, n : n + 256] = jnp.dot(
            block, w_v_ref[:, n : n + 256], preferred_element_type=F32
        ).astype(BF16)
    return block


def project_kernel(w_qk_ref, w_v_ref, *refs):
    *block_refs, hot_ref, k_ref, v_ref = refs
    rows = hot_ref.shape[0] // len(block_refs)
    project_blocks(block_refs, rows, w_qk_ref, w_v_ref, hot_ref, k_ref, v_ref)


def part_kernel(count, first, last, w_qk_ref, w_v_ref, *refs):
    block_refs, refs = refs[:count], refs[count:]
    hot_refs, k_refs, v_refs = ([ref] for ref in refs[-6:-3])
    p_refs, top_ref = refs[-3:-1], refs[-1]
    refs = refs[:-6]
    if first:
        bias_ref, q_ref, shifted_ref, *outs = refs
    else:
        ready, (q_ref, bias_ref, *refs) = refs[:3], refs[3:]
        old_refs, outs = (refs[:2], refs[2:]) if len(refs) in (3, 5) else (refs[:3], refs[3:])
    rows = q_ref.shape[0]
    width = w_v_ref.shape[0]
    block = project_blocks(
        block_refs, rows, w_qk_ref, w_v_ref, hot_refs[0], k_refs[0], v_refs[0]
    )
    if first:
        for n in range(0, width, 256):
            q_ref[:, n : n + 256] = jnp.dot(
                block[:rows, :], w_qk_ref[:, n : n + 256], preferred_element_type=F32
            ).astype(BF16)
    else:
        for some, ref in zip((hot_refs, k_refs, v_refs), ready):
            some.insert(0, ref)
    keys = sum(ref.shape[0] for ref in hot_refs)

    def every(some, cols=slice(None)):
        return jnp.concatenate([ref[:, cols] for ref in some], axis=0)

    lane = lax.broadcasted_iota(jnp.int32, (rows, LANES), 1)
    ones = jnp.ones((keys, LANES), BF16)

    def span(start, size):
        return pl.ds(start if isinstance(start, int) else pl.multiple_of(start, LANES), size)

    def scores(half, slab):
        cols = span(half * HALF + slab * LANES, LANES)
        begin, end = slab_heads(slab)
        q = q_ref[:, cols]
        zero = jnp.zeros_like(q)
        lefts, rights = [], []
        for h in range(begin, end + 1):
            inside = (lane >= h * HD - slab * LANES) & (lane < (h + 1) * HD - slab * LANES)
            lefts.append(jnp.where(inside, q, zero))
            if h * HD >= slab * LANES:
                rights.append(bias_ref[:, span((half * SET + h) * LANES, LANES)])
            else:
                rights.append(zero)
        query = jnp.concatenate(
            [jnp.concatenate(lefts, axis=0), jnp.concatenate(rights, axis=0)], axis=1
        )
        key = jnp.concatenate([every(k_refs, cols), every(hot_refs)], axis=1)
        return lax.dot_general(query, key, NT, preferred_element_type=F32)

    def weigh(half, slab, x, carried, p_ref, local):
        begin, end = slab_heads(slab)
        for h in range(begin, end + 1):
            own = x[(h - begin) * rows : (h - begin + 1) * rows, :]
            if h * HD < slab * LANES:
                own = own + carried
            if (h + 1) * HD > (slab + 1) * LANES:
                return own
            if local:
                peak = jnp.max(own, axis=-1, keepdims=True)
                own = own - peak
                keep_peak(half, h, peak)
            p_ref[h * rows : (h + 1) * rows, :] = jnp.exp2(own * FACTOR).astype(BF16)
        return None

    def keep_peak(half, h, peak):
        if first:
            at = span((half * SET + h) * LANES, LANES)
            mark = jnp.zeros((rows, LANES), F32)
            for number, piece in enumerate(split_three(-peak)):
                mark = jnp.where(lane == SHIFT + number, piece, mark)
            shifted_ref[:, at] = bias_ref[:, at] + mark.astype(BF16)
        else:
            top_ref[h * rows : (h + 1) * rows, :] = jnp.broadcast_to(peak, (rows, LANES))

    def pick(array, slab, base):
        begin, end = slab_heads(slab)
        out = array[(begin - base) * rows : (begin - base + 1) * rows, :]
        for h in range(begin + 1, end + 1):
            piece = array[(h - base) * rows : (h - base + 1) * rows, :]
            out = jnp.where(lane >= h * HD - slab * LANES, piece, out)
        return out

    def mix(half, slab, p_ref):
        cols = span(half * HALF + slab * LANES, LANES)
        begin, end = slab_heads(slab)
        value = jnp.concatenate([every(v_refs, cols), ones], axis=1)
        mixed = jnp.dot(
            p_ref[begin * rows : (end + 1) * rows, :], value, preferred_element_type=F32
        )
        return cols, pick(mixed[:, :LANES], slab, begin), pick(mixed[:, LANES:], slab, begin)

    def add(half, slab, p_ref):
        cols, top, total = mix(half, slab, p_ref)
        if not first:
            top = top + old_refs[0][:, cols]
            total = total + old_refs[1][:, cols]
        if last:
            outs[0][:, cols] = (top / total).astype(BF16)
        else:
            outs[0][:, cols] = top
            outs[1][:, cols] = total
            if not first:
                outs[2][:, cols] = jnp.zeros_like(top)
        return total

    steps = [divmod(step, SLABS) for step in range(width // LANES)]
    largest = jnp.zeros((rows, LANES), F32)
    x = scores(*steps[0])
    carried = None
    for number, (half, slab) in enumerate(steps):
        ahead = scores(*steps[number + 1]) if number + 1 < len(steps) else None
        carried = weigh(half, slab, x, carried, p_refs[half % 2], first)
        if number:
            before = steps[number - 1]
            largest = jnp.maximum(largest, add(*before, p_refs[before[0] % 2]))
        x = ahead
    largest = jnp.maximum(largest, add(*steps[-1], p_refs[steps[-1][0] % 2]))
    if first:
        return
    fine = jnp.max(largest) < SAFE
    if len(old_refs) == 3:
        fine = fine & (jnp.max(old_refs[2][...]) == 0.0)

    @pl.when(jnp.logical_not(fine))
    def _():
        def careful(half, carry):
            left = None
            for slab in range(SLABS):
                left = weigh(half, slab, scores(half, slab), left, p_refs[0], True)
            for slab in range(SLABS):
                cols, top, total = mix(half, slab, p_refs[0])
                peak = pick(top_ref[...], slab, 0)
                old = old_refs[2][:, cols] if len(old_refs) == 3 else jnp.zeros_like(top)
                best = jnp.maximum(old, peak)
                share = jnp.exp2((peak - best) * FACTOR)
                old_share = jnp.exp2((old - best) * FACTOR)
                top = top * share + old_refs[0][:, cols] * old_share
                total = total * share + old_refs[1][:, cols] * old_share
                if last:
                    outs[0][:, cols] = (top / total).astype(BF16)
                else:
                    outs[0][:, cols] = top
                    outs[1][:, cols] = total
                    outs[2][:, cols] = best
            return carry

        lax.fori_loop(0, width // HALF, careful, 0)


def attend_part(first, last, w_qk, w_v, blocks, inputs):
    width = w_v.shape[0]
    rows = inputs[0].shape[0]
    ready = []
    if not first:
        near, blocks = blocks[::2], blocks[1::2]
        count = rows * len(near)
        ready = pl.pallas_call(
            project_kernel,
            out_shape=[shape(count, LANES), shape(count, width), shape(count, width)],
            in_specs=[vmem()] * (2 + len(near)),
            out_specs=[vmem()] * 3,
            compiler_params=limit(8),
            cost_estimate=pl.CostEstimate(flops=1000, bytes_accessed=1000, transcendentals=0),
            name="project",
        )(w_qk, w_v, *near)
    count = rows * len(blocks)
    keys = count + sum(item.shape[0] for item in ready[:1])
    state = shape(rows, width, dtype=F32)
    if first:
        outs = [shape(rows, width), shape(rows, H * LANES), state, state]
    elif last:
        outs = [shape(rows, width)]
    else:
        outs = [state] * 3
    operands = [w_qk, w_v, *blocks, *ready, *inputs]
    tall = SET * rows
    need = 4 * tall * keys + 4 * keys * width + 4 * tall * LANES
    return pl.pallas_call(
        lambda *refs: part_kernel(len(blocks), first, last, *refs),
        out_shape=outs,
        in_specs=[vmem()] * len(operands),
        out_specs=[vmem()] * len(outs),
        scratch_shapes=[
            pltpu.VMEM((count, LANES), BF16),
            pltpu.VMEM((count, width), BF16),
            pltpu.VMEM((count, width), BF16),
            pltpu.VMEM((tall, keys), BF16),
            pltpu.VMEM((tall, keys), BF16),
            pltpu.VMEM((tall, LANES), F32),
        ],
        compiler_params=limit(need // MIB + 8),
        cost_estimate=pl.CostEstimate(
            flops=1000 if not last else 10**9, bytes_accessed=1000 if not last else 4_000_000, transcendentals=0
        ),
        name="part",
    )(*operands)


def swap(array, axis, distance):
    return lax.ppermute(array, axis, [(i, i ^ distance) for i in range(lax.axis_size(axis))])


def after(value, *others):
    return lax.optimization_barrier((value, others))[0]


def on_device(features, tiles, tile_src, tile_count, node_bucket, w_qk, w_v, bias_table):
    rows, width = features.shape
    groups = lax.axis_size("group")
    seq_count = lax.axis_size("seq")
    chips = seq_count // 2
    any_space = pl.BlockSpec(memory_space=pl.ANY)

    order = [1, *range(groups - 1, 1, -1)]
    received = [swap(features, "group", d) for d in order]
    own_bucket = node_bucket.reshape(1, rows)

    bias, own_features, masked, extra, source = pl.pallas_call(
        stage_kernel,
        out_shape=[
            shape(rows, H * LANES), shape(rows, width), shape(rows, TILES * rows),
            shape(EXTRA, width, dtype=F32),
            shape(TILES, LANES, dtype=jnp.int32),
        ],
        in_specs=[smem()] * 3 + [vmem(), vmem(), any_space, any_space],
        out_specs=[vmem()] * 5,
        scratch_shapes=[pltpu.VMEM((rows, TILES * rows), BF16), pltpu.SemaphoreType.DMA((2,))],
        compiler_params=limit(8),
        cost_estimate=pl.CostEstimate(flops=10**9, bytes_accessed=4_000_000, transcendentals=0),
        name="stage",
    )(tile_count, lax.axis_index("group").reshape(1), tile_src, bias_table, own_bucket, features, tiles)

    own, short = pl.pallas_call(
        lambda *refs: aggregate_kernel(order, *refs),
        out_shape=[shape(rows + EXTRA, width), shape(rows + EXTRA // 2, width)],
        in_specs=[vmem()] * (3 + groups),
        out_specs=[vmem()] * 2,
        scratch_shapes=[pltpu.VMEM((groups * rows, width), BF16)],
        compiler_params=limit(8),
        cost_estimate=pl.CostEstimate(flops=10**9, bytes_accessed=4_000_000, transcendentals=0),
        name="aggregate",
    )(source, extra, masked, own_features, *received)

    far = [short] + [None] * (chips - 1)
    top = 1
    while 2 * top < chips:
        top *= 2
    far[top] = swap(own, "seq", 2 * top)
    step = 1
    while step < top:
        far[step] = swap(short, "seq", 2 * step)
        step *= 2
    for d in range(3, chips):
        if far[d] is None:
            far[d] = swap(far[d & (d - 1)], "seq", 2 * (d & -d))
    parts = [[0], [1, top]] if top > 1 else [[0, 1]]
    parts += [[d] for d in range(2, chips) if d != top]
    queries, state = [], [bias]
    for number, part in enumerate(parts):
        blocks = []
        for d in part:
            block = far[d]
            if d:
                block = after(block, *state)
                near = swap(block, "seq", 1)
            else:
                near = swap(short, "seq", 1)
            blocks += [block, near]
        state = attend_part(
            number == 0, number == len(parts) - 1, w_qk, w_v, blocks, [*queries, *state]
        )
        if number == 0:
            queries, state = state[:2], state[2:]
    return state[0]


def solution(mesh):
    in_specs = (
        P(("group", "seq"), None),
        P(("group", "seq"), None),
        P(("group", "seq"), None),
        P(("group", "seq")),
        P(("group", "seq")),
        P(),
        P(),
        P(),
    )
    out_specs = P(("group", "seq"), None)
    return jax.shard_map(
        on_device, mesh=mesh, in_specs=in_specs, out_specs=out_specs, check_vma=False
    )
```

```python
import math

import jax
import jax.numpy as jnp
from jax import lax
from jax.experimental import pallas as pl
from jax.experimental.pallas import tpu as pltpu
from jax.sharding import PartitionSpec as P

H = 32
HD = 24
NB = 16
TILES = 8
LANES = 128
SET = 16
HALF = SET * HD
SLABS = HALF // LANES
SAFE = 1e30
EXTRA = 8
SHIFT = 3 * NB
NT = (((1,), (1,)), ((), ()))
MIB = 1024 * 1024
BF16 = jnp.bfloat16
F32 = jnp.float32
FACTOR = math.log2(math.e) / math.sqrt(HD)


def vmem():
    return pl.BlockSpec(memory_space=pltpu.VMEM)


def smem():
    return pl.BlockSpec(memory_space=pltpu.SMEM)


def limit(mib):
    return pltpu.CompilerParams(vmem_limit_bytes=mib * MIB)


def shape(*dims, dtype=BF16):
    return jax.ShapeDtypeStruct(dims, dtype)


def one_hot_slab(bucket_row):
    n = bucket_row.shape[1]
    index = lax.broadcasted_iota(jnp.int32, (LANES, n), 0)
    wanted = jnp.where(index < 3 * NB, index % NB, -1).astype(F32)
    hot = jnp.where((wanted == bucket_row) | ((index >= SHIFT) & (index < SHIFT + 3)), 1.0, 0.0)
    return hot.T.astype(BF16)


def split_three(x):
    high = x.astype(BF16).astype(F32)
    mid = (x - high).astype(BF16).astype(F32)
    return high, mid, x - high - mid


def stage_kernel(
    count_ref, me_ref, src_ref, table_ref, bucket_ref, features_ref, tiles_ref,
    bias_ref, own_ref, masked_ref, extra_ref, from_ref, tiles_held, sems,
):
    rows = own_ref.shape[0]
    copies = [
        pltpu.make_async_copy(tiles_ref, tiles_held, sems.at[0]),
        pltpu.make_async_copy(features_ref, own_ref, sems.at[1]),
    ]
    for copy in copies:
        copy.start()
    for t in range(TILES):
        from_ref[t : t + 1, :] = jnp.full((1, LANES), src_ref[0, t] ^ me_ref[0], jnp.int32)
    width = own_ref.shape[1]
    extra = jnp.concatenate(
        [bucket_ref[...].astype(F32), jnp.zeros((1, width - rows), F32)], axis=1
    )
    extra_ref[...] = jnp.broadcast_to(extra, (EXTRA, width))
    table = table_ref[...] * math.sqrt(HD)
    at = lax.broadcasted_iota(jnp.int32, (NB, NB * NB), 1) // NB
    mine = at == lax.broadcasted_iota(jnp.int32, (NB, NB * NB), 0)
    key = lax.broadcasted_iota(jnp.int32, (NB * NB, LANES), 0) % NB
    column = lax.broadcasted_iota(jnp.int32, (NB * NB, LANES), 1)
    cube = jnp.zeros((H * NB, LANES), F32)
    for number, piece in enumerate(split_three(table)):
        spread = [jnp.where(mine, piece[h : h + 1, :], 0.0) for h in range(H)]
        place = jnp.where(column == key + number * NB, 1.0, 0.0).astype(BF16)
        cube = cube + jnp.dot(
            jnp.concatenate(spread, axis=0).astype(BF16), place, preferred_element_type=F32
        )
    cube = cube.astype(BF16)
    hot = one_hot_slab(bucket_ref[...].astype(F32))[:, :NB]
    for h in range(H):
        bias_ref[:, h * LANES : (h + 1) * LANES] = jnp.dot(
            hot, cube[h * NB : (h + 1) * NB, :], preferred_element_type=F32
        ).astype(BF16)
    for copy in copies:
        copy.wait()
    for t in range(TILES):
        tile = tiles_held[:, t * rows : (t + 1) * rows]
        masked_ref[:, t * rows : (t + 1) * rows] = jnp.where(
            t < count_ref[0], tile, jnp.zeros_like(tile)
        )


def aggregate_kernel(order, from_ref, extra_ref, masked_ref, *refs):
    feature_refs, out_ref, short_ref, held = refs[:-3], refs[-3], refs[-2], refs[-1]
    rows = feature_refs[0].shape[0]
    for d, ref in zip([0, *order], feature_refs):
        held[d * rows : (d + 1) * rows, :] = ref[...]
    picked = []
    for t in range(TILES):
        start = pl.multiple_of(from_ref[t, 0] * rows, rows)
        picked.append(held[pl.ds(start, rows), :])
    total = feature_refs[0][...].astype(F32) + jnp.dot(
        masked_ref[...], jnp.concatenate(picked, axis=0), preferred_element_type=F32
    )
    mean_square = jnp.mean(total * total, axis=-1, keepdims=True)
    result = jnp.concatenate(
        [total * lax.rsqrt(mean_square + 1e-06), extra_ref[...]], axis=0
    ).astype(BF16)
    out_ref[...] = result
    short_ref[...] = result[: short_ref.shape[0], :]


def slab_heads(slab):
    return slab * LANES // HD, ((slab + 1) * LANES - 1) // HD


def project_blocks(block_refs, rows, w_qk_ref, w_v_ref, hot_ref, k_ref, v_ref):
    width = w_v_ref.shape[0]
    arrived = [ref[...] for ref in block_refs]
    for s, item in enumerate(arrived):
        bucket = item[rows:, :rows].astype(F32)[:1, :]
        hot_ref[s * rows : (s + 1) * rows, :] = one_hot_slab(bucket)
    block = jnp.concatenate([item[:rows, :] for item in arrived], axis=0)
    for n in range(0, width, 256):
        k_ref[:, n : n + 256] = jnp.dot(
            block, w_qk_ref[:, width + n : width + n + 256], preferred_element_type=F32
        ).astype(BF16)
        v_ref[:, n : n + 256] = jnp.dot(
            block, w_v_ref[:, n : n + 256], preferred_element_type=F32
        ).astype(BF16)
    return block


def project_kernel(w_qk_ref, w_v_ref, *refs):
    *block_refs, hot_ref, k_ref, v_ref = refs
    rows = hot_ref.shape[0] // len(block_refs)
    project_blocks(block_refs, rows, w_qk_ref, w_v_ref, hot_ref, k_ref, v_ref)


def part_kernel(count, first, last, w_qk_ref, w_v_ref, *refs):
    block_refs, refs = refs[:count], refs[count:]
    hot_refs, k_refs, v_refs = ([ref] for ref in refs[-6:-3])
    p_refs, top_ref = refs[-3:-1], refs[-1]
    refs = refs[:-6]
    if first:
        bias_ref, q_ref, shifted_ref, *outs = refs
    else:
        ready, (q_ref, bias_ref, *refs) = refs[:3], refs[3:]
        old_refs, outs = (refs[:2], refs[2:]) if len(refs) in (3, 5) else (refs[:3], refs[3:])
    rows = q_ref.shape[0]
    width = w_v_ref.shape[0]
    block = project_blocks(
        block_refs, rows, w_qk_ref, w_v_ref, hot_refs[0], k_refs[0], v_refs[0]
    )
    if first:
        for n in range(0, width, 256):
            q_ref[:, n : n + 256] = jnp.dot(
                block[:rows, :], w_qk_ref[:, n : n + 256], preferred_element_type=F32
            ).astype(BF16)
    else:
        for some, ref in zip((hot_refs, k_refs, v_refs), ready):
            some.insert(0, ref)
    keys = sum(ref.shape[0] for ref in hot_refs)

    def every(some, cols=slice(None)):
        return jnp.concatenate([ref[:, cols] for ref in some], axis=0)

    lane = lax.broadcasted_iota(jnp.int32, (rows, LANES), 1)
    ones = jnp.ones((keys, LANES), BF16)

    def span(start, size):
        return pl.ds(start if isinstance(start, int) else pl.multiple_of(start, LANES), size)

    def scores(half, slab):
        cols = span(half * HALF + slab * LANES, LANES)
        begin, end = slab_heads(slab)
        q = q_ref[:, cols]
        zero = jnp.zeros_like(q)
        lefts, rights = [], []
        for h in range(begin, end + 1):
            inside = (lane >= h * HD - slab * LANES) & (lane < (h + 1) * HD - slab * LANES)
            lefts.append(jnp.where(inside, q, zero))
            if h * HD >= slab * LANES:
                rights.append(bias_ref[:, span((half * SET + h) * LANES, LANES)])
            else:
                rights.append(zero)
        query = jnp.concatenate(
            [jnp.concatenate(lefts, axis=0), jnp.concatenate(rights, axis=0)], axis=1
        )
        key = jnp.concatenate([every(k_refs, cols), every(hot_refs)], axis=1)
        return lax.dot_general(query, key, NT, preferred_element_type=F32)

    def weigh(half, slab, x, carried, p_ref, local):
        begin, end = slab_heads(slab)
        for h in range(begin, end + 1):
            own = x[(h - begin) * rows : (h - begin + 1) * rows, :]
            if h * HD < slab * LANES:
                own = own + carried
            if (h + 1) * HD > (slab + 1) * LANES:
                return own
            if local:
                peak = jnp.max(own, axis=-1, keepdims=True)
                own = own - peak
                keep_peak(half, h, peak)
            p_ref[h * rows : (h + 1) * rows, :] = jnp.exp2(own * FACTOR).astype(BF16)
        return None

    def keep_peak(half, h, peak):
        if first:
            at = span((half * SET + h) * LANES, LANES)
            mark = jnp.zeros((rows, LANES), F32)
            for number, piece in enumerate(split_three(-peak)):
                mark = jnp.where(lane == SHIFT + number, piece, mark)
            shifted_ref[:, at] = bias_ref[:, at] + mark.astype(BF16)
        else:
            top_ref[h * rows : (h + 1) * rows, :] = jnp.broadcast_to(peak, (rows, LANES))

    def pick(array, slab, base):
        begin, end = slab_heads(slab)
        out = array[(begin - base) * rows : (begin - base + 1) * rows, :]
        for h in range(begin + 1, end + 1):
            piece = array[(h - base) * rows : (h - base + 1) * rows, :]
            out = jnp.where(lane >= h * HD - slab * LANES, piece, out)
        return out

    def mix(half, slab, p_ref):
        cols = span(half * HALF + slab * LANES, LANES)
        begin, end = slab_heads(slab)
        value = jnp.concatenate([every(v_refs, cols), ones], axis=1)
        mixed = jnp.dot(
            p_ref[begin * rows : (end + 1) * rows, :], value, preferred_element_type=F32
        )
        return cols, pick(mixed[:, :LANES], slab, begin), pick(mixed[:, LANES:], slab, begin)

    def add(half, slab, p_ref):
        cols, top, total = mix(half, slab, p_ref)
        if not first:
            top = top + old_refs[0][:, cols]
            total = total + old_refs[1][:, cols]
        if last:
            outs[0][:, cols] = (top / total).astype(BF16)
        else:
            outs[0][:, cols] = top
            outs[1][:, cols] = total
            if not first:
                outs[2][:, cols] = jnp.zeros_like(top)
        return total

    steps = [divmod(step, SLABS) for step in range(width // LANES)]
    largest = jnp.zeros((rows, LANES), F32)
    x = scores(*steps[0])
    carried = None
    for number, (half, slab) in enumerate(steps):
        ahead = scores(*steps[number + 1]) if number + 1 < len(steps) else None
        carried = weigh(half, slab, x, carried, p_refs[half % 2], first)
        if number:
            before = steps[number - 1]
            largest = jnp.maximum(largest, add(*before, p_refs[before[0] % 2]))
        x = ahead
    largest = jnp.maximum(largest, add(*steps[-1], p_refs[steps[-1][0] % 2]))
    if first:
        return
    fine = jnp.max(largest) < SAFE
    if len(old_refs) == 3:
        fine = fine & (jnp.max(old_refs[2][...]) == 0.0)

    @pl.when(jnp.logical_not(fine))
    def _():
        def careful(half, carry):
            left = None
            for slab in range(SLABS):
                left = weigh(half, slab, scores(half, slab), left, p_refs[0], True)
            for slab in range(SLABS):
                cols, top, total = mix(half, slab, p_refs[0])
                peak = pick(top_ref[...], slab, 0)
                old = old_refs[2][:, cols] if len(old_refs) == 3 else jnp.zeros_like(top)
                best = jnp.maximum(old, peak)
                share = jnp.exp2((peak - best) * FACTOR)
                old_share = jnp.exp2((old - best) * FACTOR)
                top = top * share + old_refs[0][:, cols] * old_share
                total = total * share + old_refs[1][:, cols] * old_share
                if last:
                    outs[0][:, cols] = (top / total).astype(BF16)
                else:
                    outs[0][:, cols] = top
                    outs[1][:, cols] = total
                    outs[2][:, cols] = best
            return carry

        lax.fori_loop(0, width // HALF, careful, 0)


def attend_part(first, last, w_qk, w_v, blocks, inputs):
    width = w_v.shape[0]
    rows = inputs[0].shape[0]
    ready = []
    if not first:
        near, blocks = blocks[::2], blocks[1::2]
        count = rows * len(near)
        ready = pl.pallas_call(
            project_kernel,
            out_shape=[shape(count, LANES), shape(count, width), shape(count, width)],
            in_specs=[vmem()] * (2 + len(near)),
            out_specs=[vmem()] * 3,
            compiler_params=limit(8),
            cost_estimate=pl.CostEstimate(flops=1000, bytes_accessed=1000, transcendentals=0),
            name="project",
        )(w_qk, w_v, *near)
    count = rows * len(blocks)
    keys = count + sum(item.shape[0] for item in ready[:1])
    state = shape(rows, width, dtype=F32)
    if first:
        outs = [shape(rows, width), shape(rows, H * LANES), state, state]
    elif last:
        outs = [shape(rows, width)]
    else:
        outs = [state] * 3
    operands = [w_qk, w_v, *blocks, *ready, *inputs]
    tall = SET * rows
    need = 4 * tall * keys + 4 * keys * width + 4 * tall * LANES
    return pl.pallas_call(
        lambda *refs: part_kernel(len(blocks), first, last, *refs),
        out_shape=outs,
        in_specs=[vmem()] * len(operands),
        out_specs=[vmem()] * len(outs),
        scratch_shapes=[
            pltpu.VMEM((count, LANES), BF16),
            pltpu.VMEM((count, width), BF16),
            pltpu.VMEM((count, width), BF16),
            pltpu.VMEM((tall, keys), BF16),
            pltpu.VMEM((tall, keys), BF16),
            pltpu.VMEM((tall, LANES), F32),
        ],
        compiler_params=limit(need // MIB + 8),
        cost_estimate=pl.CostEstimate(
            flops=1000 if not last else 10**9, bytes_accessed=1000 if not last else 4_000_000, transcendentals=0
        ),
        name="part",
    )(*operands)


def swap(array, axis, distance):
    return lax.ppermute(array, axis, [(i, i ^ distance) for i in range(lax.axis_size(axis))])


def after(value, *others):
    return lax.optimization_barrier((value, others))[0]


def on_device(features, tiles, tile_src, tile_count, node_bucket, w_qk, w_v, bias_table):
    rows, width = features.shape
    groups = lax.axis_size("group")
    seq_count = lax.axis_size("seq")
    chips = seq_count // 2
    any_space = pl.BlockSpec(memory_space=pl.ANY)

    order = [1, *range(groups - 1, 1, -1)]
    received = [swap(features, "group", d) for d in order]
    own_bucket = node_bucket.reshape(1, rows)

    bias, own_features, masked, extra, source = pl.pallas_call(
        stage_kernel,
        out_shape=[
            shape(rows, H * LANES), shape(rows, width), shape(rows, TILES * rows),
            shape(EXTRA, width, dtype=F32),
            shape(TILES, LANES, dtype=jnp.int32),
        ],
        in_specs=[smem()] * 3 + [vmem(), vmem(), any_space, any_space],
        out_specs=[vmem()] * 5,
        scratch_shapes=[pltpu.VMEM((rows, TILES * rows), BF16), pltpu.SemaphoreType.DMA((2,))],
        compiler_params=limit(8),
        cost_estimate=pl.CostEstimate(flops=10**9, bytes_accessed=4_000_000, transcendentals=0),
        name="stage",
    )(tile_count, lax.axis_index("group").reshape(1), tile_src, bias_table, own_bucket, features, tiles)

    own, short = pl.pallas_call(
        lambda *refs: aggregate_kernel(order, *refs),
        out_shape=[shape(rows + EXTRA, width), shape(rows + EXTRA // 2, width)],
        in_specs=[vmem()] * (3 + groups),
        out_specs=[vmem()] * 2,
        scratch_shapes=[pltpu.VMEM((groups * rows, width), BF16)],
        compiler_params=limit(8),
        cost_estimate=pl.CostEstimate(flops=10**9, bytes_accessed=4_000_000, transcendentals=0),
        name="aggregate",
    )(source, extra, masked, own_features, *received)

    far = [short] + [None] * (chips - 1)
    top = 1
    while 2 * top < chips:
        top *= 2
    if top == 2:
        lead = [(i, i ^ (2 if i % 2 else 2 * top)) for i in range(seq_count)]
        other = [(i, i ^ (2 * top if i % 2 else 2)) for i in range(seq_count)]
        far[top] = lax.ppermute(own, "seq", lead)
        far[1] = lax.ppermute(short, "seq", other)
        far[top + 1] = lax.ppermute(far[top], "seq", other)
    else:
        step = top
        while step:
            far[step] = swap(own, "seq", 2 * step)
            step //= 2
    for d in range(3, chips):
        if far[d] is None:
            far[d] = swap(far[d & (d - 1)], "seq", 2 * (d & -d))
    parts = [[0], [1, top]] if top > 1 else [[0, 1]]
    parts += [[d] for d in range(2, chips) if d != top]
    queries, state = [], [bias]
    for number, part in enumerate(parts):
        blocks = []
        for d in part:
            block = far[d]
            if d:
                block = after(block, *state)
                near = swap(block, "seq", 1)
            else:
                near = swap(short, "seq", 1)
            blocks += [block, near]
        state = attend_part(
            number == 0, number == len(parts) - 1, w_qk, w_v, blocks, [*queries, *state]
        )
        if number == 0:
            queries, state = state[:2], state[2:]
    return state[0]


def solution(mesh):
    in_specs = (
        P(("group", "seq"), None),
        P(("group", "seq"), None),
        P(("group", "seq"), None),
        P(("group", "seq")),
        P(("group", "seq")),
        P(),
        P(),
        P(),
    )
    out_specs = P(("group", "seq"), None)
    return jax.shard_map(
        on_device, mesh=mesh, in_specs=in_specs, out_specs=out_specs, check_vma=False
    )
```

```python
import math

import jax
import jax.numpy as jnp
from jax import lax
from jax.experimental import pallas as pl
from jax.experimental.pallas import tpu as pltpu
from jax.sharding import PartitionSpec as P

H = 32
HD = 24
NB = 16
TILES = 8
LANES = 128
SET = 16
HALF = SET * HD
SLABS = HALF // LANES
SAFE = 1e30
EXTRA = 8
SHIFT = 3 * NB
NT = (((1,), (1,)), ((), ()))
MIB = 1024 * 1024
BF16 = jnp.bfloat16
F32 = jnp.float32
FACTOR = math.log2(math.e) / math.sqrt(HD)


def vmem():
    return pl.BlockSpec(memory_space=pltpu.VMEM)


def smem():
    return pl.BlockSpec(memory_space=pltpu.SMEM)


def limit(mib):
    return pltpu.CompilerParams(vmem_limit_bytes=mib * MIB)


def shape(*dims, dtype=BF16):
    return jax.ShapeDtypeStruct(dims, dtype)


def one_hot_slab(bucket_row):
    n = bucket_row.shape[1]
    index = lax.broadcasted_iota(jnp.int32, (LANES, n), 0)
    wanted = jnp.where(index < 3 * NB, index % NB, -1).astype(F32)
    hot = jnp.where((wanted == bucket_row) | ((index >= SHIFT) & (index < SHIFT + 3)), 1.0, 0.0)
    return hot.T.astype(BF16)


def split_three(x):
    high = x.astype(BF16).astype(F32)
    mid = (x - high).astype(BF16).astype(F32)
    return high, mid, x - high - mid


def stage_kernel(
    count_ref, me_ref, src_ref, table_ref, bucket_ref, features_ref, tiles_ref,
    bias_ref, own_ref, masked_ref, extra_ref, from_ref, tiles_held, sems,
):
    rows = own_ref.shape[0]
    copies = [
        pltpu.make_async_copy(tiles_ref, tiles_held, sems.at[0]),
        pltpu.make_async_copy(features_ref, own_ref, sems.at[1]),
    ]
    for copy in copies:
        copy.start()
    for t in range(TILES):
        from_ref[t : t + 1, :] = jnp.full((1, LANES), src_ref[0, t] ^ me_ref[0], jnp.int32)
    width = own_ref.shape[1]
    extra = jnp.concatenate(
        [bucket_ref[...].astype(F32), jnp.zeros((1, width - rows), F32)], axis=1
    )
    extra_ref[...] = jnp.broadcast_to(extra, (EXTRA, width))
    table = table_ref[...] * math.sqrt(HD)
    at = lax.broadcasted_iota(jnp.int32, (NB, NB * NB), 1) // NB
    mine = at == lax.broadcasted_iota(jnp.int32, (NB, NB * NB), 0)
    key = lax.broadcasted_iota(jnp.int32, (NB * NB, LANES), 0) % NB
    column = lax.broadcasted_iota(jnp.int32, (NB * NB, LANES), 1)
    cube = jnp.zeros((H * NB, LANES), F32)
    for number, piece in enumerate(split_three(table)):
        spread = [jnp.where(mine, piece[h : h + 1, :], 0.0) for h in range(H)]
        place = jnp.where(column == key + number * NB, 1.0, 0.0).astype(BF16)
        cube = cube + jnp.dot(
            jnp.concatenate(spread, axis=0).astype(BF16), place, preferred_element_type=F32
        )
    cube = cube.astype(BF16)
    hot = one_hot_slab(bucket_ref[...].astype(F32))[:, :NB]
    for h in range(H):
        bias_ref[:, h * LANES : (h + 1) * LANES] = jnp.dot(
            hot, cube[h * NB : (h + 1) * NB, :], preferred_element_type=F32
        ).astype(BF16)
    for copy in copies:
        copy.wait()
    for t in range(TILES):
        tile = tiles_held[:, t * rows : (t + 1) * rows]
        masked_ref[:, t * rows : (t + 1) * rows] = jnp.where(
            t < count_ref[0], tile, jnp.zeros_like(tile)
        )


def aggregate_kernel(order, from_ref, extra_ref, masked_ref, *refs):
    feature_refs, out_ref, short_ref, least_ref, held = refs[:-4], *refs[-4:]
    rows = feature_refs[0].shape[0]
    for d, ref in zip([0, *order], feature_refs):
        held[d * rows : (d + 1) * rows, :] = ref[...]
    picked = []
    for t in range(TILES):
        start = pl.multiple_of(from_ref[t, 0] * rows, rows)
        picked.append(held[pl.ds(start, rows), :])
    total = feature_refs[0][...].astype(F32) + jnp.dot(
        masked_ref[...], jnp.concatenate(picked, axis=0), preferred_element_type=F32
    )
    mean_square = jnp.mean(total * total, axis=-1, keepdims=True)
    result = jnp.concatenate(
        [total * lax.rsqrt(mean_square + 1e-06), extra_ref[...]], axis=0
    ).astype(BF16)
    out_ref[...] = result
    short_ref[...] = result[: short_ref.shape[0], :]
    least_ref[...] = result[: least_ref.shape[0], :]


def slab_heads(slab):
    return slab * LANES // HD, ((slab + 1) * LANES - 1) // HD


def project_blocks(block_refs, rows, w_qk_ref, w_v_ref, hot_ref, k_ref, v_ref):
    width = w_v_ref.shape[0]
    arrived = [ref[...] for ref in block_refs]
    for s, item in enumerate(arrived):
        bucket = item[rows:, :rows].astype(F32)[:1, :]
        hot_ref[s * rows : (s + 1) * rows, :] = one_hot_slab(bucket)
    block = jnp.concatenate([item[:rows, :] for item in arrived], axis=0)
    for n in range(0, width, 256):
        k_ref[:, n : n + 256] = jnp.dot(
            block, w_qk_ref[:, width + n : width + n + 256], preferred_element_type=F32
        ).astype(BF16)
        v_ref[:, n : n + 256] = jnp.dot(
            block, w_v_ref[:, n : n + 256], preferred_element_type=F32
        ).astype(BF16)
    return block


def project_kernel(w_qk_ref, w_v_ref, *refs):
    *block_refs, hot_ref, k_ref, v_ref = refs
    rows = hot_ref.shape[0] // len(block_refs)
    project_blocks(block_refs, rows, w_qk_ref, w_v_ref, hot_ref, k_ref, v_ref)


def part_kernel(count, first, last, w_qk_ref, w_v_ref, *refs):
    block_refs, refs = refs[:count], refs[count:]
    hot_refs, k_refs, v_refs = ([ref] for ref in refs[-6:-3])
    p_refs, top_ref = refs[-3:-1], refs[-1]
    refs = refs[:-6]
    if first:
        bias_ref, q_ref, shifted_ref, *outs = refs
    else:
        ready, (q_ref, bias_ref, *refs) = refs[:3], refs[3:]
        old_refs, outs = (refs[:2], refs[2:]) if len(refs) in (3, 5) else (refs[:3], refs[3:])
    rows = q_ref.shape[0]
    width = w_v_ref.shape[0]
    block = project_blocks(
        block_refs, rows, w_qk_ref, w_v_ref, hot_refs[0], k_refs[0], v_refs[0]
    )
    if first:
        for n in range(0, width, 256):
            q_ref[:, n : n + 256] = jnp.dot(
                block[:rows, :], w_qk_ref[:, n : n + 256], preferred_element_type=F32
            ).astype(BF16)
    else:
        for some, ref in zip((hot_refs, k_refs, v_refs), ready):
            some.insert(0, ref)
    keys = sum(ref.shape[0] for ref in hot_refs)

    def every(some, cols=slice(None)):
        return jnp.concatenate([ref[:, cols] for ref in some], axis=0)

    lane = lax.broadcasted_iota(jnp.int32, (rows, LANES), 1)
    ones = jnp.ones((keys, LANES), BF16)

    def span(start, size):
        return pl.ds(start if isinstance(start, int) else pl.multiple_of(start, LANES), size)

    def scores(half, slab):
        cols = span(half * HALF + slab * LANES, LANES)
        begin, end = slab_heads(slab)
        q = q_ref[:, cols]
        zero = jnp.zeros_like(q)
        lefts, rights = [], []
        for h in range(begin, end + 1):
            inside = (lane >= h * HD - slab * LANES) & (lane < (h + 1) * HD - slab * LANES)
            lefts.append(jnp.where(inside, q, zero))
            if h * HD >= slab * LANES:
                rights.append(bias_ref[:, span((half * SET + h) * LANES, LANES)])
            else:
                rights.append(zero)
        query = jnp.concatenate(
            [jnp.concatenate(lefts, axis=0), jnp.concatenate(rights, axis=0)], axis=1
        )
        key = jnp.concatenate([every(k_refs, cols), every(hot_refs)], axis=1)
        return lax.dot_general(query, key, NT, preferred_element_type=F32)

    def weigh(half, slab, x, carried, p_ref, local):
        begin, end = slab_heads(slab)
        for h in range(begin, end + 1):
            own = x[(h - begin) * rows : (h - begin + 1) * rows, :]
            if h * HD < slab * LANES:
                own = own + carried
            if (h + 1) * HD > (slab + 1) * LANES:
                return own
            if local:
                peak = jnp.max(own, axis=-1, keepdims=True)
                own = own - peak
                keep_peak(half, h, peak)
            p_ref[h * rows : (h + 1) * rows, :] = jnp.exp2(own * FACTOR).astype(BF16)
        return None

    def keep_peak(half, h, peak):
        if first:
            at = span((half * SET + h) * LANES, LANES)
            mark = jnp.zeros((rows, LANES), F32)
            for number, piece in enumerate(split_three(-peak)):
                mark = jnp.where(lane == SHIFT + number, piece, mark)
            shifted_ref[:, at] = bias_ref[:, at] + mark.astype(BF16)
        else:
            top_ref[h * rows : (h + 1) * rows, :] = jnp.broadcast_to(peak, (rows, LANES))

    def pick(array, slab, base):
        begin, end = slab_heads(slab)
        out = array[(begin - base) * rows : (begin - base + 1) * rows, :]
        for h in range(begin + 1, end + 1):
            piece = array[(h - base) * rows : (h - base + 1) * rows, :]
            out = jnp.where(lane >= h * HD - slab * LANES, piece, out)
        return out

    def mix(half, slab, p_ref):
        cols = span(half * HALF + slab * LANES, LANES)
        begin, end = slab_heads(slab)
        value = jnp.concatenate([every(v_refs, cols), ones], axis=1)
        mixed = jnp.dot(
            p_ref[begin * rows : (end + 1) * rows, :], value, preferred_element_type=F32
        )
        return cols, pick(mixed[:, :LANES], slab, begin), pick(mixed[:, LANES:], slab, begin)

    def add(half, slab, p_ref):
        cols, top, total = mix(half, slab, p_ref)
        if not first:
            top = top + old_refs[0][:, cols]
            total = total + old_refs[1][:, cols]
        if last:
            outs[0][:, cols] = (top / total).astype(BF16)
        else:
            outs[0][:, cols] = top
            outs[1][:, cols] = total
            if not first:
                outs[2][:, cols] = jnp.zeros_like(top)
        return total

    steps = [divmod(step, SLABS) for step in range(width // LANES)]
    largest = jnp.zeros((rows, LANES), F32)
    x = scores(*steps[0])
    carried = None
    for number, (half, slab) in enumerate(steps):
        ahead = scores(*steps[number + 1]) if number + 1 < len(steps) else None
        carried = weigh(half, slab, x, carried, p_refs[half % 2], first)
        if number:
            before = steps[number - 1]
            largest = jnp.maximum(largest, add(*before, p_refs[before[0] % 2]))
        x = ahead
    largest = jnp.maximum(largest, add(*steps[-1], p_refs[steps[-1][0] % 2]))
    if first:
        return
    fine = jnp.max(largest) < SAFE
    if len(old_refs) == 3:
        fine = fine & (jnp.max(old_refs[2][...]) == 0.0)

    @pl.when(jnp.logical_not(fine))
    def _():
        def careful(half, carry):
            left = None
            for slab in range(SLABS):
                left = weigh(half, slab, scores(half, slab), left, p_refs[0], True)
            for slab in range(SLABS):
                cols, top, total = mix(half, slab, p_refs[0])
                peak = pick(top_ref[...], slab, 0)
                old = old_refs[2][:, cols] if len(old_refs) == 3 else jnp.zeros_like(top)
                best = jnp.maximum(old, peak)
                share = jnp.exp2((peak - best) * FACTOR)
                old_share = jnp.exp2((old - best) * FACTOR)
                top = top * share + old_refs[0][:, cols] * old_share
                total = total * share + old_refs[1][:, cols] * old_share
                if last:
                    outs[0][:, cols] = (top / total).astype(BF16)
                else:
                    outs[0][:, cols] = top
                    outs[1][:, cols] = total
                    outs[2][:, cols] = best
            return carry

        lax.fori_loop(0, width // HALF, careful, 0)


def attend_part(first, last, w_qk, w_v, blocks, inputs):
    width = w_v.shape[0]
    rows = inputs[0].shape[0]
    ready = []
    if not first:
        near, blocks = blocks[::2], blocks[1::2]
        count = rows * len(near)
        ready = pl.pallas_call(
            project_kernel,
            out_shape=[shape(count, LANES), shape(count, width), shape(count, width)],
            in_specs=[vmem()] * (2 + len(near)),
            out_specs=[vmem()] * 3,
            compiler_params=limit(8),
            cost_estimate=pl.CostEstimate(flops=1000, bytes_accessed=1000, transcendentals=0),
            name="project",
        )(w_qk, w_v, *near)
    count = rows * len(blocks)
    keys = count + sum(item.shape[0] for item in ready[:1])
    state = shape(rows, width, dtype=F32)
    if first:
        outs = [shape(rows, width), shape(rows, H * LANES), state, state]
    elif last:
        outs = [shape(rows, width)]
    else:
        outs = [state] * 3
    operands = [w_qk, w_v, *blocks, *ready, *inputs]
    tall = SET * rows
    need = 4 * tall * keys + 4 * keys * width + 4 * tall * LANES
    return pl.pallas_call(
        lambda *refs: part_kernel(len(blocks), first, last, *refs),
        out_shape=outs,
        in_specs=[vmem()] * len(operands),
        out_specs=[vmem()] * len(outs),
        scratch_shapes=[
            pltpu.VMEM((count, LANES), BF16),
            pltpu.VMEM((count, width), BF16),
            pltpu.VMEM((count, width), BF16),
            pltpu.VMEM((tall, keys), BF16),
            pltpu.VMEM((tall, keys), BF16),
            pltpu.VMEM((tall, LANES), F32),
        ],
        compiler_params=limit(need // MIB + 8),
        cost_estimate=pl.CostEstimate(
            flops=1000 if not last else 10**9, bytes_accessed=1000 if not last else 4_000_000, transcendentals=0
        ),
        name="part",
    )(*operands)


def swap(array, axis, distance):
    return lax.ppermute(array, axis, [(i, i ^ distance) for i in range(lax.axis_size(axis))])


def after(value, *others):
    return lax.optimization_barrier((value, others))[0]


def on_device(features, tiles, tile_src, tile_count, node_bucket, w_qk, w_v, bias_table):
    rows, width = features.shape
    groups = lax.axis_size("group")
    seq_count = lax.axis_size("seq")
    chips = seq_count // 2
    any_space = pl.BlockSpec(memory_space=pl.ANY)

    order = [1, *range(groups - 1, 1, -1)]
    received = [swap(features, "group", d) for d in order]
    own_bucket = node_bucket.reshape(1, rows)

    bias, own_features, masked, extra, source = pl.pallas_call(
        stage_kernel,
        out_shape=[
            shape(rows, H * LANES), shape(rows, width), shape(rows, TILES * rows),
            shape(EXTRA, width, dtype=F32),
            shape(TILES, LANES, dtype=jnp.int32),
        ],
        in_specs=[smem()] * 3 + [vmem(), vmem(), any_space, any_space],
        out_specs=[vmem()] * 5,
        scratch_shapes=[pltpu.VMEM((rows, TILES * rows), BF16), pltpu.SemaphoreType.DMA((2,))],
        compiler_params=limit(8),
        cost_estimate=pl.CostEstimate(flops=10**9, bytes_accessed=4_000_000, transcendentals=0),
        name="stage",
    )(tile_count, lax.axis_index("group").reshape(1), tile_src, bias_table, own_bucket, features, tiles)

    own, short, least = pl.pallas_call(
        lambda *refs: aggregate_kernel(order, *refs),
        out_shape=[shape(rows + EXTRA, width), shape(rows + EXTRA - 2, width),
            shape(rows + 1, width)],
        in_specs=[vmem()] * (3 + groups),
        out_specs=[vmem()] * 3,
        scratch_shapes=[pltpu.VMEM((groups * rows, width), BF16)],
        compiler_params=limit(8),
        cost_estimate=pl.CostEstimate(flops=10**9, bytes_accessed=4_000_000, transcendentals=0),
        name="aggregate",
    )(source, extra, masked, own_features, *received)

    far = [least] + [None] * (chips - 1)
    top = 1
    while 2 * top < chips:
        top *= 2
    far[top] = swap(own, "seq", 2 * top)
    step = 1
    while step < top:
        far[step] = swap(short, "seq", 2 * step)
        step *= 2
    for d in range(3, chips):
        if far[d] is None:
            far[d] = swap(far[d & (d - 1)], "seq", 2 * (d & -d))
    parts = [[0], [1, top]] if top > 1 else [[0, 1]]
    parts += [[d] for d in range(2, chips) if d != top]
    queries, state = [], [bias]
    for number, part in enumerate(parts):
        blocks = []
        for d in part:
            block = far[d]
            if d:
                block = after(block, *state)
                near = swap(block, "seq", 1)
            else:
                near = swap(least, "seq", 1)
            blocks += [block, near]
        state = attend_part(
            number == 0, number == len(parts) - 1, w_qk, w_v, blocks, [*queries, *state]
        )
        if number == 0:
            queries, state = state[:2], state[2:]
    return state[0]


def solution(mesh):
    in_specs = (
        P(("group", "seq"), None),
        P(("group", "seq"), None),
        P(("group", "seq"), None),
        P(("group", "seq")),
        P(("group", "seq")),
        P(),
        P(),
        P(),
    )
    out_specs = P(("group", "seq"), None)
    return jax.shard_map(
        on_device, mesh=mesh, in_specs=in_specs, out_specs=out_specs, check_vma=False
    )
```

```python
import math

import jax
import jax.numpy as jnp
from jax import lax
from jax.experimental import pallas as pl
from jax.experimental.pallas import tpu as pltpu
from jax.sharding import PartitionSpec as P

H = 32
HD = 24
NB = 16
TILES = 8
LANES = 128
SET = 16
HALF = SET * HD
SLABS = HALF // LANES
SAFE = 1e30
EXTRA = 8
SHIFT = 3 * NB
NT = (((1,), (1,)), ((), ()))
MIB = 1024 * 1024
BF16 = jnp.bfloat16
F32 = jnp.float32
FACTOR = math.log2(math.e) / math.sqrt(HD)


def vmem():
    return pl.BlockSpec(memory_space=pltpu.VMEM)


def smem():
    return pl.BlockSpec(memory_space=pltpu.SMEM)


def limit(mib):
    return pltpu.CompilerParams(vmem_limit_bytes=mib * MIB)


def shape(*dims, dtype=BF16):
    return jax.ShapeDtypeStruct(dims, dtype)


def one_hot_slab(bucket_row):
    n = bucket_row.shape[1]
    index = lax.broadcasted_iota(jnp.int32, (LANES, n), 0)
    wanted = jnp.where(index < 3 * NB, index % NB, -1).astype(F32)
    hot = jnp.where((wanted == bucket_row) | ((index >= SHIFT) & (index < SHIFT + 3)), 1.0, 0.0)
    return hot.T.astype(BF16)


def split_three(x):
    high = x.astype(BF16).astype(F32)
    mid = (x - high).astype(BF16).astype(F32)
    return high, mid, x - high - mid


def stage_kernel(
    count_ref, me_ref, src_ref, table_ref, bucket_ref, features_ref, tiles_ref,
    bias_ref, own_ref, masked_ref, extra_ref, from_ref, tiles_held, sems,
):
    rows = own_ref.shape[0]
    copies = [
        pltpu.make_async_copy(tiles_ref, tiles_held, sems.at[0]),
        pltpu.make_async_copy(features_ref, own_ref, sems.at[1]),
    ]
    for copy in copies:
        copy.start()
    for t in range(TILES):
        from_ref[t : t + 1, :] = jnp.full((1, LANES), src_ref[0, t] ^ me_ref[0], jnp.int32)
    width = own_ref.shape[1]
    extra = jnp.concatenate(
        [bucket_ref[...].astype(F32), jnp.zeros((1, width - rows), F32)], axis=1
    )
    extra_ref[...] = jnp.broadcast_to(extra, (EXTRA, width))
    table = table_ref[...] * math.sqrt(HD)
    at = lax.broadcasted_iota(jnp.int32, (NB, NB * NB), 1) // NB
    mine = at == lax.broadcasted_iota(jnp.int32, (NB, NB * NB), 0)
    key = lax.broadcasted_iota(jnp.int32, (NB * NB, LANES), 0) % NB
    column = lax.broadcasted_iota(jnp.int32, (NB * NB, LANES), 1)
    cube = jnp.zeros((H * NB, LANES), F32)
    for number, piece in enumerate(split_three(table)):
        spread = [jnp.where(mine, piece[h : h + 1, :], 0.0) for h in range(H)]
        place = jnp.where(column == key + number * NB, 1.0, 0.0).astype(BF16)
        cube = cube + jnp.dot(
            jnp.concatenate(spread, axis=0).astype(BF16), place, preferred_element_type=F32
        )
    cube = cube.astype(BF16)
    hot = one_hot_slab(bucket_ref[...].astype(F32))[:, :NB]
    for h in range(H):
        bias_ref[:, h * LANES : (h + 1) * LANES] = jnp.dot(
            hot, cube[h * NB : (h + 1) * NB, :], preferred_element_type=F32
        ).astype(BF16)
    for copy in copies:
        copy.wait()
    for t in range(TILES):
        tile = tiles_held[:, t * rows : (t + 1) * rows]
        masked_ref[:, t * rows : (t + 1) * rows] = jnp.where(
            t < count_ref[0], tile, jnp.zeros_like(tile)
        )


def aggregate_kernel(order, from_ref, extra_ref, masked_ref, *refs):
    feature_refs, out_ref, short_ref, least_ref, held = refs[:-4], *refs[-4:]
    rows = feature_refs[0].shape[0]
    for d, ref in zip([0, *order], feature_refs):
        held[d * rows : (d + 1) * rows, :] = ref[...]
    picked = []
    for t in range(TILES):
        start = pl.multiple_of(from_ref[t, 0] * rows, rows)
        picked.append(held[pl.ds(start, rows), :])
    total = feature_refs[0][...].astype(F32) + jnp.dot(
        masked_ref[...], jnp.concatenate(picked, axis=0), preferred_element_type=F32
    )
    mean_square = jnp.mean(total * total, axis=-1, keepdims=True)
    result = jnp.concatenate(
        [total * lax.rsqrt(mean_square + 1e-06), extra_ref[...]], axis=0
    ).astype(BF16)
    out_ref[...] = result
    short_ref[...] = result[: short_ref.shape[0], :]
    least_ref[...] = result[: least_ref.shape[0], :]


def slab_heads(slab):
    return slab * LANES // HD, ((slab + 1) * LANES - 1) // HD


def arrived_rows(block_refs, rows, hot_ref):
    arrived = [ref[...] for ref in block_refs]
    for s, item in enumerate(arrived):
        bucket = item[rows:, :rows].astype(F32)[:1, :]
        hot_ref[s * rows : (s + 1) * rows, :] = one_hot_slab(bucket)
    return jnp.concatenate([item[:rows, :] for item in arrived], axis=0)


def project(block, n, w_qk_ref, w_v_ref, k_ref, v_ref):
    width = w_v_ref.shape[0]
    k_ref[:, n : n + 256] = jnp.dot(
        block, w_qk_ref[:, width + n : width + n + 256], preferred_element_type=F32
    ).astype(BF16)
    v_ref[:, n : n + 256] = jnp.dot(
        block, w_v_ref[:, n : n + 256], preferred_element_type=F32
    ).astype(BF16)


def project_kernel(w_qk_ref, w_v_ref, *refs):
    *block_refs, hot_ref, k_ref, v_ref = refs
    rows = hot_ref.shape[0] // len(block_refs)
    block = arrived_rows(block_refs, rows, hot_ref)
    for n in range(0, k_ref.shape[1], 256):
        project(block, n, w_qk_ref, w_v_ref, k_ref, v_ref)


def part_kernel(count, first, last, w_qk_ref, w_v_ref, *refs):
    block_refs, refs = refs[:count], refs[count:]
    hot_refs, k_refs, v_refs = ([ref] for ref in refs[-6:-3])
    p_refs, top_ref = refs[-3:-1], refs[-1]
    refs = refs[:-6]
    if first:
        bias_ref, q_ref, shifted_ref, *outs = refs
    else:
        ready, (q_ref, bias_ref, *refs) = refs[:3], refs[3:]
        old_refs, outs = (refs[:2], refs[2:]) if len(refs) in (3, 5) else (refs[:3], refs[3:])
    rows = q_ref.shape[0]
    width = w_v_ref.shape[0]
    block = arrived_rows(block_refs, rows, hot_refs[0])
    raw_k_ref, raw_v_ref = k_refs[0], v_refs[0]

    def prepare(step):
        n = step * LANES
        if n % 256:
            return
        if first:
            q_ref[:, n : n + 256] = jnp.dot(
                block[:rows, :], w_qk_ref[:, n : n + 256], preferred_element_type=F32
            ).astype(BF16)
        project(block, n, w_qk_ref, w_v_ref, raw_k_ref, raw_v_ref)

    if not first:
        for some, ref in zip((hot_refs, k_refs, v_refs), ready):
            some.insert(0, ref)
    keys = sum(ref.shape[0] for ref in hot_refs)

    def every(some, cols=slice(None)):
        return jnp.concatenate([ref[:, cols] for ref in some], axis=0)

    lane = lax.broadcasted_iota(jnp.int32, (rows, LANES), 1)
    ones = jnp.ones((keys, LANES), BF16)

    def span(start, size):
        return pl.ds(start if isinstance(start, int) else pl.multiple_of(start, LANES), size)

    def scores(half, slab):
        cols = span(half * HALF + slab * LANES, LANES)
        begin, end = slab_heads(slab)
        q = q_ref[:, cols]
        zero = jnp.zeros_like(q)
        lefts, rights = [], []
        for h in range(begin, end + 1):
            inside = (lane >= h * HD - slab * LANES) & (lane < (h + 1) * HD - slab * LANES)
            lefts.append(jnp.where(inside, q, zero))
            if h * HD >= slab * LANES:
                rights.append(bias_ref[:, span((half * SET + h) * LANES, LANES)])
            else:
                rights.append(zero)
        query = jnp.concatenate(
            [jnp.concatenate(lefts, axis=0), jnp.concatenate(rights, axis=0)], axis=1
        )
        key = jnp.concatenate([every(k_refs, cols), every(hot_refs)], axis=1)
        return lax.dot_general(query, key, NT, preferred_element_type=F32)

    def weigh(half, slab, x, carried, p_ref, local):
        begin, end = slab_heads(slab)
        for h in range(begin, end + 1):
            own = x[(h - begin) * rows : (h - begin + 1) * rows, :]
            if h * HD < slab * LANES:
                own = own + carried
            if (h + 1) * HD > (slab + 1) * LANES:
                return own
            if local:
                peak = jnp.max(own, axis=-1, keepdims=True)
                own = own - peak
                keep_peak(half, h, peak)
            p_ref[h * rows : (h + 1) * rows, :] = jnp.exp2(own * FACTOR).astype(BF16)
        return None

    def keep_peak(half, h, peak):
        if first:
            at = span((half * SET + h) * LANES, LANES)
            mark = jnp.zeros((rows, LANES), F32)
            for number, piece in enumerate(split_three(-peak)):
                mark = jnp.where(lane == SHIFT + number, piece, mark)
            shifted_ref[:, at] = bias_ref[:, at] + mark.astype(BF16)
        else:
            top_ref[h * rows : (h + 1) * rows, :] = jnp.broadcast_to(peak, (rows, LANES))

    def pick(array, slab, base):
        begin, end = slab_heads(slab)
        out = array[(begin - base) * rows : (begin - base + 1) * rows, :]
        for h in range(begin + 1, end + 1):
            piece = array[(h - base) * rows : (h - base + 1) * rows, :]
            out = jnp.where(lane >= h * HD - slab * LANES, piece, out)
        return out

    def mix(half, slab, p_ref):
        cols = span(half * HALF + slab * LANES, LANES)
        begin, end = slab_heads(slab)
        value = jnp.concatenate([every(v_refs, cols), ones], axis=1)
        mixed = jnp.dot(
            p_ref[begin * rows : (end + 1) * rows, :], value, preferred_element_type=F32
        )
        return cols, pick(mixed[:, :LANES], slab, begin), pick(mixed[:, LANES:], slab, begin)

    def add(half, slab, p_ref):
        cols, top, total = mix(half, slab, p_ref)
        if not first:
            top = top + old_refs[0][:, cols]
            total = total + old_refs[1][:, cols]
        if last:
            outs[0][:, cols] = (top / total).astype(BF16)
        else:
            outs[0][:, cols] = top
            outs[1][:, cols] = total
            if not first:
                outs[2][:, cols] = jnp.zeros_like(top)
        return total

    steps = [divmod(step, SLABS) for step in range(width // LANES)]
    largest = jnp.zeros((rows, LANES), F32)
    prepare(0)
    x = scores(*steps[0])
    carried = None
    for number, (half, slab) in enumerate(steps):
        ahead = None
        if number + 1 < len(steps):
            prepare(number + 1)
            ahead = scores(*steps[number + 1])
        carried = weigh(half, slab, x, carried, p_refs[half % 2], first)
        if number:
            before = steps[number - 1]
            largest = jnp.maximum(largest, add(*before, p_refs[before[0] % 2]))
        x = ahead
    largest = jnp.maximum(largest, add(*steps[-1], p_refs[steps[-1][0] % 2]))
    if first:
        return
    fine = jnp.max(largest) < SAFE
    if len(old_refs) == 3:
        fine = fine & (jnp.max(old_refs[2][...]) == 0.0)

    @pl.when(jnp.logical_not(fine))
    def _():
        def careful(half, carry):
            left = None
            for slab in range(SLABS):
                left = weigh(half, slab, scores(half, slab), left, p_refs[0], True)
            for slab in range(SLABS):
                cols, top, total = mix(half, slab, p_refs[0])
                peak = pick(top_ref[...], slab, 0)
                old = old_refs[2][:, cols] if len(old_refs) == 3 else jnp.zeros_like(top)
                best = jnp.maximum(old, peak)
                share = jnp.exp2((peak - best) * FACTOR)
                old_share = jnp.exp2((old - best) * FACTOR)
                top = top * share + old_refs[0][:, cols] * old_share
                total = total * share + old_refs[1][:, cols] * old_share
                if last:
                    outs[0][:, cols] = (top / total).astype(BF16)
                else:
                    outs[0][:, cols] = top
                    outs[1][:, cols] = total
                    outs[2][:, cols] = best
            return carry

        lax.fori_loop(0, width // HALF, careful, 0)


def attend_part(first, last, w_qk, w_v, blocks, inputs):
    width = w_v.shape[0]
    rows = inputs[0].shape[0]
    ready = []
    if not first:
        near, blocks = blocks[::2], blocks[1::2]
        count = rows * len(near)
        ready = pl.pallas_call(
            project_kernel,
            out_shape=[shape(count, LANES), shape(count, width), shape(count, width)],
            in_specs=[vmem()] * (2 + len(near)),
            out_specs=[vmem()] * 3,
            compiler_params=limit(8),
            cost_estimate=pl.CostEstimate(flops=1000, bytes_accessed=1000, transcendentals=0),
            name="project",
        )(w_qk, w_v, *near)
    count = rows * len(blocks)
    keys = count + sum(item.shape[0] for item in ready[:1])
    state = shape(rows, width, dtype=F32)
    if first:
        outs = [shape(rows, width), shape(rows, H * LANES), state, state]
    elif last:
        outs = [shape(rows, width)]
    else:
        outs = [state] * 3
    operands = [w_qk, w_v, *blocks, *ready, *inputs]
    tall = SET * rows
    need = 4 * tall * keys + 4 * keys * width + 4 * tall * LANES
    return pl.pallas_call(
        lambda *refs: part_kernel(len(blocks), first, last, *refs),
        out_shape=outs,
        in_specs=[vmem()] * len(operands),
        out_specs=[vmem()] * len(outs),
        scratch_shapes=[
            pltpu.VMEM((count, LANES), BF16),
            pltpu.VMEM((count, width), BF16),
            pltpu.VMEM((count, width), BF16),
            pltpu.VMEM((tall, keys), BF16),
            pltpu.VMEM((tall, keys), BF16),
            pltpu.VMEM((tall, LANES), F32),
        ],
        compiler_params=limit(need // MIB + 8),
        cost_estimate=pl.CostEstimate(
            flops=1000 if not last else 10**9, bytes_accessed=1000 if not last else 4_000_000, transcendentals=0
        ),
        name="part",
    )(*operands)


def swap(array, axis, distance):
    return lax.ppermute(array, axis, [(i, i ^ distance) for i in range(lax.axis_size(axis))])


def after(value, *others):
    return lax.optimization_barrier((value, others))[0]


def on_device(features, tiles, tile_src, tile_count, node_bucket, w_qk, w_v, bias_table):
    rows, width = features.shape
    groups = lax.axis_size("group")
    seq_count = lax.axis_size("seq")
    chips = seq_count // 2
    any_space = pl.BlockSpec(memory_space=pl.ANY)

    order = [1, *range(groups - 1, 1, -1)]
    received = [swap(features, "group", d) for d in order]
    own_bucket = node_bucket.reshape(1, rows)

    bias, own_features, masked, extra, source = pl.pallas_call(
        stage_kernel,
        out_shape=[
            shape(rows, H * LANES), shape(rows, width), shape(rows, TILES * rows),
            shape(EXTRA, width, dtype=F32),
            shape(TILES, LANES, dtype=jnp.int32),
        ],
        in_specs=[smem()] * 3 + [vmem(), vmem(), any_space, any_space],
        out_specs=[vmem()] * 5,
        scratch_shapes=[pltpu.VMEM((rows, TILES * rows), BF16), pltpu.SemaphoreType.DMA((2,))],
        compiler_params=limit(8),
        cost_estimate=pl.CostEstimate(flops=10**9, bytes_accessed=4_000_000, transcendentals=0),
        name="stage",
    )(tile_count, lax.axis_index("group").reshape(1), tile_src, bias_table, own_bucket, features, tiles)

    own, short, least = pl.pallas_call(
        lambda *refs: aggregate_kernel(order, *refs),
        out_shape=[shape(rows + EXTRA, width), shape(rows + EXTRA - 2, width),
            shape(rows + 1, width)],
        in_specs=[vmem()] * (3 + groups),
        out_specs=[vmem()] * 3,
        scratch_shapes=[pltpu.VMEM((groups * rows, width), BF16)],
        compiler_params=limit(8),
        cost_estimate=pl.CostEstimate(flops=10**9, bytes_accessed=4_000_000, transcendentals=0),
        name="aggregate",
    )(source, extra, masked, own_features, *received)

    far = [least] + [None] * (chips - 1)
    top = 1
    while 2 * top < chips:
        top *= 2
    far[top] = swap(own, "seq", 2 * top)
    step = 1
    while step < top:
        far[step] = swap(short, "seq", 2 * step)
        step *= 2
    for d in range(3, chips):
        if far[d] is None:
            far[d] = swap(far[d & (d - 1)], "seq", 2 * (d & -d))
    parts = [[0], [1, top]] if top > 1 else [[0, 1]]
    parts += [[d] for d in range(2, chips) if d != top]
    queries, state = [], [bias]
    for number, part in enumerate(parts):
        blocks = []
        for d in part:
            block = far[d]
            if d:
                block = after(block, *state)
                near = swap(block, "seq", 1)
            else:
                near = swap(least, "seq", 1)
            blocks += [block, near]
        state = attend_part(
            number == 0, number == len(parts) - 1, w_qk, w_v, blocks, [*queries, *state]
        )
        if number == 0:
            queries, state = state[:2], state[2:]
    return state[0]


def solution(mesh):
    in_specs = (
        P(("group", "seq"), None),
        P(("group", "seq"), None),
        P(("group", "seq"), None),
        P(("group", "seq")),
        P(("group", "seq")),
        P(),
        P(),
        P(),
    )
    out_specs = P(("group", "seq"), None)
    return jax.shard_map(
        on_device, mesh=mesh, in_specs=in_specs, out_specs=out_specs, check_vma=False
    )
```

```python
import math

import jax
import jax.numpy as jnp
from jax import lax
from jax.experimental import pallas as pl
from jax.experimental.pallas import tpu as pltpu
from jax.sharding import PartitionSpec as P

H = 32
HD = 24
NB = 16
TILES = 8
LANES = 128
SET = 16
HALF = SET * HD
SLABS = HALF // LANES
SAFE = 1e30
EXTRA = 8
SHIFT = 3 * NB
NT = (((1,), (1,)), ((), ()))
MIB = 1024 * 1024
BF16 = jnp.bfloat16
F32 = jnp.float32
FACTOR = math.log2(math.e) / math.sqrt(HD)


def vmem():
    return pl.BlockSpec(memory_space=pltpu.VMEM)


def smem():
    return pl.BlockSpec(memory_space=pltpu.SMEM)


def limit(mib):
    return pltpu.CompilerParams(vmem_limit_bytes=mib * MIB)


def shape(*dims, dtype=BF16):
    return jax.ShapeDtypeStruct(dims, dtype)


def one_hot_slab(bucket_row):
    n = bucket_row.shape[1]
    index = lax.broadcasted_iota(jnp.int32, (LANES, n), 0)
    wanted = jnp.where(index < 3 * NB, index % NB, -1).astype(F32)
    hot = jnp.where((wanted == bucket_row) | ((index >= SHIFT) & (index < SHIFT + 3)), 1.0, 0.0)
    return hot.T.astype(BF16)


def split_three(x):
    high = x.astype(BF16).astype(F32)
    mid = (x - high).astype(BF16).astype(F32)
    return high, mid, x - high - mid


def stage_kernel(
    count_ref, me_ref, src_ref, table_ref, bucket_ref, features_ref, tiles_ref,
    bias_ref, own_ref, masked_ref, extra_ref, from_ref, tiles_held, sems,
):
    rows = own_ref.shape[0]
    copies = [
        pltpu.make_async_copy(tiles_ref, tiles_held, sems.at[0]),
        pltpu.make_async_copy(features_ref, own_ref, sems.at[1]),
    ]
    for copy in copies:
        copy.start()
    for t in range(TILES):
        from_ref[t : t + 1, :] = jnp.full((1, LANES), src_ref[0, t] ^ me_ref[0], jnp.int32)
    width = own_ref.shape[1]
    extra = jnp.concatenate(
        [bucket_ref[...].astype(F32), jnp.zeros((1, width - rows), F32)], axis=1
    )
    extra_ref[...] = jnp.broadcast_to(extra, (EXTRA, width))
    table = table_ref[...] * math.sqrt(HD)
    at = lax.broadcasted_iota(jnp.int32, (NB, NB * NB), 1) // NB
    mine = at == lax.broadcasted_iota(jnp.int32, (NB, NB * NB), 0)
    key = lax.broadcasted_iota(jnp.int32, (NB * NB, LANES), 0) % NB
    column = lax.broadcasted_iota(jnp.int32, (NB * NB, LANES), 1)
    cube = jnp.zeros((H * NB, LANES), F32)
    for number, piece in enumerate(split_three(table)):
        spread = [jnp.where(mine, piece[h : h + 1, :], 0.0) for h in range(H)]
        place = jnp.where(column == key + number * NB, 1.0, 0.0).astype(BF16)
        cube = cube + jnp.dot(
            jnp.concatenate(spread, axis=0).astype(BF16), place, preferred_element_type=F32
        )
    cube = cube.astype(BF16)
    hot = one_hot_slab(bucket_ref[...].astype(F32))[:, :NB]
    for h in range(H):
        bias_ref[:, h * LANES : (h + 1) * LANES] = jnp.dot(
            hot, cube[h * NB : (h + 1) * NB, :], preferred_element_type=F32
        ).astype(BF16)
    for copy in copies:
        copy.wait()
    for t in range(TILES):
        tile = tiles_held[:, t * rows : (t + 1) * rows]
        masked_ref[:, t * rows : (t + 1) * rows] = jnp.where(
            t < count_ref[0], tile, jnp.zeros_like(tile)
        )


def aggregate_kernel(order, from_ref, extra_ref, masked_ref, *refs):
    feature_refs, out_ref, short_ref, least_ref, held = refs[:-4], *refs[-4:]
    rows = feature_refs[0].shape[0]
    for d, ref in zip([0, *order], feature_refs):
        held[d * rows : (d + 1) * rows, :] = ref[...]
    picked = []
    for t in range(TILES):
        start = pl.multiple_of(from_ref[t, 0] * rows, rows)
        picked.append(held[pl.ds(start, rows), :])
    total = feature_refs[0][...].astype(F32) + jnp.dot(
        masked_ref[...], jnp.concatenate(picked, axis=0), preferred_element_type=F32
    )
    mean_square = jnp.mean(total * total, axis=-1, keepdims=True)
    result = jnp.concatenate(
        [total * lax.rsqrt(mean_square + 1e-06), extra_ref[...]], axis=0
    ).astype(BF16)
    out_ref[...] = result
    short_ref[...] = result[: short_ref.shape[0], :]
    least_ref[...] = result[: least_ref.shape[0], :]


def slab_heads(slab):
    return slab * LANES // HD, ((slab + 1) * LANES - 1) // HD


def arrived_rows(block_refs, rows, hot_ref):
    arrived = [ref[...] for ref in block_refs]
    for s, item in enumerate(arrived):
        bucket = item[rows:, :rows].astype(F32)[:1, :]
        hot_ref[s * rows : (s + 1) * rows, :] = one_hot_slab(bucket)
    return jnp.concatenate([item[:rows, :] for item in arrived], axis=0)


def project(block, n, w_qk_ref, w_v_ref, k_ref, v_ref):
    width = w_v_ref.shape[0]
    k_ref[:, n : n + 256] = jnp.dot(
        block, w_qk_ref[:, width + n : width + n + 256], preferred_element_type=F32
    ).astype(BF16)
    v_ref[:, n : n + 256] = jnp.dot(
        block, w_v_ref[:, n : n + 256], preferred_element_type=F32
    ).astype(BF16)


def project_kernel(w_qk_ref, w_v_ref, *refs):
    *block_refs, hot_ref, k_ref, v_ref = refs
    rows = hot_ref.shape[0] // len(block_refs)
    block = arrived_rows(block_refs, rows, hot_ref)
    for n in range(0, k_ref.shape[1], 256):
        project(block, n, w_qk_ref, w_v_ref, k_ref, v_ref)


def part_kernel(count, first, last, w_qk_ref, w_v_ref, *refs):
    block_refs, refs = refs[:count], refs[count:]
    hot_refs, k_refs, v_refs = ([ref] for ref in refs[-6:-3])
    p_refs, top_ref = refs[-3:-1], refs[-1]
    refs = refs[:-6]
    if first:
        bias_ref, q_ref, shifted_ref, *outs = refs
    else:
        ready, (q_ref, bias_ref, *refs) = refs[:3], refs[3:]
        old_refs, outs = (refs[:2], refs[2:]) if len(refs) in (3, 5) else (refs[:3], refs[3:])
    rows = q_ref.shape[0]
    width = w_v_ref.shape[0]
    block = arrived_rows(block_refs, rows, hot_refs[0])
    raw_k_ref, raw_v_ref = k_refs[0], v_refs[0]

    def prepare(step):
        n = step * LANES
        if n % 256:
            return
        if first:
            q_ref[:, n : n + 256] = jnp.dot(
                block[:rows, :], w_qk_ref[:, n : n + 256], preferred_element_type=F32
            ).astype(BF16)
        project(block, n, w_qk_ref, w_v_ref, raw_k_ref, raw_v_ref)

    if not first:
        for some, ref in zip((hot_refs, k_refs, v_refs), ready):
            some.insert(0, ref)
    keys = sum(ref.shape[0] for ref in hot_refs)

    def every(some, cols=slice(None)):
        return jnp.concatenate([ref[:, cols] for ref in some], axis=0)

    lane = lax.broadcasted_iota(jnp.int32, (rows, LANES), 1)
    ones = jnp.ones((keys, LANES), BF16)

    def span(start, size):
        return pl.ds(start if isinstance(start, int) else pl.multiple_of(start, LANES), size)

    def scores(half, slab):
        cols = span(half * HALF + slab * LANES, LANES)
        begin, end = slab_heads(slab)
        q = q_ref[:, cols]
        zero = jnp.zeros_like(q)
        lefts, rights = [], []
        for h in range(begin, end + 1):
            inside = (lane >= h * HD - slab * LANES) & (lane < (h + 1) * HD - slab * LANES)
            lefts.append(jnp.where(inside, q, zero))
            if h * HD >= slab * LANES:
                rights.append(bias_ref[:, span((half * SET + h) * LANES, LANES)])
            else:
                rights.append(zero)
        query = jnp.concatenate(
            [jnp.concatenate(lefts, axis=0), jnp.concatenate(rights, axis=0)], axis=1
        )
        key = jnp.concatenate([every(k_refs, cols), every(hot_refs)], axis=1)
        return lax.dot_general(query, key, NT, preferred_element_type=F32)

    def weigh(half, slab, x, carried, p_ref, local):
        begin, end = slab_heads(slab)
        for h in range(begin, end + 1):
            own = x[(h - begin) * rows : (h - begin + 1) * rows, :]
            if h * HD < slab * LANES:
                own = own + carried
            if (h + 1) * HD > (slab + 1) * LANES:
                return own
            if local:
                peak = jnp.max(own, axis=-1, keepdims=True)
                own = own - peak
                keep_peak(half, h, peak)
            p_ref[h * rows : (h + 1) * rows, :] = jnp.exp2(own * FACTOR).astype(BF16)
        return None

    def keep_peak(half, h, peak):
        if first:
            at = span((half * SET + h) * LANES, LANES)
            mark = jnp.zeros((rows, LANES), F32)
            for number, piece in enumerate(split_three(-peak)):
                mark = jnp.where(lane == SHIFT + number, piece, mark)
            shifted_ref[:, at] = bias_ref[:, at] + mark.astype(BF16)
        else:
            top_ref[h * rows : (h + 1) * rows, :] = jnp.broadcast_to(peak, (rows, LANES))

    def pick(array, slab, base):
        begin, end = slab_heads(slab)
        out = array[(begin - base) * rows : (begin - base + 1) * rows, :]
        for h in range(begin + 1, end + 1):
            piece = array[(h - base) * rows : (h - base + 1) * rows, :]
            out = jnp.where(lane >= h * HD - slab * LANES, piece, out)
        return out

    def mix(half, slab, p_ref):
        cols = span(half * HALF + slab * LANES, LANES)
        begin, end = slab_heads(slab)
        value = jnp.concatenate([every(v_refs, cols), ones], axis=1)
        mixed = jnp.dot(
            p_ref[begin * rows : (end + 1) * rows, :], value, preferred_element_type=F32
        )
        return cols, pick(mixed[:, :LANES], slab, begin), pick(mixed[:, LANES:], slab, begin)

    def add(half, slab, p_ref):
        cols, top, total = mix(half, slab, p_ref)
        if not first:
            top = top + old_refs[0][:, cols]
            total = total + old_refs[1][:, cols]
        if last:
            outs[0][:, cols] = (top / total).astype(BF16)
        else:
            outs[0][:, cols] = top
            outs[1][:, cols] = total
            if not first:
                outs[2][:, cols] = jnp.zeros_like(top)
        return total

    steps = [divmod(step, SLABS) for step in range(width // LANES)]
    largest = jnp.zeros((rows, LANES), F32)
    prepare(0)
    x = scores(*steps[0])
    carried = None
    for number, (half, slab) in enumerate(steps):
        ahead = None
        if number + 1 < len(steps):
            prepare(number + 1)
            ahead = scores(*steps[number + 1])
        carried = weigh(half, slab, x, carried, p_refs[half % 2], first)
        if number:
            before = steps[number - 1]
            largest = jnp.maximum(largest, add(*before, p_refs[before[0] % 2]))
        x = ahead
    largest = jnp.maximum(largest, add(*steps[-1], p_refs[steps[-1][0] % 2]))
    if first:
        return
    fine = jnp.max(largest) < SAFE
    if len(old_refs) == 3:
        fine = fine & (jnp.max(old_refs[2][...]) == 0.0)

    @pl.when(jnp.logical_not(fine))
    def _():
        def careful(half, carry):
            left = None
            for slab in range(SLABS):
                left = weigh(half, slab, scores(half, slab), left, p_refs[0], True)
            for slab in range(SLABS):
                cols, top, total = mix(half, slab, p_refs[0])
                peak = pick(top_ref[...], slab, 0)
                old = old_refs[2][:, cols] if len(old_refs) == 3 else jnp.zeros_like(top)
                best = jnp.maximum(old, peak)
                share = jnp.exp2((peak - best) * FACTOR)
                old_share = jnp.exp2((old - best) * FACTOR)
                top = top * share + old_refs[0][:, cols] * old_share
                total = total * share + old_refs[1][:, cols] * old_share
                if last:
                    outs[0][:, cols] = (top / total).astype(BF16)
                else:
                    outs[0][:, cols] = top
                    outs[1][:, cols] = total
                    outs[2][:, cols] = best
            return carry

        lax.fori_loop(0, width // HALF, careful, 0)


def attend_part(first, last, w_qk, w_v, blocks, inputs):
    width = w_v.shape[0]
    rows = inputs[0].shape[0]
    ready = []
    if not first:
        near, blocks = blocks[::2], blocks[1::2]
        count = rows * len(near)
        ready = pl.pallas_call(
            project_kernel,
            out_shape=[shape(count, LANES), shape(count, width), shape(count, width)],
            in_specs=[vmem()] * (2 + len(near)),
            out_specs=[vmem()] * 3,
            compiler_params=limit(8),
            cost_estimate=pl.CostEstimate(flops=1000, bytes_accessed=1000, transcendentals=0),
            name="project",
        )(w_qk, w_v, *near)
    count = rows * len(blocks)
    keys = count + sum(item.shape[0] for item in ready[:1])
    state = shape(rows, width, dtype=F32)
    if first:
        outs = [shape(rows, width), shape(rows, H * LANES), state, state]
    elif last:
        outs = [shape(rows, width)]
    else:
        outs = [state] * 3
    operands = [w_qk, w_v, *blocks, *ready, *inputs]
    tall = SET * rows
    need = 4 * tall * keys + 4 * keys * width + 4 * tall * LANES
    return pl.pallas_call(
        lambda *refs: part_kernel(len(blocks), first, last, *refs),
        out_shape=outs,
        in_specs=[vmem()] * len(operands),
        out_specs=[vmem()] * len(outs),
        scratch_shapes=[
            pltpu.VMEM((count, LANES), BF16),
            pltpu.VMEM((count, width), BF16),
            pltpu.VMEM((count, width), BF16),
            pltpu.VMEM((tall, keys), BF16),
            pltpu.VMEM((tall, keys), BF16),
            pltpu.VMEM((tall, LANES), F32),
        ],
        compiler_params=limit(need // MIB + 8),
        cost_estimate=pl.CostEstimate(
            flops=1000 if not last else 10**9, bytes_accessed=1000 if not last else 4_000_000, transcendentals=0
        ),
        name="part",
    )(*operands)


def swap(array, axis, distance):
    return lax.ppermute(array, axis, [(i, i ^ distance) for i in range(lax.axis_size(axis))])


def after(value, *others):
    return lax.optimization_barrier((value, others))[0]


def on_device(features, tiles, tile_src, tile_count, node_bucket, w_qk, w_v, bias_table):
    rows, width = features.shape
    groups = lax.axis_size("group")
    seq_count = lax.axis_size("seq")
    chips = seq_count // 2
    any_space = pl.BlockSpec(memory_space=pl.ANY)

    order = list(range(1, groups))
    received = [swap(features, "group", d) for d in order]
    own_bucket = node_bucket.reshape(1, rows)

    bias, own_features, masked, extra, source = pl.pallas_call(
        stage_kernel,
        out_shape=[
            shape(rows, H * LANES), shape(rows, width), shape(rows, TILES * rows),
            shape(EXTRA, width, dtype=F32),
            shape(TILES, LANES, dtype=jnp.int32),
        ],
        in_specs=[smem()] * 3 + [vmem(), vmem(), any_space, any_space],
        out_specs=[vmem()] * 5,
        scratch_shapes=[pltpu.VMEM((rows, TILES * rows), BF16), pltpu.SemaphoreType.DMA((2,))],
        compiler_params=limit(8),
        cost_estimate=pl.CostEstimate(flops=10**9, bytes_accessed=4_000_000, transcendentals=0),
        name="stage",
    )(tile_count, lax.axis_index("group").reshape(1), tile_src, bias_table, own_bucket, features, tiles)

    own, short, least = pl.pallas_call(
        lambda *refs: aggregate_kernel(order, *refs),
        out_shape=[shape(rows + EXTRA, width), shape(rows + EXTRA - 2, width),
            shape(rows + 1, width)],
        in_specs=[vmem()] * (3 + groups),
        out_specs=[vmem()] * 3,
        scratch_shapes=[pltpu.VMEM((groups * rows, width), BF16)],
        compiler_params=limit(8),
        cost_estimate=pl.CostEstimate(flops=10**9, bytes_accessed=4_000_000, transcendentals=0),
        name="aggregate",
    )(source, extra, masked, own_features, *received)

    far = [least] + [None] * (chips - 1)
    top = 1
    while 2 * top < chips:
        top *= 2
    far[top] = swap(own, "seq", 2 * top)
    step = 1
    while step < top:
        far[step] = swap(short, "seq", 2 * step)
        step *= 2
    for d in range(3, chips):
        if far[d] is None:
            far[d] = swap(far[d & (d - 1)], "seq", 2 * (d & -d))
    parts = [[0], [1, top]] if top > 1 else [[0, 1]]
    parts += [[d] for d in range(2, chips) if d != top]
    queries, state = [], [bias]
    for number, part in enumerate(parts):
        blocks = []
        for d in part:
            block = far[d]
            if d:
                block = after(block, *state)
                near = swap(block, "seq", 1)
            else:
                near = swap(least, "seq", 1)
            blocks += [block, near]
        state = attend_part(
            number == 0, number == len(parts) - 1, w_qk, w_v, blocks, [*queries, *state]
        )
        if number == 0:
            queries, state = state[:2], state[2:]
    return state[0]


def solution(mesh):
    in_specs = (
        P(("group", "seq"), None),
        P(("group", "seq"), None),
        P(("group", "seq"), None),
        P(("group", "seq")),
        P(("group", "seq")),
        P(),
        P(),
        P(),
    )
    out_specs = P(("group", "seq"), None)
    return jax.shard_map(
        on_device, mesh=mesh, in_specs=in_specs, out_specs=out_specs, check_vma=False
    )
```

```python
import math

import jax
import jax.numpy as jnp
from jax import lax
from jax.experimental import pallas as pl
from jax.experimental.pallas import tpu as pltpu
from jax.sharding import PartitionSpec as P

H = 32
HD = 24
NB = 16
TILES = 8
LANES = 128
SET = 16
HALF = SET * HD
SLABS = HALF // LANES
SAFE = 1e30
EXTRA = 8
SHIFT = 3 * NB
NT = (((1,), (1,)), ((), ()))
MIB = 1024 * 1024
BF16 = jnp.bfloat16
F32 = jnp.float32
FACTOR = math.log2(math.e) / math.sqrt(HD)


def vmem():
    return pl.BlockSpec(memory_space=pltpu.VMEM)


def smem():
    return pl.BlockSpec(memory_space=pltpu.SMEM)


def limit(mib):
    return pltpu.CompilerParams(vmem_limit_bytes=mib * MIB)


def shape(*dims, dtype=BF16):
    return jax.ShapeDtypeStruct(dims, dtype)


def one_hot_slab(bucket_row):
    n = bucket_row.shape[1]
    index = lax.broadcasted_iota(jnp.int32, (LANES, n), 0)
    wanted = jnp.where(index < 3 * NB, index % NB, -1).astype(F32)
    hot = jnp.where((wanted == bucket_row) | ((index >= SHIFT) & (index < SHIFT + 3)), 1.0, 0.0)
    return hot.T.astype(BF16)


def split_three(x):
    high = x.astype(BF16).astype(F32)
    mid = (x - high).astype(BF16).astype(F32)
    return high, mid, x - high - mid


def stage_kernel(
    count_ref, me_ref, src_ref, table_ref, bucket_ref, features_ref, tiles_ref,
    bias_ref, own_ref, masked_ref, extra_ref, from_ref, tiles_held, sems,
):
    rows = own_ref.shape[0]
    copies = [
        pltpu.make_async_copy(tiles_ref, tiles_held, sems.at[0]),
        pltpu.make_async_copy(features_ref, own_ref, sems.at[1]),
    ]
    for copy in copies:
        copy.start()
    for t in range(TILES):
        from_ref[t : t + 1, :] = jnp.full((1, LANES), src_ref[0, t] ^ me_ref[0], jnp.int32)
    width = own_ref.shape[1]
    extra = jnp.concatenate(
        [bucket_ref[...].astype(F32), jnp.zeros((1, width - rows), F32)], axis=1
    )
    extra_ref[...] = jnp.broadcast_to(extra, (EXTRA, width))
    table = table_ref[...] * math.sqrt(HD)
    at = lax.broadcasted_iota(jnp.int32, (NB, NB * NB), 1) // NB
    mine = at == lax.broadcasted_iota(jnp.int32, (NB, NB * NB), 0)
    key = lax.broadcasted_iota(jnp.int32, (NB * NB, LANES), 0) % NB
    column = lax.broadcasted_iota(jnp.int32, (NB * NB, LANES), 1)
    cube = jnp.zeros((H * NB, LANES), F32)
    for number, piece in enumerate(split_three(table)):
        spread = [jnp.where(mine, piece[h : h + 1, :], 0.0) for h in range(H)]
        place = jnp.where(column == key + number * NB, 1.0, 0.0).astype(BF16)
        cube = cube + jnp.dot(
            jnp.concatenate(spread, axis=0).astype(BF16), place, preferred_element_type=F32
        )
    cube = cube.astype(BF16)
    hot = one_hot_slab(bucket_ref[...].astype(F32))[:, :NB]
    for h in range(H):
        bias_ref[:, h * LANES : (h + 1) * LANES] = jnp.dot(
            hot, cube[h * NB : (h + 1) * NB, :], preferred_element_type=F32
        ).astype(BF16)
    for copy in copies:
        copy.wait()
    for t in range(TILES):
        tile = tiles_held[:, t * rows : (t + 1) * rows]
        masked_ref[:, t * rows : (t + 1) * rows] = jnp.where(
            t < count_ref[0], tile, jnp.zeros_like(tile)
        )


def aggregate_kernel(order, from_ref, extra_ref, masked_ref, *refs):
    feature_refs, out_ref, short_ref, least_ref, held = refs[:-4], *refs[-4:]
    rows = feature_refs[0].shape[0]
    for d, ref in zip([0, *order], feature_refs):
        held[d * rows : (d + 1) * rows, :] = ref[...]
    picked = []
    for t in range(TILES):
        start = pl.multiple_of(from_ref[t, 0] * rows, rows)
        picked.append(held[pl.ds(start, rows), :])
    total = feature_refs[0][...].astype(F32) + jnp.dot(
        masked_ref[...], jnp.concatenate(picked, axis=0), preferred_element_type=F32
    )
    mean_square = jnp.mean(total * total, axis=-1, keepdims=True)
    result = jnp.concatenate(
        [total * lax.rsqrt(mean_square + 1e-06), extra_ref[...]], axis=0
    ).astype(BF16)
    out_ref[...] = result
    short_ref[...] = result[: short_ref.shape[0], :]
    least_ref[...] = result[: least_ref.shape[0], :]


def slab_heads(slab):
    return slab * LANES // HD, ((slab + 1) * LANES - 1) // HD


def arrived_rows(block_refs, rows, hot_ref):
    arrived = [ref[...] for ref in block_refs]
    for s, item in enumerate(arrived):
        bucket = item[rows:, :rows].astype(F32)[:1, :]
        hot_ref[s * rows : (s + 1) * rows, :] = one_hot_slab(bucket)
    return jnp.concatenate([item[:rows, :] for item in arrived], axis=0)


def project(block, n, w_qk_ref, w_v_ref, k_ref, v_ref):
    width = w_v_ref.shape[0]
    k_ref[:, n : n + 256] = jnp.dot(
        block, w_qk_ref[:, width + n : width + n + 256], preferred_element_type=F32
    ).astype(BF16)
    v_ref[:, n : n + 256] = jnp.dot(
        block, w_v_ref[:, n : n + 256], preferred_element_type=F32
    ).astype(BF16)


def project_kernel(w_qk_ref, w_v_ref, *refs):
    *block_refs, hot_ref, k_ref, v_ref = refs
    rows = hot_ref.shape[0] // len(block_refs)
    block = arrived_rows(block_refs, rows, hot_ref)
    for n in range(0, k_ref.shape[1], 256):
        project(block, n, w_qk_ref, w_v_ref, k_ref, v_ref)


def part_kernel(count, first, last, w_qk_ref, w_v_ref, *refs):
    block_refs, refs = refs[:count], refs[count:]
    hot_refs, k_refs, v_refs = ([ref] for ref in refs[-6:-3])
    p_refs, top_ref = refs[-3:-1], refs[-1]
    refs = refs[:-6]
    if first:
        bias_ref, q_ref, shifted_ref, *outs = refs
    else:
        ready, (q_ref, bias_ref, *refs) = refs[:3], refs[3:]
        old_refs, outs = (refs[:2], refs[2:]) if len(refs) in (3, 5) else (refs[:3], refs[3:])
    rows = q_ref.shape[0]
    width = w_v_ref.shape[0]
    block = arrived_rows(block_refs, rows, hot_refs[0])
    raw_k_ref, raw_v_ref = k_refs[0], v_refs[0]

    def prepare(step):
        n = step * LANES
        if n % 256:
            return
        if first:
            q_ref[:, n : n + 256] = jnp.dot(
                block[:rows, :], w_qk_ref[:, n : n + 256], preferred_element_type=F32
            ).astype(BF16)
        project(block, n, w_qk_ref, w_v_ref, raw_k_ref, raw_v_ref)

    if not first:
        for some, ref in zip((hot_refs, k_refs, v_refs), ready):
            some.insert(0, ref)
    keys = sum(ref.shape[0] for ref in hot_refs)

    def every(some, cols=slice(None)):
        return jnp.concatenate([ref[:, cols] for ref in some], axis=0)

    lane = lax.broadcasted_iota(jnp.int32, (rows, LANES), 1)
    ones = jnp.ones((keys, LANES), BF16)

    def span(start, size):
        return pl.ds(start if isinstance(start, int) else pl.multiple_of(start, LANES), size)

    def scores(half, slab):
        cols = span(half * HALF + slab * LANES, LANES)
        begin, end = slab_heads(slab)
        q = q_ref[:, cols]
        zero = jnp.zeros_like(q)
        lefts, rights = [], []
        for h in range(begin, end + 1):
            inside = (lane >= h * HD - slab * LANES) & (lane < (h + 1) * HD - slab * LANES)
            lefts.append(jnp.where(inside, q, zero))
            if h * HD >= slab * LANES:
                rights.append(bias_ref[:, span((half * SET + h) * LANES, LANES)])
            else:
                rights.append(zero)
        query = jnp.concatenate(
            [jnp.concatenate(lefts, axis=0), jnp.concatenate(rights, axis=0)], axis=1
        )
        key = jnp.concatenate([every(k_refs, cols), every(hot_refs)], axis=1)
        return lax.dot_general(query, key, NT, preferred_element_type=F32)

    def weigh(half, slab, x, carried, p_ref, local):
        begin, end = slab_heads(slab)
        for h in range(begin, end + 1):
            own = x[(h - begin) * rows : (h - begin + 1) * rows, :]
            if h * HD < slab * LANES:
                own = own + carried
            if (h + 1) * HD > (slab + 1) * LANES:
                return own
            if local:
                peak = jnp.max(own, axis=-1, keepdims=True)
                own = own - peak
                keep_peak(half, h, peak)
            p_ref[h * rows : (h + 1) * rows, :] = jnp.exp2(own * FACTOR).astype(BF16)
        return None

    def keep_peak(half, h, peak):
        if first:
            at = span((half * SET + h) * LANES, LANES)
            mark = jnp.zeros((rows, LANES), F32)
            for number, piece in enumerate(split_three(-peak)):
                mark = jnp.where(lane == SHIFT + number, piece, mark)
            shifted_ref[:, at] = bias_ref[:, at] + mark.astype(BF16)
        else:
            top_ref[h * rows : (h + 1) * rows, :] = jnp.broadcast_to(peak, (rows, LANES))

    def pick(array, slab, base):
        begin, end = slab_heads(slab)
        out = array[(begin - base) * rows : (begin - base + 1) * rows, :]
        for h in range(begin + 1, end + 1):
            piece = array[(h - base) * rows : (h - base + 1) * rows, :]
            out = jnp.where(lane >= h * HD - slab * LANES, piece, out)
        return out

    def mix(half, slab, p_ref):
        cols = span(half * HALF + slab * LANES, LANES)
        begin, end = slab_heads(slab)
        value = jnp.concatenate([every(v_refs, cols), ones], axis=1)
        mixed = jnp.dot(
            p_ref[begin * rows : (end + 1) * rows, :], value, preferred_element_type=F32
        )
        return cols, pick(mixed[:, :LANES], slab, begin), pick(mixed[:, LANES:], slab, begin)

    def add(half, slab, p_ref):
        cols, top, total = mix(half, slab, p_ref)
        if not first:
            top = top + old_refs[0][:, cols]
            total = total + old_refs[1][:, cols]
        if last:
            outs[0][:, cols] = (top / total).astype(BF16)
        else:
            outs[0][:, cols] = top
            outs[1][:, cols] = total
            if not first:
                outs[2][:, cols] = jnp.zeros_like(top)
        return total

    steps = [divmod(step, SLABS) for step in range(width // LANES)]
    largest = jnp.zeros((rows, LANES), F32)
    prepare(0)
    x = scores(*steps[0])
    carried = None
    for number, (half, slab) in enumerate(steps):
        ahead = None
        if number + 1 < len(steps):
            prepare(number + 1)
            ahead = scores(*steps[number + 1])
        carried = weigh(half, slab, x, carried, p_refs[half % 2], first)
        if number:
            before = steps[number - 1]
            largest = jnp.maximum(largest, add(*before, p_refs[before[0] % 2]))
        x = ahead
    largest = jnp.maximum(largest, add(*steps[-1], p_refs[steps[-1][0] % 2]))
    if first:
        return
    fine = jnp.max(largest) < SAFE
    if len(old_refs) == 3:
        fine = fine & (jnp.max(old_refs[2][...]) == 0.0)

    @pl.when(jnp.logical_not(fine))
    def _():
        def careful(half, carry):
            left = None
            for slab in range(SLABS):
                left = weigh(half, slab, scores(half, slab), left, p_refs[0], True)
            for slab in range(SLABS):
                cols, top, total = mix(half, slab, p_refs[0])
                peak = pick(top_ref[...], slab, 0)
                old = old_refs[2][:, cols] if len(old_refs) == 3 else jnp.zeros_like(top)
                best = jnp.maximum(old, peak)
                share = jnp.exp2((peak - best) * FACTOR)
                old_share = jnp.exp2((old - best) * FACTOR)
                top = top * share + old_refs[0][:, cols] * old_share
                total = total * share + old_refs[1][:, cols] * old_share
                if last:
                    outs[0][:, cols] = (top / total).astype(BF16)
                else:
                    outs[0][:, cols] = top
                    outs[1][:, cols] = total
                    outs[2][:, cols] = best
            return carry

        lax.fori_loop(0, width // HALF, careful, 0)


def attend_part(first, last, w_qk, w_v, blocks, inputs):
    width = w_v.shape[0]
    rows = inputs[0].shape[0]
    ready = []
    if not first:
        near, blocks = blocks[::2], blocks[1::2]
        count = rows * len(near)
        ready = pl.pallas_call(
            project_kernel,
            out_shape=[shape(count, LANES), shape(count, width), shape(count, width)],
            in_specs=[vmem()] * (2 + len(near)),
            out_specs=[vmem()] * 3,
            compiler_params=limit(8),
            cost_estimate=pl.CostEstimate(flops=1000, bytes_accessed=1000, transcendentals=0),
            name="project",
        )(w_qk, w_v, *near)
    count = rows * len(blocks)
    keys = count + sum(item.shape[0] for item in ready[:1])
    state = shape(rows, width, dtype=F32)
    if first:
        outs = [shape(rows, width), shape(rows, H * LANES), state, state]
    elif last:
        outs = [shape(rows, width)]
    else:
        outs = [state] * 3
    operands = [w_qk, w_v, *blocks, *ready, *inputs]
    tall = SET * rows
    need = 4 * tall * keys + 4 * keys * width + 4 * tall * LANES
    return pl.pallas_call(
        lambda *refs: part_kernel(len(blocks), first, last, *refs),
        out_shape=outs,
        in_specs=[vmem()] * len(operands),
        out_specs=[vmem()] * len(outs),
        scratch_shapes=[
            pltpu.VMEM((count, LANES), BF16),
            pltpu.VMEM((count, width), BF16),
            pltpu.VMEM((count, width), BF16),
            pltpu.VMEM((tall, keys), BF16),
            pltpu.VMEM((tall, keys), BF16),
            pltpu.VMEM((tall, LANES), F32),
        ],
        compiler_params=limit(need // MIB + 8),
        cost_estimate=pl.CostEstimate(
            flops=1000 if not last else 10**9, bytes_accessed=1000 if not last else 4_000_000, transcendentals=0
        ),
        name="part",
    )(*operands)


def swap(array, axis, distance):
    return lax.ppermute(array, axis, [(i, i ^ distance) for i in range(lax.axis_size(axis))])


def after(value, *others):
    return lax.optimization_barrier((value, others))[0]


def on_device(features, tiles, tile_src, tile_count, node_bucket, w_qk, w_v, bias_table):
    rows, width = features.shape
    groups = lax.axis_size("group")
    seq_count = lax.axis_size("seq")
    chips = seq_count // 2
    any_space = pl.BlockSpec(memory_space=pl.ANY)

    order = [1, *range(groups - 1, 1, -1)]
    received = [swap(features, "group", d) for d in order]
    own_bucket = node_bucket.reshape(1, rows)

    bias, own_features, masked, extra, source = pl.pallas_call(
        stage_kernel,
        out_shape=[
            shape(rows, H * LANES), shape(rows, width), shape(rows, TILES * rows),
            shape(EXTRA, width, dtype=F32),
            shape(TILES, LANES, dtype=jnp.int32),
        ],
        in_specs=[smem()] * 3 + [vmem(), vmem(), any_space, any_space],
        out_specs=[vmem()] * 5,
        scratch_shapes=[pltpu.VMEM((rows, TILES * rows), BF16), pltpu.SemaphoreType.DMA((2,))],
        compiler_params=limit(8),
        cost_estimate=pl.CostEstimate(flops=10**9, bytes_accessed=4_000_000, transcendentals=0),
        name="stage",
    )(tile_count, lax.axis_index("group").reshape(1), tile_src, bias_table, own_bucket, features, tiles)

    own, short, least = pl.pallas_call(
        lambda *refs: aggregate_kernel(order, *refs),
        out_shape=[shape(rows + EXTRA, width), shape(rows + EXTRA - 2, width),
            shape(rows + 1, width)],
        in_specs=[vmem()] * (3 + groups),
        out_specs=[vmem()] * 3,
        scratch_shapes=[pltpu.VMEM((groups * rows, width), BF16)],
        compiler_params=limit(8),
        cost_estimate=pl.CostEstimate(flops=10**9, bytes_accessed=4_000_000, transcendentals=0),
        name="aggregate",
    )(source, extra, masked, own_features, *received)

    far = [least] + [None] * (chips - 1)
    top = 1
    while 2 * top < chips:
        top *= 2
    far[top] = swap(own, "seq", 2 * top)
    step = 1
    while step < top:
        far[step] = swap(short, "seq", 2 * step)
        step *= 2
    parts = [[0], [1, top]] if top > 1 else [[0, 1]]
    parts += [[d] for d in range(2, chips) if d != top]
    queries, state = [], [bias]
    for number, part in enumerate(parts):
        if number == 1:
            for d in range(3, chips):
                if far[d] is None:
                    far[d] = swap(after(far[d & (d - 1)], *state), "seq", 2 * (d & -d))
        blocks = []
        for d in part:
            block = far[d]
            if d:
                block = after(block, *state)
                sent = block[: rows + EXTRA // 2] if d == top else block
                near = swap(sent, "seq", 1)
            else:
                near = swap(least, "seq", 1)
            blocks += [block, near]
        state = attend_part(
            number == 0, number == len(parts) - 1, w_qk, w_v, blocks, [*queries, *state]
        )
        if number == 0:
            queries, state = state[:2], state[2:]
    return state[0]


def solution(mesh):
    in_specs = (
        P(("group", "seq"), None),
        P(("group", "seq"), None),
        P(("group", "seq"), None),
        P(("group", "seq")),
        P(("group", "seq")),
        P(),
        P(),
        P(),
    )
    out_specs = P(("group", "seq"), None)
    return jax.shard_map(
        on_device, mesh=mesh, in_specs=in_specs, out_specs=out_specs, check_vma=False
    )
```
